32 devices in a mesh: strip: 4 (over x, core), img: 8 (over z, y).
Axes of the slice: x: 2, y: 2, z: 4, core: 2. Of those that a mesh axis runs over, the one named last changes fastest.
Arguments:
- features: bfloat16 [160, 32, 32, 256], P('img', 'strip'), may hold values from -6 to 6
- cotangent: bfloat16 [160, 32, 32, 256], P('img', 'strip'), may hold values from -6 to 6
- present: int32 [160], replicated, may hold values from 0 to 1, as said below
- owners: int32 [40], replicated, may hold values from 0 to 39, as said below
- tile_master: float32 [40, 128, 128], P('img'), may hold values from -0.3125 to 0.3125
- tile_mom1: float32 [40, 128, 128], P('img'), may hold values from -80 to 80
- tile_mom2: float32 [40, 128, 128], P('img'), may hold values from 336 to 5120
- stat_left: float32 [40, 128, 128], P('img'), may hold values from -182 to 182044, as said below
- stat_right: float32 [40, 128, 128], P('img'), may hold values from -182 to 182044, as said below
- basis_left: float32 [40, 128, 128], P('img'), may hold values from -1 to 1
- basis_right: float32 [40, 128, 128], P('img'), may hold values from -1 to 1
- proj_master: float32 [256, 64], replicated, may hold values from -0.375 to 0.375
- proj_mom1: float32 [256, 64], replicated, may hold values from -512 to 512
- proj_mom2: float32 [256, 64], replicated, may hold values from 4000 to 32000
- dec_master: float32 [64, 256], replicated, may hold values from -0.75 to 0.75
- dec_mom1: float32 [64, 256], replicated, may hold values from -80 to 80
- dec_mom2: float32 [64, 256], replicated, may hold values from 320 to 5120
- code_master: float32 [512, 64], replicated, may hold values from -3 to 3
- code_mom1: float32 [512, 64], replicated, may hold values from -40 to 40
- code_mom2: float32 [512, 64], replicated, may hold values from 64 to 960
Outputs:
- decoded: bfloat16 [160, 32, 32, 256], P('img', 'strip')
- input_grad: bfloat16 [160, 32, 32, 256], P('img', 'strip')
- quant_loss: float32 [], replicated
- tile_master_new: float32 [40, 128, 128], P('img')
- tile_mom1_new: float32 [40, 128, 128], P('img')
- tile_mom2_new: float32 [40, 128, 128], P('img')
- stat_left_new: float32 [40, 128, 128], P('img')
- stat_right_new: float32 [40, 128, 128], P('img')
- basis_left_new: float32 [40, 128, 128], P('img')
- basis_right_new: float32 [40, 128, 128], P('img')
- proj_new: float32 [256, 64], replicated
- proj_mom1_new: float32 [256, 64], replicated
- proj_mom2_new: float32 [256, 64], replicated
- dec_new: float32 [64, 256], replicated
- dec_mom1_new: float32 [64, 256], replicated
- dec_mom2_new: float32 [64, 256], replicated
- code_new: float32 [512, 64], replicated
- code_mom1_new: float32 [512, 64], replicated
- code_mom2_new: float32 [512, 64], replicated
The draws below stay inside these ranges and needn't reach their ends.
Inputs may be any that keep to these rules, and one draw needn't show every extreme that they name: On each index of img its present images come first; every index has one or more, some index has all 20. `owners`: distinct slots; both 0 and 39 are used. `stat_left`: symmetric positive definite. `stat_right`: symmetric positive definite.
All inputs are finite; a program needn't handle non-finite values.
Results may differ from the reference program's by a relative error of at most 0.019.
The reference program's roundings to bfloat16 on the way count: a program that leaves them out, or rounds other values in their place, can miss the bound.
Values may be sent and summed in bfloat16 or wider, within the bound.
No kernel may reach another device: no remote copies, remote signals or barrier semaphores. Data moves between devices by JAX's collectives and lax.ppermute only.
A program may use at most 192 MiB of HBM per device.

```python
import math
import jax
import jax.numpy as jnp
from jax import lax

C = 256
LAT = 64
K = 512
IMG_DEV = 20
HEIGHT = 32
WIDE = 32
STEP = 5
TILE = 128
TILES = 40
IMGS = 160
SLOTS = 40
GSQ = 12800
N_IMG = 8


def draw_present(key, part):
    key = jax.random.fold_in(key, 11)
    first_key, second_key = jax.random.split(key)
    counts = jax.random.randint(first_key, (N_IMG,), 1, IMG_DEV + 1)
    chosen = jax.random.randint(second_key, (), 0, N_IMG)
    counts = jnp.where(jnp.arange(N_IMG) == chosen, IMG_DEV, counts)
    places = jnp.arange(IMG_DEV)
    flags = (places[None, :] < counts[:, None]).astype(jnp.int32)
    return flags.reshape(N_IMG * IMG_DEV)


def draw_owners(key, part):
    key = jax.random.fold_in(key, 12)
    order = jax.random.permutation(key, SLOTS).astype(jnp.int32)
    highest = SLOTS - 1
    where_top = jnp.argmax(order == highest)
    order = order.at[where_top].set(order[0]).at[0].set(highest)
    where_zero = jnp.argmax(order == 0)
    order = order.at[where_zero].set(order[1]).at[1].set(0)
    return order[:TILES].astype(jnp.int32)


def stat_shared(key):
    first_key, second_key = jax.random.split(key)
    base = (1.0 - 0.95) / 0.95 * GSQ
    spread = jax.random.uniform(first_key, (SLOTS, TILE), jnp.float32, math.log(0.5), math.log(2.0))
    diagonal = jnp.exp(spread) * (base * TILE)
    noise = jax.random.uniform(second_key, (SLOTS, TILE, TILE), jnp.float32, -1.0, 1.0)
    noise = 0.125 * base * (noise + jnp.swapaxes(noise, 1, 2))
    unit = jnp.eye(TILE, dtype=jnp.float32)[None]
    return noise * (1.0 - unit) + unit * diagonal[:, :, None]


def draw_stat_left(key, part):
    key = jax.random.fold_in(key, 13)
    return stat_shared(key)


def draw_stat_right(key, part):
    key = jax.random.fold_in(key, 14)
    return stat_shared(key)


def basis_shared(key):
    index = jnp.arange(TILE)
    rotated = jnp.broadcast_to(jnp.eye(TILE, dtype=jnp.float32), (SLOTS, TILE, TILE))
    for level in range(TILE.bit_length() - 1):
        stride = 1 << level
        angles = jax.random.uniform(jax.random.fold_in(key, level), (SLOTS, TILE), jnp.float32, -math.pi, math.pi)
        partner = index ^ stride
        upper = index & stride > 0
        lower = jnp.where(upper, index - stride, index)
        theta = angles[:, lower]
        signs = jnp.where(upper, 1.0, -1.0).astype(jnp.float32)
        rotated = jnp.cos(theta)[:, :, None] * rotated + (signs[None, :] * jnp.sin(theta))[:, :, None] * rotated[:, partner, :]
    return rotated


def draw_basis_left(key, part):
    key = jax.random.fold_in(key, 15)
    return basis_shared(key)


def draw_basis_right(key, part):
    key = jax.random.fold_in(key, 16)
    return basis_shared(key)


def shard_levels(rng, dims, cuts, low, top_value):
    def one(dim, shards_of):
        steps = jax.random.uniform(jax.random.fold_in(jax.random.fold_in(rng, 6), dim), (shards_of,), jnp.float32, low / len(cuts), top_value / len(cuts))
        return jnp.repeat(jnp.exp(steps), dims[dim] // shards_of).reshape((-1,) + (1,) * (len(dims) - dim - 1))

    loudness = one(*cuts[0])
    for cut in cuts[1:]:
        loudness = loudness * one(*cut)
    return loudness


def centred(stream_key, dims, scale, limit, cuts=(), held_as=jnp.bfloat16):
    drawn = jax.random.normal(stream_key, dims, jnp.float32) * scale
    if len(cuts) > 0:
        drawn = shard_levels(stream_key, dims, cuts, -0.22, 0.18) * drawn
    return jnp.clip(drawn, min=-limit, max=limit).astype(held_as)


def setup_inputs(seed: int = 0) -> dict:
    seeds = jax.random.split(jax.random.key(seed), 21)
    features = centred(seeds[0], (IMGS, HEIGHT, WIDE, C), 1.0, 6.0, ((0, 8), (1, 4)))
    cotangent = centred(seeds[1], (IMGS, HEIGHT, WIDE, C), 1.0, 6.0, ((0, 8), (1, 4)))
    present = draw_present(jax.random.fold_in(seeds[20], 71), 0)
    owners = draw_owners(jax.random.fold_in(seeds[20], 71), 0)
    tile_master = centred(seeds[4], (SLOTS, TILE, TILE), (25 * C // 16) ** -0.5, 0.3125, ((0, 8),), jnp.float32)
    tile_mom1 = centred(seeds[5], (SLOTS, TILE, TILE), (GSQ ** 0.5 / 9), 80.0, ((0, 8),), jnp.float32)
    tile_mom2 = jnp.clip(jnp.exp(math.log(5120.0) - 2.7237986 * jax.random.uniform(seeds[6], (SLOTS, TILE, TILE), jnp.float32) ** shard_levels(seeds[6], (SLOTS, TILE, TILE), ((0, 8),), -0.2, 0.2)), 336.0, 5120.0)
    stat_left = draw_stat_left(jax.random.fold_in(seeds[20], 71), 0)
    stat_right = draw_stat_right(jax.random.fold_in(seeds[20], 71), 0)
    basis_left = draw_basis_left(jax.random.fold_in(seeds[20], 71), 0)
    basis_right = draw_basis_right(jax.random.fold_in(seeds[20], 71), 0)
    proj_master = centred(seeds[11], (C, LAT), C ** -0.5, 0.375, (), jnp.float32)
    proj_mom1 = centred(seeds[12], (C, LAT), (7 * (IMG_DEV * N_IMG) ** 0.5), 512.0, (), jnp.float32)
    proj_mom2 = jnp.clip(jnp.exp(jax.random.uniform(seeds[13], (C, LAT), jnp.float32, math.log(4000.0), math.log(32000.0))), 4000.0, 32000.0)
    dec_master = centred(seeds[14], (LAT, C), LAT ** -0.5, 0.75, (), jnp.float32)
    dec_mom1 = centred(seeds[15], (LAT, C), ((IMG_DEV * N_IMG) ** 0.5), 80.0, (), jnp.float32)
    dec_mom2 = jnp.clip(jnp.exp(jax.random.uniform(seeds[16], (LAT, C), jnp.float32, math.log(320.0), math.log(5120.0))), 320.0, 5120.0)
    code_master = centred(seeds[17], (K, LAT), 0.5, 3.0, (), jnp.float32)
    code_mom1 = centred(seeds[18], (K, LAT), ((IMG_DEV * N_IMG) ** 0.5 / 2), 40.0, (), jnp.float32)
    code_mom2 = jnp.clip(jnp.exp(jax.random.uniform(seeds[19], (K, LAT), jnp.float32, math.log(64.0), math.log(960.0))), 64.0, 960.0)
    return {"features": features, "cotangent": cotangent, "present": present, "owners": owners, "tile_master": tile_master, "tile_mom1": tile_mom1, "tile_mom2": tile_mom2, "stat_left": stat_left, "stat_right": stat_right, "basis_left": basis_left, "basis_right": basis_right, "proj_master": proj_master, "proj_mom1": proj_mom1, "proj_mom2": proj_mom2, "dec_master": dec_master, "dec_mom1": dec_mom1, "dec_mom2": dec_mom2, "code_master": code_master, "code_mom1": code_mom1, "code_mom2": code_mom2}


EXACT_PRECISION = lax.Precision.HIGHEST
BETA_ONE = 0.9
BETA_TWO = 0.95
EPSILON = 1e-08
WEIGHT_DECAY = 0.01
SOFTMAX_WARMTH = 4.0
LOSS_WEIGHT = 1.25
TILE_RATE = 0.05
PROJ_RATE = 0.05
DEC_RATE = 0.1
CODE_RATE = 0.3

@jax.custom_vjp
def reduced_input(v):
    return lax.optimization_barrier(v.astype(jnp.bfloat16)).astype(jnp.float32)

@jax.custom_vjp
def reduced_backward(v):
    return v

def low_keep(v):
    return (reduced_input(v), None)

def low_pass(kept, grad):
    return (grad,)

def back_keep(v):
    return (v, None)

def back_low(kept, grad):
    return (reduced_input(grad),)
reduced_input.defvjp(low_keep, low_pass)
reduced_backward.defvjp(back_keep, back_low)

def split_tiles(conv_three, conv_one):
    tile = conv_three.shape[1] // 2
    first = conv_three.reshape(9, 2, tile, 2, tile).transpose(0, 1, 3, 2, 4).reshape(36, tile, tile)
    second = conv_one.reshape(2, tile, 2, tile).transpose(0, 2, 1, 3).reshape(4, tile, tile)
    return jnp.concatenate([first, second], axis=0)

def join_tiles(tiles):
    tile = tiles.shape[1]
    conv_three = tiles[:36].reshape(9, 2, 2, tile, tile).transpose(0, 1, 3, 2, 4).reshape(9, 2 * tile, 2 * tile)
    conv_one = tiles[36:].reshape(2, 2, tile, tile).transpose(0, 2, 1, 3).reshape(2 * tile, 2 * tile)
    return (conv_three, conv_one)

def conv_taps(framed, kernel, height, breadth):
    total = None
    for position in range(9):
        row_off = position // 3
        col_off = position % 3
        term = jnp.einsum('nrcx,xy->nrcy', framed[:, row_off:row_off + height, col_off:col_off + breadth], kernel[position], precision=EXACT_PRECISION)
        total = term if total is None else total + term
    return total

def forward(features, tiles, proj, code, decoder, alive, count):
    kernel, mixer = join_tiles(reduced_input(tiles))
    height, breadth = (features.shape[1], features.shape[2])
    activated = reduced_input(jax.nn.gelu(features))
    framed = jnp.pad(activated, ((0, 0), (1, 1), (1, 1), (0, 0)))
    preact = reduced_backward(conv_taps(framed, kernel, height, breadth))
    inner = reduced_input(jax.nn.gelu(preact))
    branch = reduced_backward(jnp.einsum('nrcx,xy->nrcy', inner, mixer, precision=EXACT_PRECISION))
    resid = features + branch
    latent_features = reduced_backward(jnp.einsum('nrcx,xl->nrcl', reduced_input(resid), reduced_input(proj), precision=EXACT_PRECISION))
    codebook_reduced = reduced_input(code)
    codeword_norms = lax.optimization_barrier(jnp.sum(codebook_reduced * codebook_reduced, axis=1))
    assignment_scores = reduced_backward((2.0 * jnp.einsum('htzf,af->htza', reduced_input(latent_features), codebook_reduced, precision=EXACT_PRECISION) - codeword_norms) / SOFTMAX_WARMTH)
    probs = reduced_input(jax.nn.softmax(assignment_scores, axis=-1))
    quant = reduced_backward(jnp.einsum('nrck,kl->nrcl', probs, codebook_reduced, precision=EXACT_PRECISION))
    mask = alive[:, None, None, None]
    decoded = jnp.einsum('nrcl,ly->nrcy', reduced_input(quant), reduced_input(decoder), precision=EXACT_PRECISION) * mask
    diff = latent_features - quant
    loss = LOSS_WEIGHT * jnp.sum(lax.optimization_barrier(jnp.sum(diff * diff, axis=-1)) * alive[:, None, None]) / (count * latent_features.shape[-1])
    return (decoded, loss)

def ortho_step(stats, basis):
    moved = jnp.einsum('sij,sjk->sik', stats, basis, precision=EXACT_PRECISION)
    gram = jnp.einsum('sji,sjk->sik', moved, moved, precision=EXACT_PRECISION)
    factor = jnp.linalg.cholesky(gram)
    solved = jax.scipy.linalg.solve_triangular(factor, jnp.swapaxes(moved, 1, 2), lower=True)
    return jnp.swapaxes(solved, 1, 2)

def rotated_adam(gradient, master, first, second, left, right, basis_left, basis_right):
    turned = jnp.einsum('sji,sjk->sik', basis_left, gradient, precision=EXACT_PRECISION)
    turned = jnp.einsum('sik,skl->sil', turned, basis_right, precision=EXACT_PRECISION)
    first_new = BETA_ONE * first + (1.0 - BETA_ONE) * turned
    second_new = BETA_TWO * second + (1.0 - BETA_TWO) * turned * turned
    ratio = first_new / (1.0 - BETA_ONE ** STEP) / (jnp.sqrt(second_new / (1.0 - BETA_TWO ** STEP)) + EPSILON)
    back = jnp.einsum('sij,sjk->sik', basis_left, ratio, precision=EXACT_PRECISION)
    back = jnp.einsum('sik,slk->sil', back, basis_right, precision=EXACT_PRECISION)
    master_new = master - TILE_RATE * (back + WEIGHT_DECAY * master)
    left_new = BETA_TWO * left + (1.0 - BETA_TWO) * jnp.einsum('sik,sjk->sij', gradient, gradient, precision=EXACT_PRECISION)
    right_new = BETA_TWO * right + (1.0 - BETA_TWO) * jnp.einsum('ski,skj->sij', gradient, gradient, precision=EXACT_PRECISION)
    return (master_new, first_new, second_new, left_new, right_new, ortho_step(left_new, basis_left), ortho_step(right_new, basis_right))

def plain_adam(gradient, master, first, second, rate):
    first_new = BETA_ONE * first + (1.0 - BETA_ONE) * gradient
    second_new = BETA_TWO * second + (1.0 - BETA_TWO) * gradient * gradient
    ratio = first_new / (1.0 - BETA_ONE ** STEP) / (jnp.sqrt(second_new / (1.0 - BETA_TWO ** STEP)) + EPSILON)
    return (master - rate * (ratio + WEIGHT_DECAY * master), first_new, second_new)

def reference(features, cotangent, present, owners, tile_master, tile_mom1, tile_mom2, stat_left, stat_right, basis_left, basis_right, proj_master, proj_mom1, proj_mom2, dec_master, dec_mom1, dec_mom2, code_master, code_mom1, code_mom2):
    alive_all = present.astype(jnp.float32)
    count = jnp.sum(alive_all) * HEIGHT * WIDE
    tiles = jnp.take(tile_master, owners, axis=0)
    shape_in = (N_IMG, IMG_DEV, HEIGHT, WIDE, C)
    feature_blocks = features.reshape(shape_in)
    cot_blocks = cotangent.reshape(shape_in)
    alive_blocks = alive_all.reshape(N_IMG, IMG_DEV)

    def block(carry, item):
        feature_block, cot_block, alive_block = item

        def wrapped(feats, tile_arg, proj_arg, code_arg, dec_arg):
            return forward(feats, tile_arg, proj_arg, code_arg, dec_arg, alive_block, count)
        (decoded, loss), pull = jax.vjp(wrapped, feature_block.astype(jnp.float32), tiles, proj_master, code_master, dec_master)
        grads = pull((cot_block.astype(jnp.float32), jnp.ones((), jnp.float32)))
        updated = (carry[0] + grads[1], carry[1] + grads[2], carry[2] + grads[3], carry[3] + grads[4], carry[4] + loss)
        return (updated, (decoded.astype(jnp.bfloat16), grads[0].astype(jnp.bfloat16)))
    start = (jnp.zeros_like(tiles), jnp.zeros_like(proj_master), jnp.zeros_like(code_master), jnp.zeros_like(dec_master), jnp.zeros((), jnp.float32))
    totals, (decoded_all, grad_all) = lax.scan(block, start, (feature_blocks, cot_blocks, alive_blocks))
    grad_tiles, grad_proj, codebook_gradient, grad_dec, quant_loss = totals
    stacked = jnp.zeros_like(tile_master).at[owners].set(grad_tiles)
    tile_out = rotated_adam(stacked, tile_master, tile_mom1, tile_mom2, stat_left, stat_right, basis_left, basis_right)
    proj_out = plain_adam(grad_proj, proj_master, proj_mom1, proj_mom2, PROJ_RATE)
    dec_out = plain_adam(grad_dec, dec_master, dec_mom1, dec_mom2, DEC_RATE)
    code_out = plain_adam(codebook_gradient, code_master, code_mom1, code_mom2, CODE_RATE)
    full = (IMGS, HEIGHT, WIDE, C)
    return (decoded_all.reshape(full), grad_all.reshape(full), quant_loss, tile_out[0], tile_out[1], tile_out[2], tile_out[3], tile_out[4], tile_out[5], tile_out[6], proj_out[0], proj_out[1], proj_out[2], dec_out[0], dec_out[1], dec_out[2], code_out[0], code_out[1], code_out[2])
```

```python
import jax
import jax.numpy as jnp
from jax import lax
from jax.experimental import pallas as pl
from jax.experimental.pallas import tpu as pltpu
from jax.sharding import PartitionSpec as P

STEP = 5
HIGHEST = lax.Precision.HIGHEST
BETA_ONE = 0.9
BETA_TWO = 0.95
EPSILON = 1e-08
WEIGHT_DECAY = 0.01
SOFTMAX_WARMTH = 4.0
LOSS_WEIGHT = 1.25
TILE_RATE = 0.05
PROJ_RATE = 0.05
DEC_RATE = 0.1
CODE_RATE = 0.3

F32 = jnp.float32
BF16 = jnp.bfloat16
NN = ((1,), (0,))
NT = ((1,), (1,))
TN = ((0,), (0,))
GELU_A = 0.7978845608028654
GELU_B = 0.044715
VMEM_LIMIT = 56 * 1024 * 1024


def dot(a, b, dims=NN, precision=None):
    return lax.dot_general(a, b, (dims, ((), ())), precision=precision, preferred_element_type=F32)


def gelu_tanh(x):
    return jnp.tanh(GELU_A * (x + GELU_B * (x * x * x)))


def gelu(x):
    return 0.5 * x * (1.0 + gelu_tanh(x))


def gelu_both(x):
    square = x * x
    t = jnp.tanh(GELU_A * x * (1.0 + GELU_B * square))
    half = 0.5 * (1.0 + t)
    slope = half + 0.5 * x * (1.0 - t * t) * (GELU_A + 3.0 * GELU_A * GELU_B * square)
    return x * half, slope


def column_shifts(rows, wide):
    count = rows.shape[0]
    column = lax.broadcasted_iota(jnp.int32, rows.shape, 0) % wide
    before = jnp.where(column == 0, 0.0, pltpu.roll(rows, 1, 0))
    after = jnp.where(column == wide - 1, 0.0, pltpu.roll(rows, count - 1, 0))
    return before, after


def place_weights(place, gathered, weights, mixer):
    tile = gathered.shape[1]
    for t in range(40):
        block = gathered[place[t]]
        i, j = (t // 2) % 2, t % 2
        if t < 36:
            p = t // 4
            row = (p % 3) * 2 * tile + i * tile
            weights[p // 3, row : row + tile, j * tile : (j + 1) * tile] = block
        else:
            mixer[i * tile : (i + 1) * tile, j * tile : (j + 1) * tile] = block


def main_kernel(
    place,
    slots,
    alive_all,
    pull_all,
    core,
    feat,
    above,
    below,
    cot,
    gathered,
    proj,
    dec,
    code,
    norms,
    decoded,
    d_pre_out,
    d_resid_out,
    keep,
    send,
    g_proj,
    g_dec,
    g_code,
    totals,
    loss,
    weights,
    mixer,
    framed,
    d_pre_turned,
    sums,
    g_mixer,
):
    step = pl.program_id(0)
    steps = pl.num_programs(0)
    height, wide, channels = feat.shape[1:]
    count = height * wide
    tile = gathered.shape[1]

    @pl.when(step == 0)
    def _():
        place_weights(place, gathered, weights, mixer)
        g_mixer[...] = jnp.zeros_like(g_mixer)
        g_proj[...] = jnp.zeros_like(g_proj)
        g_dec[...] = jnp.zeros_like(g_dec)
        g_code[...] = jnp.zeros_like(g_code)
        totals[...] = jnp.zeros_like(totals)
        loss[...] = jnp.zeros_like(loss)

    alive = alive_all[step]
    pull = pull_all[step]
    feats = feat[0].reshape(count, channels).astype(F32)
    column = jnp.concatenate(
        [above[0, 0].astype(F32), feats, below[0, 0].astype(F32)], axis=0
    )
    activated = gelu(column)
    before, after = column_shifts(activated, wide)
    framed[step, :, 0:channels] = before.astype(BF16)
    framed[step, :, channels : 2 * channels] = activated.astype(BF16)
    framed[step, :, 2 * channels : 3 * channels] = after.astype(BF16)
    preact = dot(framed[step, 0:count, :], weights[0])
    preact += dot(framed[step, wide : wide + count, :], weights[1])
    preact += dot(framed[step, 2 * wide : 2 * wide + count, :], weights[2])
    inner_full, slope = gelu_both(preact)
    inner = inner_full.astype(BF16)
    resid_low = (feats + dot(inner, mixer[...])).astype(BF16)
    latent = dot(resid_low, proj[...])
    latent_low = latent.astype(BF16)
    logits = (2.0 / SOFTMAX_WARMTH) * dot(latent_low, code[...], NT) - norms[...]
    powers = jnp.exp(logits - jnp.max(logits, axis=1, keepdims=True))
    probs = powers * (1.0 / jnp.sum(powers, axis=1, keepdims=True))
    probs_low = probs.astype(BF16)
    quant = dot(probs_low, code[...])
    quant_low = quant.astype(BF16)
    decoded[0] = (dot(quant_low, dec[...]) * alive).astype(BF16).reshape(height, wide, channels)
    diff = latent - quant
    loss[...] += alive * jnp.sum(diff * diff, axis=0, keepdims=True)
    back_out = (cot[0].reshape(count, channels).astype(F32) * alive).astype(BF16)
    g_dec[...] += dot(quant_low, back_out, TN)
    pulled = pull * diff
    d_quant = (dot(back_out, dec[...], NT) - pulled).astype(BF16)
    d_probs = dot(d_quant, code[...], NT)
    d_logits = probs * (d_probs - jnp.sum(probs * d_probs, axis=1, keepdims=True))
    d_logits = d_logits.astype(BF16)
    totals[...] += jnp.sum(d_logits.astype(F32), axis=0, keepdims=True)
    g_code[...] += dot(d_quant, probs_low, TN) + (2.0 / SOFTMAX_WARMTH) * dot(
        latent_low, d_logits, TN
    )
    d_latent = ((2.0 / SOFTMAX_WARMTH) * dot(d_logits, code[...]) + pulled).astype(BF16)
    g_proj[...] += dot(d_latent, resid_low, TN)
    d_resid = dot(d_latent, proj[...], NT).astype(BF16)
    d_resid_out[0] = d_resid.reshape(height, wide, channels)
    g_mixer[...] += dot(d_resid, inner, TN)
    d_pre = (slope * dot(d_resid, mixer[...], NT)).astype(BF16)
    d_pre_out[0] = d_pre.reshape(height, wide, channels)
    d_pre_turned[step] = d_pre.T

    @pl.when(step == steps - 1)
    def _():
        group = 4 if steps % 4 == 0 else 1
        sums[...] = jnp.zeros_like(sums)
        for line in range(3):

            def add(g, carry, line=line):
                total = None
                for n in range(group):
                    i = g * group + n
                    window = framed[i, line * wide : line * wide + count, :]
                    term = dot(d_pre_turned[i], window)
                    total = term if total is None else total + term
                sums[line] += total
                return carry

            lax.fori_loop(0, steps // group, add, 0)
        for ref in (keep, send):
            ref[...] = jnp.zeros_like(ref)
        quarter = tile // 4
        for t in range(40):
            i, j = (t // 2) % 2, t % 2
            if t < 36:
                p = t // 4
                left = (p % 3) * channels + i * tile
                block = sums[p // 3, j * tile : (j + 1) * tile, left : left + tile]
            else:
                block = g_mixer[j * tile : (j + 1) * tile, i * tile : (i + 1) * tile]
            block = block.astype(BF16)
            for q in range(4):
                part = block[q * quarter : (q + 1) * quarter]

                @pl.when(core[0] == q % 2)
                def _(part=part, q=q, t=t):
                    keep[q // 2, slots[t]] = part

                @pl.when(core[0] != q % 2)
                def _(part=part, q=q, t=t):
                    send[q // 2, slots[t]] = part


def main_call(place, slots, alive, pull, core, feat, above, below, cot, gathered, proj, dec, code, norms):
    images, height, wide, channels = feat.shape
    latent = proj.shape[1]
    words = code.shape[0]
    slot_count, tile = gathered.shape[:2]
    smem = pl.BlockSpec(memory_space=pltpu.SMEM)
    strip = pl.BlockSpec((1, height, wide, channels), lambda i: (i, 0, 0, 0))
    line = pl.BlockSpec((1, 1, wide, channels), lambda i: (i, 0, 0, 0))

    def whole(shape):
        return pl.BlockSpec(shape, lambda i: (0,) * len(shape))

    big = jax.ShapeDtypeStruct(feat.shape, BF16)
    part = (2, slot_count, tile // 4, tile)
    shapes = (
        big,
        big,
        big,
        jax.ShapeDtypeStruct(part, BF16),
        jax.ShapeDtypeStruct(part, BF16),
        jax.ShapeDtypeStruct((latent, channels), F32),
        jax.ShapeDtypeStruct((latent, channels), F32),
        jax.ShapeDtypeStruct((latent, words), F32),
        jax.ShapeDtypeStruct((1, words), F32),
        jax.ShapeDtypeStruct((1, latent), F32),
    )
    return pl.pallas_call(
        main_kernel,
        grid=(images,),
        in_specs=[smem] * 5
        + [strip, line, line, strip]
        + [whole(a.shape) for a in (gathered, proj, dec, code, norms)],
        out_specs=[strip] * 3 + [whole(s.shape) for s in shapes[3:]],
        out_shape=shapes,
        scratch_shapes=[
            pltpu.VMEM((3, 3 * channels, channels), BF16),
            pltpu.VMEM((channels, channels), BF16),
            pltpu.VMEM((images, (height + 2) * wide, 3 * channels), BF16),
            pltpu.VMEM((images, channels, height * wide), BF16),
            pltpu.VMEM((3, channels, 3 * channels), F32),
            pltpu.VMEM((channels, channels), F32),
        ],
        compiler_params=pltpu.CompilerParams(vmem_limit_bytes=VMEM_LIMIT),
    )(place, slots, alive, pull, core, feat, above, below, cot, gathered, proj, dec, code, norms)


def input_kernel(place, feat, d_resid, d_pre, above, below, gathered, out, weights, mixer):
    height, wide, channels = feat.shape[1:]
    count = height * wide

    @pl.when(pl.program_id(0) == 0)
    def _():
        place_weights(place, gathered, weights, mixer)

    column = jnp.concatenate(
        [
            above[0, 0].astype(F32),
            d_pre[0].reshape(count, channels).astype(F32),
            below[0, 0].astype(F32),
        ],
        axis=0,
    )
    before, after = column_shifts(column, wide)
    sides = (after.astype(BF16), column.astype(BF16), before.astype(BF16))
    d_act = None
    for line in range(3):
        for side in range(3):
            window = sides[side][(2 - line) * wide : (2 - line) * wide + count]
            term = dot(window, weights[line, side * channels : (side + 1) * channels, :], NT)
            d_act = term if d_act is None else d_act + term
    _, slope = gelu_both(feat[0].reshape(count, channels).astype(F32))
    total = d_resid[0].reshape(count, channels).astype(F32) + slope * d_act
    out[0] = total.astype(BF16).reshape(height, wide, channels)


def input_call(place, feat, d_resid, d_pre, above, below, gathered):
    images, height, wide, channels = feat.shape
    strip = pl.BlockSpec((1, height, wide, channels), lambda i: (i, 0, 0, 0))
    line = pl.BlockSpec((1, 1, wide, channels), lambda i: (i, 0, 0, 0))
    return pl.pallas_call(
        input_kernel,
        grid=(images,),
        in_specs=[
            pl.BlockSpec(memory_space=pltpu.SMEM),
            strip,
            strip,
            strip,
            line,
            line,
            pl.BlockSpec(gathered.shape, lambda i: (0, 0, 0)),
        ],
        out_specs=strip,
        out_shape=jax.ShapeDtypeStruct(feat.shape, BF16),
        scratch_shapes=[
            pltpu.VMEM((3, 3 * channels, channels), BF16),
            pltpu.VMEM((channels, channels), BF16),
        ],
        compiler_params=pltpu.CompilerParams(vmem_limit_bytes=VMEM_LIMIT),
    )(place, feat, d_resid, d_pre, above, below, gathered)


BLOCK = 32


def inverse_factors(blocks):
    size = BLOCK
    lane = lax.broadcasted_iota(jnp.int32, (8, 128), 1)
    sub = lax.broadcasted_iota(jnp.int32, (8, 128), 0)
    mats = []
    for block in blocks:
        wide = jnp.concatenate([block, jnp.zeros((size, 128 - size), F32)], axis=1)
        mats.append(
            [
                wide[8 * v : 8 * v + 8] + jnp.where(lane == sub + (8 * v + size), 1.0, 0.0)
                for v in range(size // 8)
            ]
        )
    for k in range(size):
        v0, s0 = k // 8, k % 8
        for rows in mats:
            pivot = rows[v0][s0 : s0 + 1, :]
            scaled = jnp.broadcast_to(pivot * (1.0 / pivot[:, k : k + 1]), (8, 128))
            for v in range(v0, size // 8):
                if v == v0 and s0 == 7:
                    continue
                col = jnp.broadcast_to(rows[v][:, k : k + 1], (8, 128))
                if v == v0:
                    col = jnp.where(sub > s0, col, 0.0)
                rows[v] = rows[v] - col * scaled
    out = []
    for rows in mats:
        done = []
        for v in range(size // 8):
            diagonal = jnp.where(lane == sub + 8 * v, rows[v], 0.0)
            diagonal = jnp.sum(diagonal, axis=1, keepdims=True)
            done.append((rows[v] * lax.rsqrt(diagonal))[:, size : 2 * size])
        out.append(jnp.concatenate(done, axis=0))
    return out


def tile_kernel(
    turned_grad, master, first, second, left, right, basis_left, basis_right,
    master_new, first_new, second_new, left_new, right_new, basis_left_new, basis_right_new,
    work,
):
    count, tile = master.shape[:2]
    for t in range(count):
        grad_t = turned_grad[t]
        left_new[t] = BETA_TWO * left[t] + (1.0 - BETA_TWO) * dot(grad_t, grad_t, TN, HIGHEST)
        right_new[t] = BETA_TWO * right[t] + (1.0 - BETA_TWO) * dot(grad_t, grad_t, NT, HIGHEST)
        for side, (stat, basis) in enumerate(((left_new, basis_left), (right_new, basis_right))):
            moved = dot(stat[t], basis[t], NN, HIGHEST)
            work[2 * t + side, :, :tile] = dot(moved, moved, TN, HIGHEST)
            work[2 * t + side, :, tile:] = moved.T
    for t in range(count):
        turned = dot(basis_left[t], turned_grad[t], ((0,), (1,)), HIGHEST)
        turned = dot(turned, basis_right[t], NN, HIGHEST)
        mom = BETA_ONE * first[t] + (1.0 - BETA_ONE) * turned
        var = BETA_TWO * second[t] + (1.0 - BETA_TWO) * turned * turned
        first_new[t] = mom
        second_new[t] = var
        ratio = mom / (1.0 - BETA_ONE**STEP) / (jnp.sqrt(var / (1.0 - BETA_TWO**STEP)) + EPSILON)
        back = dot(dot(basis_left[t], ratio, NN, HIGHEST), basis_right[t], NT, HIGHEST)
        master_new[t] = master[t] - TILE_RATE * (back + WEIGHT_DECAY * master[t])
    for low in range(0, tile, BLOCK):
        high = low + BLOCK
        factors = inverse_factors([work[n, low:high, low:high] for n in range(2 * count)])
        for n in range(2 * count):
            panel = dot(factors[n], work[n, low:high, :], NN, HIGHEST)
            work[n, low:high, :] = panel
            if high < tile:
                work[n, high:, :] = work[n, high:, :] - dot(panel[:, high:tile], panel, TN, HIGHEST)
    for t in range(count):
        basis_left_new[t] = work[2 * t, :, tile:].T
        basis_right_new[t] = work[2 * t + 1, :, tile:].T


def tile_call(turned_grad, *arrays):
    shape = jax.ShapeDtypeStruct(turned_grad.shape, F32)
    vmem = pl.BlockSpec(memory_space=pltpu.VMEM)
    count, tile = turned_grad.shape[:2]
    return pl.pallas_call(
        tile_kernel,
        in_specs=[vmem] * 8,
        out_specs=(vmem,) * 7,
        out_shape=(shape,) * 7,
        scratch_shapes=[pltpu.VMEM((2 * count, tile, 2 * tile), F32)],
        compiler_params=pltpu.CompilerParams(vmem_limit_bytes=VMEM_LIMIT),
    )(turned_grad, *arrays)


def plain_adam(gradient, master, first, second, rate):
    first_new = BETA_ONE * first + (1.0 - BETA_ONE) * gradient
    second_new = BETA_TWO * second + (1.0 - BETA_TWO) * gradient * gradient
    ratio = (
        first_new
        / (1.0 - BETA_ONE**STEP)
        / (jnp.sqrt(second_new / (1.0 - BETA_TWO**STEP)) + EPSILON)
    )
    return (master - rate * (ratio + WEIGHT_DECAY * master), first_new, second_new)


def swap(x, axis, distance):
    count = lax.axis_size(axis)
    return lax.ppermute(x, axis, [(i, i ^ distance) for i in range(count)])


def edges(rows):
    ends = lax.axis_size("strip") - 1
    above = lax.ppermute(rows[:, -1:], "strip", [(i, i + 1) for i in range(ends)])
    below = lax.ppermute(rows[:, :1], "strip", [(i + 1, i) for i in range(ends)])
    return above, below


def gather_tiles(mine):
    core = lax.axis_index("strip") % 2
    half = mine.shape[1] // 2
    part = lax.dynamic_slice_in_dim(mine, core * half, half, axis=1)
    parts = [part] + [swap(part, "img", d) for d in range(1, lax.axis_size("img"))]
    mine_half = jnp.stack(parts)
    other_half = swap(mine_half, "strip", 1)
    low = jnp.where(core == 0, mine_half, other_half)
    high = jnp.where(core == 0, other_half, mine_half)
    whole = jnp.concatenate([low, high], axis=2)
    return whole.reshape(-1, *mine.shape[1:])


def reduce_tiles(keep, send, tiles):
    strip = lax.axis_index("strip")
    across = strip // 2
    img = lax.axis_index("img")
    groups = lax.axis_size("img")
    half = keep + swap(send, "strip", 1)
    other = lax.dynamic_index_in_dim(half, 1 - across, 0, False)
    quarter = lax.dynamic_index_in_dim(half, across, 0, False) + swap(other, "strip", 2)
    quarter = quarter.reshape(groups, tiles, *quarter.shape[1:])
    total = lax.dynamic_index_in_dim(quarter, img, 0, False).astype(F32)
    for d in range(1, groups):
        piece = lax.dynamic_index_in_dim(quarter, img ^ d, 0, False)
        total = total + swap(piece, "img", d).astype(F32)
    parts = jnp.stack([total] + [swap(total, "strip", d) for d in range(1, 4)])
    ordered = [lax.dynamic_index_in_dim(parts, strip_of ^ strip, 0, False) for strip_of in range(4)]
    return ordered


def body(
    features,
    cotangent,
    present,
    owners,
    tile_master,
    tile_mom1,
    tile_mom2,
    stat_left,
    stat_right,
    basis_left,
    basis_right,
    proj_master,
    proj_mom1,
    proj_mom2,
    dec_master,
    dec_mom1,
    dec_mom2,
    code_master,
    code_mom1,
    code_mom2,
):
    images, height, wide, channels = features.shape
    tiles = tile_master.shape[0]
    img = lax.axis_index("img")
    strip = lax.axis_index("strip")
    gathered = gather_tiles(tile_master.astype(BF16))
    place = ((owners // tiles) ^ img) * tiles + owners % tiles
    alive = lax.dynamic_slice_in_dim(present, img * images, images).astype(F32)
    count = jnp.sum(present).astype(F32) * (height * lax.axis_size("strip") * wide)
    latent = proj_master.shape[1]
    scale = LOSS_WEIGHT / (count * latent)
    code_low = code_master.astype(BF16)
    code_full = code_low.astype(F32)
    norms = jnp.sum(code_full * code_full, axis=1)[None] / SOFTMAX_WARMTH
    above, below = edges(features)
    (decoded, d_pre, d_resid, keep, send, g_proj, g_dec, g_code, totals, loss) = main_call(
        place,
        owners,
        alive,
        2.0 * scale * alive,
        (strip % 2).reshape(1),
        features,
        above,
        below,
        cotangent,
        gathered,
        proj_master.astype(BF16),
        dec_master.astype(BF16),
        code_low,
        norms,
    )
    above, below = edges(d_pre)
    small = lax.psum((g_proj, g_dec, g_code, totals, loss), ("strip", "img"))
    input_grad = input_call(place, features, d_resid, d_pre, above, below, gathered)
    ordered = reduce_tiles(keep, send, tiles)
    owned = jnp.concatenate([ordered[0], ordered[1], ordered[2], ordered[3]], axis=1)
    tile_out = tile_call(
        owned, tile_master, tile_mom1, tile_mom2, stat_left, stat_right, basis_left, basis_right
    )
    quant_loss = scale * jnp.sum(small[4])
    g_code_all = small[2].T - (2.0 / SOFTMAX_WARMTH) * small[3][0][:, None] * code_full
    proj_out = plain_adam(small[0].T, proj_master, proj_mom1, proj_mom2, PROJ_RATE)
    dec_out = plain_adam(small[1], dec_master, dec_mom1, dec_mom2, DEC_RATE)
    code_out = plain_adam(g_code_all, code_master, code_mom1, code_mom2, CODE_RATE)
    return (decoded, input_grad, quant_loss, *tile_out, *proj_out, *dec_out, *code_out)


def solution(mesh):
    big = P("img", "strip", None, None)
    tile = P("img", None, None)
    in_specs = (big, big, P(), P()) + (tile,) * 7 + (P(),) * 9
    out_specs = (big, big, P()) + (tile,) * 7 + (P(),) * 9
    return jax.shard_map(body, mesh=mesh, in_specs=in_specs, out_specs=out_specs, check_vma=False)
```

```python
import jax
import jax.numpy as jnp
from jax import lax
from jax.experimental import pallas as pl
from jax.experimental.pallas import tpu as pltpu
from jax.sharding import PartitionSpec as P

STEP = 5
HIGHEST = lax.Precision.HIGHEST
BETA_ONE = 0.9
BETA_TWO = 0.95
EPSILON = 1e-08
WEIGHT_DECAY = 0.01
SOFTMAX_WARMTH = 4.0
LOSS_WEIGHT = 1.25
TILE_RATE = 0.05
PROJ_RATE = 0.05
DEC_RATE = 0.1
CODE_RATE = 0.3

F32 = jnp.float32
BF16 = jnp.bfloat16
NN = ((1,), (0,))
NT = ((1,), (1,))
TN = ((0,), (0,))
GELU_A = 0.7978845608028654
GELU_B = 0.044715
VMEM_LIMIT = 56 * 1024 * 1024


def dot(a, b, dims=NN, precision=None):
    return lax.dot_general(a, b, (dims, ((), ())), precision=precision, preferred_element_type=F32)


def gelu_tanh(x):
    return jnp.tanh(GELU_A * (x + GELU_B * (x * x * x)))


def gelu(x):
    return 0.5 * x * (1.0 + gelu_tanh(x))


def gelu_both(x):
    square = x * x
    t = jnp.tanh(GELU_A * x * (1.0 + GELU_B * square))
    half = 0.5 * (1.0 + t)
    slope = half + 0.5 * x * (1.0 - t * t) * (GELU_A + 3.0 * GELU_A * GELU_B * square)
    return x * half, slope


def column_shifts(rows, wide):
    count = rows.shape[0]
    column = lax.broadcasted_iota(jnp.int32, rows.shape, 0) % wide
    before = jnp.where(column == 0, 0.0, pltpu.roll(rows, 1, 0))
    after = jnp.where(column == wide - 1, 0.0, pltpu.roll(rows, count - 1, 0))
    return before, after


def place_weights(place, parts, core, put):
    half = parts[0].shape[1]
    count = len(parts) // 2
    size = parts[0].shape[0]
    for t in range(40):
        which = place[t] // size
        index = place[t] % size
        for side in range(2):
            block = parts[side * count][index]
            for n in range(1, count):
                block = jnp.where(which == n, parts[side * count + n][index], block)
            put(t, block, pl.multiple_of((core ^ side) * half, half))


def shift_lines(line, first, last):
    wide = line.shape[0]
    before = jnp.where(first, 0.0, pltpu.roll(line, 1, 0)).astype(BF16)
    after = jnp.where(last, 0.0, pltpu.roll(line, wide - 1, 0)).astype(BF16)
    return before, after


def main_kernel(batch, part_count, *refs):
    place, slots, alive_all, pull_all, core = refs[:5]
    feat, near, far, cot = refs[5:9]
    parts = refs[9 : 9 + part_count]
    proj, dec, code, norms = refs[9 + part_count : 13 + part_count]
    (decoded, d_pre_out, d_resid_out, near_out, far_out, keep, send, small) = refs[
        13 + part_count : 21 + part_count
    ]
    (weights, mixer, framed, d_pre_turned, sums, g_mixer, g_proj, g_dec, g_code, totals, loss) = refs[
        21 + part_count :
    ]
    step = pl.program_id(0)
    steps = pl.num_programs(0)
    height, wide, channels = feat.shape[1:]
    count = height * wide
    tile = parts[0].shape[2]
    half = tile // 2
    images = framed.shape[0]
    lead = core[0] == 0

    @pl.when(step == 0)
    def _():
        def put(t, block, row):
            i, j = (t // 2) % 2, t % 2
            if t < 36:
                p = t // 4
                start = (p % 3) * channels + i * tile
                weights[p // 3, pl.ds(start + row, half), j * tile : (j + 1) * tile] = block
            else:
                mixer[pl.ds(i * tile + row, half), j * tile : (j + 1) * tile] = block

        place_weights(place, parts, core[0], put)
        for ref in (g_mixer, g_proj, g_dec, g_code, totals, loss):
            ref[...] = jnp.zeros_like(ref)

    column = lax.broadcasted_iota(jnp.int32, (wide, channels), 0)
    first = column == 0
    last = column == wide - 1

    def chain(n):
        image = step * batch + n
        alive = alive_all[image]
        pull = pull_all[image]
        for r in range(height + 2):
            if r == 0:
                line = jnp.where(lead, far[n].astype(F32), near[n].astype(F32))
            elif r == height + 1:
                line = jnp.where(lead, near[n].astype(F32), far[n].astype(F32))
            else:
                line = feat[n, r - 1].astype(F32)
            line = gelu(line)
            before, after = shift_lines(line, first, last)
            rows = slice(r * wide, (r + 1) * wide)
            framed[image, rows, 0:channels] = before
            framed[image, rows, channels : 2 * channels] = line.astype(BF16)
            framed[image, rows, 2 * channels :] = after
        yield
        preact = dot(framed[image, 0:count, :], weights[0])
        preact += dot(framed[image, wide : wide + count, :], weights[1])
        preact += dot(framed[image, 2 * wide : 2 * wide + count, :], weights[2])
        yield
        inner, slope = gelu_both(preact)
        inner = inner.astype(BF16)
        yield
        feats = feat[n].reshape(count, channels).astype(F32)
        resid = (feats + dot(inner, mixer[...])).astype(BF16)
        yield
        latent = dot(resid, proj[...])
        latent_low = latent.astype(BF16)
        yield
        logits = (2.0 / SOFTMAX_WARMTH) * dot(latent_low, code[...], NT) - norms[...]
        yield
        powers = jnp.exp(logits - jnp.max(logits, axis=1, keepdims=True))
        probs = powers * (1.0 / jnp.sum(powers, axis=1, keepdims=True))
        probs_low = probs.astype(BF16)
        yield
        quant = dot(probs_low, code[...])
        quant_low = quant.astype(BF16)
        yield
        out = (dot(quant_low, dec[...]) * alive).astype(BF16)
        decoded[n] = out.reshape(height, wide, channels)
        diff = latent - quant
        loss[...] += alive * jnp.sum(diff * diff, axis=0, keepdims=True)
        back_out = (cot[n].reshape(count, channels).astype(F32) * alive).astype(BF16)
        pulled = pull * diff
        d_quant = (dot(back_out, dec[...], NT) - pulled).astype(BF16)
        g_dec[...] += dot(quant_low, back_out, TN)
        yield
        d_probs = dot(d_quant, code[...], NT)
        yield
        d_logits = probs * (d_probs - jnp.sum(probs * d_probs, axis=1, keepdims=True))
        d_logits = d_logits.astype(BF16)
        totals[...] += jnp.sum(d_logits.astype(F32), axis=0, keepdims=True)
        yield
        d_latent = ((2.0 / SOFTMAX_WARMTH) * dot(d_logits, code[...]) + pulled).astype(BF16)
        yield
        d_resid = dot(d_latent, proj[...], NT).astype(BF16)
        d_resid_out[n] = d_resid.reshape(height, wide, channels)
        g_code[...] += dot(d_quant, probs_low, TN)
        g_code[...] += (2.0 / SOFTMAX_WARMTH) * dot(latent_low, d_logits, TN)
        yield
        d_pre = (slope * dot(d_resid, mixer[...], NT)).astype(BF16)
        g_proj[...] += dot(d_latent, resid, TN)
        yield
        d_pre_out[n] = d_pre.reshape(height, wide, channels)
        top, bottom = d_pre[:wide], d_pre[count - wide :]
        near_out[n] = jnp.where(lead, bottom, top)
        far_out[n] = jnp.where(lead, top, bottom)
        g_mixer[...] += dot(d_resid, inner, TN)
        yield
        d_pre_turned[image] = d_pre.T

    live = [chain(n) for n in range(batch)]
    while live:
        live = [c for c in live if next(c, True) is None]

    @pl.when(step == steps - 1)
    def _():
        group = 4 if images % 4 == 0 else 1
        sums[...] = jnp.zeros_like(sums)
        for line in range(3):

            def add(g, carry, line=line):
                total = None
                for n in range(group):
                    i = g * group + n
                    window = framed[i, line * wide : line * wide + count, :]
                    term = dot(d_pre_turned[i], window)
                    total = term if total is None else total + term
                sums[line] += total
                return carry

            lax.fori_loop(0, images // group, add, 0)
        for ref in (keep, send):
            ref[...] = jnp.zeros_like(ref)
        quarter = tile // 4
        for t in range(40):
            i, j = (t // 2) % 2, t % 2
            if t < 36:
                p = t // 4
                left = (p % 3) * channels + i * tile
                block = sums[p // 3, j * tile : (j + 1) * tile, left : left + tile]
            else:
                block = g_mixer[j * tile : (j + 1) * tile, i * tile : (i + 1) * tile]
            block = block.astype(BF16)
            for q in range(0, 4, 2):
                even = block[q * quarter : (q + 1) * quarter]
                odd = block[(q + 1) * quarter : (q + 2) * quarter]
                keep[q // 2, slots[t]] = jnp.where(lead, even, odd)
                send[q // 2, slots[t]] = jnp.where(lead, odd, even)
        code_turned = code[...].astype(F32).T
        g_words = g_code[...] - (2.0 / SOFTMAX_WARMTH) * totals[...] * code_turned
        row = 0
        for grad in (g_proj[...], g_dec[...], g_words):
            for left in range(0, grad.shape[1], 128):
                small[row : row + grad.shape[0]] = grad[:, left : left + 128].astype(BF16)
                row += grad.shape[0]
        small[row:] = jnp.zeros((small.shape[0] - row, 128), BF16)
        small[row : row + 16, 0 : loss.shape[1]] = jnp.broadcast_to(
            loss[...] * (1.0 / 16.0), (16, loss.shape[1])
        ).astype(BF16)


def main_call(place, slots, alive, pull, core, feat, near, far, cot, parts, proj, dec, code, norms):
    images, height, wide, channels = feat.shape
    latent = proj.shape[1]
    words = code.shape[0]
    size, half, tile = parts[0].shape
    slot_count = size * len(parts) // 2
    batch = 4 if images % 4 == 0 else 1
    smem = pl.BlockSpec(memory_space=pltpu.SMEM)
    strip = pl.BlockSpec((batch, height, wide, channels), lambda i: (i, 0, 0, 0))
    line = pl.BlockSpec((batch, wide, channels), lambda i: (i, 0, 0))

    def whole(shape):
        return pl.BlockSpec(shape, lambda i: (0,) * len(shape))

    big = jax.ShapeDtypeStruct(feat.shape, BF16)
    edge = jax.ShapeDtypeStruct(near.shape, BF16)
    part = jax.ShapeDtypeStruct((2, slot_count, tile // 4, tile), BF16)
    rows = (2 * latent * channels + latent * words) // 128 + 16
    shapes = (big, big, big, edge, edge, part, part, jax.ShapeDtypeStruct((rows, 128), BF16))
    return pl.pallas_call(
        lambda *refs: main_kernel(batch, len(parts), *refs),
        grid=(images // batch,),
        in_specs=[smem] * 5
        + [strip, line, line, strip]
        + [whole(a.shape) for a in (*parts, proj, dec, code, norms)],
        out_specs=[strip] * 3 + [line] * 2 + [whole(s.shape) for s in shapes[5:]],
        out_shape=shapes,
        scratch_shapes=[
            pltpu.VMEM((3, 3 * channels, channels), BF16),
            pltpu.VMEM((channels, channels), BF16),
            pltpu.VMEM((images, (height + 2) * wide, 3 * channels), BF16),
            pltpu.VMEM((images, channels, height * wide), BF16),
            pltpu.VMEM((3, channels, 3 * channels), F32),
            pltpu.VMEM((channels, channels), F32),
            pltpu.VMEM((latent, channels), F32),
            pltpu.VMEM((latent, channels), F32),
            pltpu.VMEM((latent, words), F32),
            pltpu.VMEM((1, words), F32),
            pltpu.VMEM((1, latent), F32),
        ],
        compiler_params=pltpu.CompilerParams(vmem_limit_bytes=VMEM_LIMIT),
        name="main",
    )(place, slots, alive, pull, core, feat, near, far, cot, *parts, proj, dec, code, norms)


def input_kernel(batch, part_count, *refs):
    place, core, feat, d_resid, d_pre, near, far = refs[:7]
    parts = refs[7 : 7 + part_count]
    out, weights = refs[7 + part_count :]
    height, wide, channels = feat.shape[1:]
    count = height * wide
    tile = parts[0].shape[2]
    half = tile // 2
    lead = core[0] == 0

    @pl.when(pl.program_id(0) == 0)
    def _():
        def put(t, block, row):
            if t < 36:
                i, j = (t // 2) % 2, t % 2
                p = t // 4
                start = (2 - p % 3) * channels + i * tile
                weights[2 - p // 3, pl.ds(start + row, half), j * tile : (j + 1) * tile] = block

        place_weights(place, parts, core[0], put)

    column = lax.broadcasted_iota(jnp.int32, (wide, channels), 0)
    first = column == 0
    last = column == wide - 1
    for n in range(batch):
        lines = []
        for r in range(height + 2):
            if r == 0:
                line = jnp.where(lead, far[n], near[n])
            elif r == height + 1:
                line = jnp.where(lead, near[n], far[n])
            else:
                line = d_pre[n, r - 1]
            before, after = shift_lines(line.astype(F32), first, last)
            lines.append((before, line, after))
        sides = [jnp.concatenate([l[s] for l in lines], axis=0) for s in range(3)]
        d_act = None
        for line in range(3):
            for side in range(3):
                window = sides[side][line * wide : line * wide + count]
                term = dot(window, weights[line, side * channels : (side + 1) * channels, :], NT)
                d_act = term if d_act is None else d_act + term
        _, slope = gelu_both(feat[n].reshape(count, channels).astype(F32))
        total = d_resid[n].reshape(count, channels).astype(F32) + slope * d_act
        out[n] = total.astype(BF16).reshape(height, wide, channels)


def input_call(place, core, feat, d_resid, d_pre, near, far, parts):
    images, height, wide, channels = feat.shape
    batch = 4 if images % 4 == 0 else 1
    smem = pl.BlockSpec(memory_space=pltpu.SMEM)
    strip = pl.BlockSpec((batch, height, wide, channels), lambda i: (i, 0, 0, 0))
    line = pl.BlockSpec((batch, wide, channels), lambda i: (i, 0, 0))
    return pl.pallas_call(
        lambda *refs: input_kernel(batch, len(parts), *refs),
        grid=(images // batch,),
        in_specs=[smem, smem, strip, strip, strip, line, line]
        + [pl.BlockSpec(p.shape, lambda i: (0, 0, 0)) for p in parts],
        out_specs=strip,
        out_shape=jax.ShapeDtypeStruct(feat.shape, BF16),
        scratch_shapes=[pltpu.VMEM((3, 3 * channels, channels), BF16)],
        compiler_params=pltpu.CompilerParams(vmem_limit_bytes=VMEM_LIMIT),
        name="input_grad",
    )(place, core, feat, d_resid, d_pre, near, far, *parts)


BLOCK = 32


def inverse_factors(blocks):
    size = BLOCK
    lane = lax.broadcasted_iota(jnp.int32, (8, 128), 1)
    sub = lax.broadcasted_iota(jnp.int32, (8, 128), 0)
    mats = []
    for block in blocks:
        wide = jnp.concatenate([block, jnp.zeros((size, 128 - size), F32)], axis=1)
        mats.append(
            [
                wide[8 * v : 8 * v + 8] + jnp.where(lane == sub + (8 * v + size), 1.0, 0.0)
                for v in range(size // 8)
            ]
        )
    for k in range(size):
        v0, s0 = k // 8, k % 8
        for rows in mats:
            pivot = rows[v0][s0 : s0 + 1, :]
            scaled = jnp.broadcast_to(pivot * (1.0 / pivot[:, k : k + 1]), (8, 128))
            for v in range(v0, size // 8):
                if v == v0 and s0 == 7:
                    continue
                col = jnp.broadcast_to(rows[v][:, k : k + 1], (8, 128))
                if v == v0:
                    col = jnp.where(sub > s0, col, 0.0)
                rows[v] = rows[v] - col * scaled
    out = []
    for rows in mats:
        done = []
        for v in range(size // 8):
            diagonal = jnp.where(lane == sub + 8 * v, rows[v], 0.0)
            diagonal = jnp.sum(diagonal, axis=1, keepdims=True)
            done.append((rows[v] * lax.rsqrt(diagonal))[:, size : 2 * size])
        out.append(jnp.concatenate(done, axis=0))
    return out


def tile_kernel(
    turned_grad, master, first, second, left, right, basis_left, basis_right,
    master_new, first_new, second_new, left_new, right_new, basis_left_new, basis_right_new,
    work,
):
    count, tile = master.shape[:2]
    for t in range(count):
        grad_t = turned_grad[t]
        left_new[t] = BETA_TWO * left[t] + (1.0 - BETA_TWO) * dot(grad_t, grad_t, TN, HIGHEST)
        right_new[t] = BETA_TWO * right[t] + (1.0 - BETA_TWO) * dot(grad_t, grad_t, NT, HIGHEST)
        for side, (stat, basis) in enumerate(((left_new, basis_left), (right_new, basis_right))):
            moved = dot(stat[t], basis[t], NN, HIGHEST)
            work[2 * t + side, :, :tile] = dot(moved, moved, TN, HIGHEST)
            work[2 * t + side, :, tile:] = moved.T
    for t in range(count):
        turned = dot(basis_left[t], turned_grad[t], ((0,), (1,)), HIGHEST)
        turned = dot(turned, basis_right[t], NN, HIGHEST)
        mom = BETA_ONE * first[t] + (1.0 - BETA_ONE) * turned
        var = BETA_TWO * second[t] + (1.0 - BETA_TWO) * turned * turned
        first_new[t] = mom
        second_new[t] = var
        ratio = mom / (1.0 - BETA_ONE**STEP) / (jnp.sqrt(var / (1.0 - BETA_TWO**STEP)) + EPSILON)
        back = dot(dot(basis_left[t], ratio, NN, HIGHEST), basis_right[t], NT, HIGHEST)
        master_new[t] = master[t] - TILE_RATE * (back + WEIGHT_DECAY * master[t])
    for low in range(0, tile, BLOCK):
        high = low + BLOCK
        factors = inverse_factors([work[n, low:high, low:high] for n in range(2 * count)])
        for n in range(2 * count):
            panel = dot(factors[n], work[n, low:high, :], NN, HIGHEST)
            work[n, low:high, :] = panel
            if high < tile:
                work[n, high:, :] = work[n, high:, :] - dot(panel[:, high:tile], panel, TN, HIGHEST)
    for t in range(count):
        basis_left_new[t] = work[2 * t, :, tile:].T
        basis_right_new[t] = work[2 * t + 1, :, tile:].T


def tile_call(turned_grad, *arrays):
    shape = jax.ShapeDtypeStruct(turned_grad.shape, F32)
    vmem = pl.BlockSpec(memory_space=pltpu.VMEM)
    count, tile = turned_grad.shape[:2]
    return pl.pallas_call(
        tile_kernel,
        in_specs=[vmem] * 8,
        out_specs=(vmem,) * 7,
        out_shape=(shape,) * 7,
        scratch_shapes=[pltpu.VMEM((2 * count, tile, 2 * tile), F32)],
        compiler_params=pltpu.CompilerParams(vmem_limit_bytes=VMEM_LIMIT),
    )(turned_grad, *arrays)


def plain_adam(gradient, master, first, second, rate):
    first_new = BETA_ONE * first + (1.0 - BETA_ONE) * gradient
    second_new = BETA_TWO * second + (1.0 - BETA_TWO) * gradient * gradient
    ratio = (
        first_new
        / (1.0 - BETA_ONE**STEP)
        / (jnp.sqrt(second_new / (1.0 - BETA_TWO**STEP)) + EPSILON)
    )
    return (master - rate * (ratio + WEIGHT_DECAY * master), first_new, second_new)


def small_kernel(scale, one, two, *refs):
    arrays, outs = refs[:9], refs[9:]
    total = one[...].astype(F32) + two[...].astype(F32)
    row = 0
    for n, (rate, turned) in enumerate(((PROJ_RATE, True), (DEC_RATE, False), (CODE_RATE, True))):
        shape = arrays[3 * n].shape
        rows, columns = shape[::-1] if turned else shape
        pieces = []
        for _ in range(columns // 128):
            piece = total[row : row + rows]
            pieces.append(piece.T if turned else piece)
            row += rows
        grad = jnp.concatenate(pieces, axis=0 if turned else 1)
        new = plain_adam(grad, *(a[...] for a in arrays[3 * n : 3 * n + 3]), rate)
        for out, value in zip(outs[3 * n : 3 * n + 3], new):
            out[...] = value
    outs[9][...] = jnp.sum(total[row:], axis=(0, 1), keepdims=True) * scale[0]


def small_call(scale, one, two, arrays):
    smem = pl.BlockSpec(memory_space=pltpu.SMEM)
    vmem = pl.BlockSpec(memory_space=pltpu.VMEM)
    shapes = [jax.ShapeDtypeStruct(a.shape, F32) for a in arrays]
    shapes.append(jax.ShapeDtypeStruct((1, 1), F32))
    return pl.pallas_call(
        small_kernel,
        in_specs=[smem] + [vmem] * 11,
        out_specs=[vmem] * 10,
        out_shape=shapes,
        compiler_params=pltpu.CompilerParams(vmem_limit_bytes=VMEM_LIMIT),
        name="small_adam",
    )(scale, one, two, *arrays)


def swap(x, axis, distance):
    count = lax.axis_size(axis)
    return lax.ppermute(x, axis, [(i, i ^ distance) for i in range(count)])


def radices(count):
    out = []
    stride = 1
    while stride < count:
        left = (count // stride).bit_length() - 1
        radix = 2 if left % 2 else 4
        out.append((radix, stride))
        stride *= radix
    return out


def swap_edges(near, far):
    return swap(near, "strip", 1), lax.ppermute(far, "strip", [(1, 2), (2, 1)])


def gather_tiles(mine):
    core = lax.axis_index("strip") % 2
    half = mine.shape[1] // 2
    part = lax.dynamic_slice_in_dim(mine, core * half, half, axis=1)
    steps = radices(lax.axis_size("img"))[::-1]
    for number, (radix, stride) in enumerate(steps):
        parts = [part] + [swap(part, "img", d * stride) for d in range(1, radix)]
        if number < len(steps) - 1:
            part = jnp.concatenate(parts, axis=0)
    return parts + [swap(p, "strip", 1) for p in parts]


def tile_place(owners, tiles):
    distance = (owners // tiles) ^ lax.axis_index("img")
    place = jnp.zeros_like(owners)
    size = 1
    for radix, stride in radices(lax.axis_size("img"))[::-1]:
        place = place + size * ((distance // stride) % radix)
        size *= radix
    return place * tiles + owners % tiles


def reduce_tiles(keep, send, tiles):
    strip = lax.axis_index("strip")
    across = strip // 2
    img = lax.axis_index("img")
    groups = lax.axis_size("img")
    half = keep + swap(send, "strip", 1)
    other = lax.dynamic_index_in_dim(half, 1 - across, 0, False)
    part = lax.dynamic_index_in_dim(half, across, 0, False) + swap(other, "strip", 2)
    left = groups
    for radix, stride in radices(groups):
        part = part.reshape(left // radix, radix, -1, *part.shape[-2:])
        low = (img // stride) % radix
        total = lax.dynamic_index_in_dim(part, low, 1, False).astype(F32)
        for d in range(1, radix):
            piece = lax.dynamic_index_in_dim(part, low ^ d, 1, False)
            total = total + swap(piece, "img", d * stride).astype(F32)
        part = total.astype(BF16)
        left //= radix
    total = total.reshape(tiles, *total.shape[-2:])
    parts = jnp.stack([total] + [swap(total, "strip", d) for d in range(1, 4)])
    ordered = [lax.dynamic_index_in_dim(parts, n ^ strip, 0, False) for n in range(4)]
    return jnp.concatenate(ordered, axis=1)


def reduce_small(small):
    steps = [("strip", 1), ("strip", 2)]
    for radix, stride in radices(lax.axis_size("img")):
        steps += [("img", stride << n) for n in range(radix.bit_length() - 1)]
    for number, (axis, distance) in enumerate(steps):
        other = swap(small, axis, distance)
        if number == len(steps) - 1:
            return small, other
        small = (small.astype(F32) + other.astype(F32)).astype(BF16)


def body(
    features,
    cotangent,
    present,
    owners,
    tile_master,
    tile_mom1,
    tile_mom2,
    stat_left,
    stat_right,
    basis_left,
    basis_right,
    proj_master,
    proj_mom1,
    proj_mom2,
    dec_master,
    dec_mom1,
    dec_mom2,
    code_master,
    code_mom1,
    code_mom2,
):
    images, height, wide, channels = features.shape
    tiles = tile_master.shape[0]
    img = lax.axis_index("img")
    strip = lax.axis_index("strip")
    core = strip % 2
    parts = gather_tiles(tile_master.astype(BF16))
    place = tile_place(owners, tiles)
    alive = lax.dynamic_slice_in_dim(present, img * images, images).astype(F32)
    count = jnp.sum(present).astype(F32) * (height * lax.axis_size("strip") * wide)
    latent = proj_master.shape[1]
    scale = LOSS_WEIGHT / (count * latent)
    code_low = code_master.astype(BF16)
    code_full = code_low.astype(F32)
    norms = jnp.sum(code_full * code_full, axis=1)[None] / SOFTMAX_WARMTH
    top, bottom = features[:, 0], features[:, height - 1]
    near, far = swap_edges(jnp.where(core == 0, bottom, top), jnp.where(core == 0, top, bottom))
    (decoded, d_pre, d_resid, near_out, far_out, keep, send, small) = main_call(
        place,
        owners,
        alive,
        2.0 * scale * alive,
        core.reshape(1),
        features,
        near,
        far,
        cotangent,
        parts,
        proj_master.astype(BF16),
        dec_master.astype(BF16),
        code_low,
        norms,
    )
    near, far = swap_edges(near_out, far_out)
    one, two = reduce_small(small)
    input_grad = input_call(place, core.reshape(1), features, d_resid, d_pre, near, far, parts)
    owned = reduce_tiles(keep, send, tiles)
    tile_out = tile_call(
        owned, tile_master, tile_mom1, tile_mom2, stat_left, stat_right, basis_left, basis_right
    )
    small_out = small_call(
        scale.reshape(1),
        one,
        two,
        [
            proj_master,
            proj_mom1,
            proj_mom2,
            dec_master,
            dec_mom1,
            dec_mom2,
            code_master,
            code_mom1,
            code_mom2,
        ],
    )
    return (decoded, input_grad, small_out[9].reshape(()), *tile_out, *small_out[:9])


def solution(mesh):
    big = P("img", "strip", None, None)
    tile = P("img", None, None)
    in_specs = (big, big, P(), P()) + (tile,) * 7 + (P(),) * 9
    out_specs = (big, big, P()) + (tile,) * 7 + (P(),) * 9
    return jax.shard_map(body, mesh=mesh, in_specs=in_specs, out_specs=out_specs, check_vma=False)
```

```python
import jax
import jax.numpy as jnp
from jax import lax
from jax.experimental import pallas as pl
from jax.experimental.pallas import tpu as pltpu
from jax.sharding import PartitionSpec as P

STEP = 5
BETA_ONE = 0.9
BETA_TWO = 0.95
EPSILON = 1e-08
WEIGHT_DECAY = 0.01
SOFTMAX_WARMTH = 4.0
LOSS_WEIGHT = 1.25
TILE_RATE = 0.05
PROJ_RATE = 0.05
DEC_RATE = 0.1
CODE_RATE = 0.3

F32 = jnp.float32
BF16 = jnp.bfloat16
NN = ((1,), (0,))
NT = ((1,), (1,))
TN = ((0,), (0,))
GELU_A = 0.7978845608028654
GELU_B = 0.044715
VMEM_LIMIT = 56 * 1024 * 1024


def dot(a, b, dims=NN):
    return lax.dot_general(a, b, (dims, ((), ())), preferred_element_type=F32)


def gelu_tanh(x):
    return jnp.tanh(GELU_A * (x + GELU_B * (x * x * x)))


def gelu(x):
    return 0.5 * x * (1.0 + gelu_tanh(x))


def gelu_both(x):
    square = x * x
    t = jnp.tanh(GELU_A * x * (1.0 + GELU_B * square))
    half = 0.5 * (1.0 + t)
    slope = half + 0.5 * x * (1.0 - t * t) * (GELU_A + 3.0 * GELU_A * GELU_B * square)
    return x * half, slope


def column_shifts(rows, wide):
    count = rows.shape[0]
    column = lax.broadcasted_iota(jnp.int32, rows.shape, 0) % wide
    before = jnp.where(column == 0, 0.0, pltpu.roll(rows, 1, 0))
    after = jnp.where(column == wide - 1, 0.0, pltpu.roll(rows, count - 1, 0))
    return before, after


def place_weights(place, parts, core, put):
    half = parts[0].shape[1]
    count = len(parts) // 2
    size = parts[0].shape[0]
    for t in range(40):
        which = place[t] // size
        index = place[t] % size
        for side in range(2):
            block = parts[side * count][index]
            for n in range(1, count):
                block = jnp.where(which == n, parts[side * count + n][index], block)
            put(t, block, pl.multiple_of((core ^ side) * half, half))


def shift_lines(line, first, last):
    wide = line.shape[0]
    before = jnp.where(first, 0.0, pltpu.roll(line, 1, 0)).astype(BF16)
    after = jnp.where(last, 0.0, pltpu.roll(line, wide - 1, 0)).astype(BF16)
    return before, after


def main_kernel(batch, part_count, *refs):
    place, slots, alive_all, pull_all, core = refs[:5]
    feat, near, far, cot = refs[5:9]
    parts = refs[9 : 9 + part_count]
    proj, dec, code, norms = refs[9 + part_count : 13 + part_count]
    (decoded, d_pre_out, d_resid_out, near_out, far_out, keep, send, small) = refs[
        13 + part_count : 21 + part_count
    ]
    (weights, mixer, framed, d_pre_turned, sums, g_mixer, g_proj, g_dec, g_code, totals, loss) = refs[
        21 + part_count :
    ]
    step = pl.program_id(0)
    steps = pl.num_programs(0)
    height, wide, channels = feat.shape[1:]
    count = height * wide
    tile = parts[0].shape[2]
    half = tile // 2
    images = framed.shape[0]
    lead = core[0] == 0

    @pl.when(step == 0)
    def _():
        def put(t, block, row):
            i, j = (t // 2) % 2, t % 2
            if t < 36:
                p = t // 4
                start = (p % 3) * channels + i * tile
                weights[p // 3, pl.ds(start + row, half), j * tile : (j + 1) * tile] = block
            else:
                mixer[pl.ds(i * tile + row, half), j * tile : (j + 1) * tile] = block

        place_weights(place, parts, core[0], put)
        for ref in (g_mixer, g_proj, g_dec, g_code, totals, loss):
            ref[...] = jnp.zeros_like(ref)

    column = lax.broadcasted_iota(jnp.int32, (wide, channels), 0)
    first = column == 0
    last = column == wide - 1

    def chain(n):
        image = step * batch + n
        alive = alive_all[image]
        pull = pull_all[image]
        for r in range(height + 2):
            if r == 0:
                line = jnp.where(lead, far[n].astype(F32), near[n].astype(F32))
            elif r == height + 1:
                line = jnp.where(lead, near[n].astype(F32), far[n].astype(F32))
            else:
                line = feat[n, r - 1].astype(F32)
            line = gelu(line)
            before, after = shift_lines(line, first, last)
            rows = slice(r * wide, (r + 1) * wide)
            framed[image, rows, 0:channels] = before
            framed[image, rows, channels : 2 * channels] = line.astype(BF16)
            framed[image, rows, 2 * channels :] = after
        yield
        preact = dot(framed[image, 0:count, :], weights[0])
        preact += dot(framed[image, wide : wide + count, :], weights[1])
        preact += dot(framed[image, 2 * wide : 2 * wide + count, :], weights[2])
        yield
        inner, slope = gelu_both(preact)
        inner = inner.astype(BF16)
        yield
        feats = feat[n].reshape(count, channels).astype(F32)
        resid = (feats + dot(inner, mixer[...])).astype(BF16)
        yield
        latent = dot(resid, proj[...], NT)
        latent_low = latent.astype(BF16)
        yield
        logits = (2.0 / SOFTMAX_WARMTH) * dot(latent_low, code[...]) - norms[...]
        yield
        powers = jnp.exp(logits - jnp.max(logits, axis=1, keepdims=True))
        probs = powers * (1.0 / jnp.sum(powers, axis=1, keepdims=True))
        probs_low = probs.astype(BF16)
        yield
        quant = dot(probs_low, code[...], NT)
        quant_low = quant.astype(BF16)
        yield
        out = (dot(quant_low, dec[...]) * alive).astype(BF16)
        decoded[n] = out.reshape(height, wide, channels)
        diff = latent - quant
        loss[...] += alive * jnp.sum(diff * diff, axis=0, keepdims=True)
        back_out = (cot[n].reshape(count, channels).astype(F32) * alive).astype(BF16)
        pulled = pull * diff
        d_quant = (dot(back_out, dec[...], NT) - pulled).astype(BF16)
        g_dec[...] += dot(quant_low, back_out, TN)
        yield
        d_probs = dot(d_quant, code[...])
        yield
        d_logits = probs * (d_probs - jnp.sum(probs * d_probs, axis=1, keepdims=True))
        d_logits = d_logits.astype(BF16)
        totals[...] += jnp.sum(d_logits.astype(F32), axis=0, keepdims=True)
        yield
        d_latent = ((2.0 / SOFTMAX_WARMTH) * dot(d_logits, code[...], NT) + pulled).astype(BF16)
        yield
        d_resid = dot(d_latent, proj[...]).astype(BF16)
        d_resid_out[n] = d_resid.reshape(height, wide, channels)
        g_code[...] += dot(d_quant, probs_low, TN)
        g_code[...] += (2.0 / SOFTMAX_WARMTH) * dot(latent_low, d_logits, TN)
        yield
        d_pre = (slope * dot(d_resid, mixer[...], NT)).astype(BF16)
        g_proj[...] += dot(d_latent, resid, TN)
        yield
        d_pre_out[n] = d_pre.reshape(height, wide, channels)
        top, bottom = d_pre[:wide], d_pre[count - wide :]
        near_out[n] = jnp.where(lead, bottom, top)
        far_out[n] = jnp.where(lead, top, bottom)
        g_mixer[...] += dot(d_resid, inner, TN)
        yield
        d_pre_turned[image] = d_pre.T

    live = [chain(n) for n in range(batch)]
    while live:
        live = [c for c in live if next(c, True) is None]

    @pl.when(step == steps - 1)
    def _():
        for line in range(3):
            total = None
            for n in range(images):
                term = dot(d_pre_turned[n], framed[n, line * wide : line * wide + count, :])
                total = term if total is None else total + term
            sums[line] = total
        for ref in (keep, send):
            ref[...] = jnp.zeros_like(ref)
        quarter = tile // 4
        for t in range(40):
            i, j = (t // 2) % 2, t % 2
            if t < 36:
                p = t // 4
                left = (p % 3) * channels + i * tile
                block = sums[p // 3, j * tile : (j + 1) * tile, left : left + tile]
            else:
                block = g_mixer[j * tile : (j + 1) * tile, i * tile : (i + 1) * tile]
            block = block.astype(BF16)
            for q in range(0, 4, 2):
                even = block[q * quarter : (q + 1) * quarter]
                odd = block[(q + 1) * quarter : (q + 2) * quarter]
                keep[q // 2, slots[t]] = jnp.where(lead, even, odd)
                send[q // 2, slots[t]] = jnp.where(lead, odd, even)
        g_words = g_code[...] - (2.0 / SOFTMAX_WARMTH) * totals[...] * code[...].astype(F32)
        row = 0
        for grad in (g_proj[...], g_dec[...], g_words):
            for left in range(0, grad.shape[1], 128):
                small[row : row + grad.shape[0]] = grad[:, left : left + 128].astype(BF16)
                row += grad.shape[0]
        small[row:] = jnp.zeros((small.shape[0] - row, 128), BF16)
        small[row : row + 16, 0 : loss.shape[1]] = jnp.broadcast_to(
            loss[...] * (1.0 / 16.0), (16, loss.shape[1])
        ).astype(BF16)


def main_call(place, slots, alive, pull, core, feat, near, far, cot, parts, proj, dec, code, norms):
    images, height, wide, channels = feat.shape
    latent, words = code.shape
    size, half, tile = parts[0].shape
    slot_count = size * len(parts) // 2
    batch = 5 if images % 5 == 0 else 1
    smem = pl.BlockSpec(memory_space=pltpu.SMEM)
    strip = pl.BlockSpec((batch, height, wide, channels), lambda i: (i, 0, 0, 0))
    line = pl.BlockSpec((batch, wide, channels), lambda i: (i, 0, 0))

    def whole(shape):
        return pl.BlockSpec(shape, lambda i: (0,) * len(shape))

    big = jax.ShapeDtypeStruct(feat.shape, BF16)
    edge = jax.ShapeDtypeStruct(near.shape, BF16)
    part = jax.ShapeDtypeStruct((2, slot_count, tile // 4, tile), BF16)
    rows = (2 * latent * channels + latent * words) // 128 + 16
    shapes = (big, big, big, edge, edge, part, part, jax.ShapeDtypeStruct((rows, 128), BF16))
    return pl.pallas_call(
        lambda *refs: main_kernel(batch, len(parts), *refs),
        grid=(images // batch,),
        in_specs=[smem] * 5
        + [strip, line, line, strip]
        + [whole(a.shape) for a in (*parts, proj, dec, code, norms)],
        out_specs=[strip] * 3 + [line] * 2 + [whole(s.shape) for s in shapes[5:]],
        out_shape=shapes,
        scratch_shapes=[
            pltpu.VMEM((3, 3 * channels, channels), BF16),
            pltpu.VMEM((channels, channels), BF16),
            pltpu.VMEM((images, (height + 2) * wide, 3 * channels), BF16),
            pltpu.VMEM((images, channels, height * wide), BF16),
            pltpu.VMEM((3, channels, 3 * channels), F32),
            pltpu.VMEM((channels, channels), F32),
            pltpu.VMEM((latent, channels), F32),
            pltpu.VMEM((latent, channels), F32),
            pltpu.VMEM((latent, words), F32),
            pltpu.VMEM((1, words), F32),
            pltpu.VMEM((1, latent), F32),
        ],
        compiler_params=pltpu.CompilerParams(vmem_limit_bytes=VMEM_LIMIT),
        name="main",
    )(place, slots, alive, pull, core, feat, near, far, cot, *parts, proj, dec, code, norms)


def input_kernel(batch, part_count, *refs):
    place, core, feat, d_resid, d_pre, near, far = refs[:7]
    parts = refs[7 : 7 + part_count]
    out, weights = refs[7 + part_count :]
    height, wide, channels = feat.shape[1:]
    count = height * wide
    tile = parts[0].shape[2]
    half = tile // 2
    lead = core[0] == 0

    @pl.when(pl.program_id(0) == 0)
    def _():
        def put(t, block, row):
            if t < 36:
                i, j = (t // 2) % 2, t % 2
                p = t // 4
                start = (2 - p % 3) * channels + i * tile
                weights[2 - p // 3, pl.ds(start + row, half), j * tile : (j + 1) * tile] = block

        place_weights(place, parts, core[0], put)

    column = lax.broadcasted_iota(jnp.int32, (wide, channels), 0)
    first = column == 0
    last = column == wide - 1
    for n in range(batch):
        lines = []
        for r in range(height + 2):
            if r == 0:
                line = jnp.where(lead, far[n], near[n])
            elif r == height + 1:
                line = jnp.where(lead, near[n], far[n])
            else:
                line = d_pre[n, r - 1]
            before, after = shift_lines(line.astype(F32), first, last)
            lines.append((before, line, after))
        sides = [jnp.concatenate([l[s] for l in lines], axis=0) for s in range(3)]
        d_act = None
        for line in range(3):
            for side in range(3):
                window = sides[side][line * wide : line * wide + count]
                term = dot(window, weights[line, side * channels : (side + 1) * channels, :], NT)
                d_act = term if d_act is None else d_act + term
        _, slope = gelu_both(feat[n].reshape(count, channels).astype(F32))
        total = d_resid[n].reshape(count, channels).astype(F32) + slope * d_act
        out[n] = total.astype(BF16).reshape(height, wide, channels)


def input_call(place, core, feat, d_resid, d_pre, near, far, parts):
    images, height, wide, channels = feat.shape
    batch = 5 if images % 5 == 0 else 1
    smem = pl.BlockSpec(memory_space=pltpu.SMEM)
    strip = pl.BlockSpec((batch, height, wide, channels), lambda i: (i, 0, 0, 0))
    line = pl.BlockSpec((batch, wide, channels), lambda i: (i, 0, 0))
    return pl.pallas_call(
        lambda *refs: input_kernel(batch, len(parts), *refs),
        grid=(images // batch,),
        in_specs=[smem, smem, strip, strip, strip, line, line]
        + [pl.BlockSpec(p.shape, lambda i: (0, 0, 0)) for p in parts],
        out_specs=strip,
        out_shape=jax.ShapeDtypeStruct(feat.shape, BF16),
        scratch_shapes=[pltpu.VMEM((3, 3 * channels, channels), BF16)],
        compiler_params=pltpu.CompilerParams(vmem_limit_bytes=VMEM_LIMIT),
        name="input_grad",
    )(place, core, feat, d_resid, d_pre, near, far, *parts)


BLOCK = 32
RANK = 4


def split3(x):
    high = x.astype(BF16)
    rest = x - high.astype(F32)
    middle = rest.astype(BF16)
    return high, middle, (rest - middle.astype(F32)).astype(BF16)


def dot_exact(a, b, dims=NN):
    left = jnp.concatenate([a[n] for n in (0, 0, 1, 1, 0, 2)], axis=dims[0][0])
    right = jnp.concatenate([b[n] for n in (0, 1, 0, 1, 2, 0)], axis=dims[1][0])
    return dot(left, right, dims)


def inverse_factors(pairs):
    half = 64
    lane = lax.broadcasted_iota(jnp.int32, (8, 128), 1)
    sub = lax.broadcasted_iota(jnp.int32, (8, 128), 0)
    base = jnp.where(lane >= half, half, 0)
    inner = lane - base
    count = BLOCK // 8

    def pick(x, k):
        return jnp.take_along_axis(x, base + k, axis=1)

    mats = []
    for one, two in pairs:
        zero = jnp.zeros((BLOCK, half - BLOCK), F32)
        wide = jnp.concatenate([one, zero, two, zero], axis=1)
        mats.append(
            [
                wide[8 * v : 8 * v + 8] + jnp.where(inner == sub + (8 * v + BLOCK), 1.0, 0.0)
                for v in range(count)
            ]
        )
    for start in range(0, BLOCK, RANK):
        v0, s0 = start // 8, start % 8
        for rows in mats:
            pivots = [jnp.broadcast_to(rows[v0][s0 + i : s0 + i + 1], (8, 128)) for i in range(RANK)]
            columns = [pick(rows[v0], start + j) for j in range(RANK)]
            core = {
                (i, j): jnp.broadcast_to(columns[j][s0 + i : s0 + i + 1], (8, 128))
                for i in range(RANK)
                for j in range(i, RANK)
            }
            lower = {}
            scaled = []
            for i in range(RANK):
                root = lax.rsqrt(core[i, i])
                for j in range(i + 1, RANK):
                    lower[j, i] = core[i, j] * (root * root)
                for j in range(i + 1, RANK):
                    for k in range(j, RANK):
                        core[j, k] = core[j, k] - lower[j, i] * core[i, k]
                    pivots[j] = pivots[j] - lower[j, i] * pivots[i]
                scaled.append((root, pivots[i] * root))
            if start + RANK < BLOCK:
                solved = [None] * RANK
                for i in range(RANK - 1, -1, -1):
                    solved[i] = scaled[i][1] * scaled[i][0]
                    for j in range(i + 1, RANK):
                        solved[i] = solved[i] - lower[j, i] * solved[j]
            for v in range(v0, count):
                new = rows[v]
                if v > v0 or s0 + RANK < 8:
                    for j in range(RANK):
                        column = columns[j] if v == v0 else pick(rows[v], start + j)
                        new = new - column * solved[j]
                if v == v0:
                    if s0 > 0:
                        new = jnp.where(sub < s0, rows[v], new)
                    for i in range(RANK):
                        new = jnp.where(sub == s0 + i, scaled[i][1], new)
                rows[v] = new
    return [jnp.concatenate(rows, axis=0) for rows in mats]


def small_update(scale, one, two, arrays, outs):
    total = one[...].astype(F32) + two[...].astype(F32)
    row = 0
    for n, rate in enumerate((PROJ_RATE, DEC_RATE, CODE_RATE)):
        rows, columns = arrays[3 * n].shape
        pieces = []
        for _ in range(columns // 128):
            pieces.append(total[row : row + rows])
            row += rows
        grad = jnp.concatenate(pieces, axis=1)
        new = plain_adam(grad, *(a[...] for a in arrays[3 * n : 3 * n + 3]), rate)
        for out, value in zip(outs[3 * n : 3 * n + 3], new):
            out[...] = value
    outs[9][...] = jnp.sum(total[row:], axis=(0, 1), keepdims=True) * scale[0]


def tile_kernel(*refs):
    strip, scale = refs[:2]
    quarters = refs[2:6]
    master, first, second, left, right, basis_left, basis_right = refs[6:13]
    one, two = refs[13:15]
    small_arrays = refs[15:24]
    (master_new, first_new, second_new, left_new, right_new, basis_left_new, basis_right_new) = refs[
        24:31
    ]
    small_outs = refs[31:41]
    work, grad_turned = refs[41:]
    count, tile = master.shape[:2]
    for d in range(4):
        quarter = tile // 4
        row = pl.multiple_of((strip[0] ^ d) * quarter, quarter)
        grad_turned[:, pl.ds(row, quarter), :] = quarters[d][...]
    for t in range(count):
        grad = grad_turned[t]
        left_new[t] = BETA_TWO * left[t] + (1.0 - BETA_TWO) * dot(grad, grad, TN)
        right_new[t] = BETA_TWO * right[t] + (1.0 - BETA_TWO) * dot(grad, grad, NT)
        for side, (stat, basis) in enumerate(((left_new, basis_left), (right_new, basis_right))):
            moved = dot_exact(split3(stat[t]), split3(basis[t]))
            turned = moved.T
            work[2 * t + side, :, :tile] = dot_exact(split3(turned), split3(moved))
            work[2 * t + side, :, tile:] = turned
    for t in range(count):
        one_low = basis_left[t].astype(BF16)
        two_low = basis_right[t].astype(BF16)
        turned = dot(one_low, grad_turned[t], ((0,), (1,)))
        turned = dot(turned.astype(BF16), two_low)
        mom = BETA_ONE * first[t] + (1.0 - BETA_ONE) * turned
        var = BETA_TWO * second[t] + (1.0 - BETA_TWO) * turned * turned
        first_new[t] = mom
        second_new[t] = var
        ratio = mom / (1.0 - BETA_ONE**STEP) / (jnp.sqrt(var / (1.0 - BETA_TWO**STEP)) + EPSILON)
        back = dot(dot(one_low, ratio.astype(BF16)).astype(BF16), two_low, NT)
        master_new[t] = master[t] - TILE_RATE * (back + WEIGHT_DECAY * master[t])
    small_update(scale, one, two, small_arrays, small_outs)
    for low in range(0, tile, BLOCK):
        high = low + BLOCK
        factors = inverse_factors(
            [
                (work[2 * t, low:high, low:high], work[2 * t + 1, low:high, low:high])
                for t in range(count)
            ]
        )
        for n in range(2 * count):
            start = (n % 2) * 64 + BLOCK
            factor = split3(factors[n // 2][:, start : start + BLOCK])
            panel = dot_exact(factor, split3(work[n, low:high, :]))
            work[n, low:high, tile:] = panel[:, tile:]
            if high < tile:
                panel = split3(panel)
                work[n, high:, :] = work[n, high:, :] - dot_exact(
                    [p[:, high:tile] for p in panel], panel, TN
                )
    for t in range(count):
        basis_left_new[t] = work[2 * t, :, tile:].T
        basis_right_new[t] = work[2 * t + 1, :, tile:].T


def tile_call(strip, scale, quarters, arrays, one, two, small_arrays):
    shape = jax.ShapeDtypeStruct(arrays[0].shape, F32)
    smem = pl.BlockSpec(memory_space=pltpu.SMEM)
    vmem = pl.BlockSpec(memory_space=pltpu.VMEM)
    count, tile = shape.shape[:2]
    shapes = [shape] * 7 + [jax.ShapeDtypeStruct(a.shape, F32) for a in small_arrays]
    shapes.append(jax.ShapeDtypeStruct((1, 1), F32))
    return pl.pallas_call(
        tile_kernel,
        in_specs=[smem] * 2 + [vmem] * 22,
        out_specs=[vmem] * 17,
        out_shape=shapes,
        scratch_shapes=[
            pltpu.VMEM((2 * count, tile, 2 * tile), F32),
            pltpu.VMEM((count, tile, tile), BF16),
        ],
        compiler_params=pltpu.CompilerParams(vmem_limit_bytes=VMEM_LIMIT),
        name="tile_adam",
    )(strip, scale, *quarters, *arrays, one, two, *small_arrays)


def plain_adam(gradient, master, first, second, rate):
    first_new = BETA_ONE * first + (1.0 - BETA_ONE) * gradient
    second_new = BETA_TWO * second + (1.0 - BETA_TWO) * gradient * gradient
    ratio = (
        first_new
        / (1.0 - BETA_ONE**STEP)
        / (jnp.sqrt(second_new / (1.0 - BETA_TWO**STEP)) + EPSILON)
    )
    return (master - rate * (ratio + WEIGHT_DECAY * master), first_new, second_new)


def swap(x, axis, distance):
    count = lax.axis_size(axis)
    return lax.ppermute(x, axis, [(i, i ^ distance) for i in range(count)])


def radices(count):
    out = []
    stride = 1
    while stride < count:
        left = (count // stride).bit_length() - 1
        radix = 2 if left % 2 else 4
        out.append((radix, stride))
        stride *= radix
    return out


def swap_edges(near, far):
    return swap(near, "strip", 1), lax.ppermute(far, "strip", [(1, 2), (2, 1)])


def gather_tiles(mine):
    core = lax.axis_index("strip") % 2
    half = mine.shape[1] // 2
    part = lax.dynamic_slice_in_dim(mine, core * half, half, axis=1)
    steps = radices(lax.axis_size("img"))[::-1]
    for number, (radix, stride) in enumerate(steps):
        parts = [part] + [swap(part, "img", d * stride) for d in range(1, radix)]
        if number < len(steps) - 1:
            part = jnp.concatenate(parts, axis=0)
    return parts + [swap(p, "strip", 1) for p in parts]


def tile_place(owners, tiles):
    distance = (owners // tiles) ^ lax.axis_index("img")
    place = jnp.zeros_like(owners)
    size = 1
    for radix, stride in radices(lax.axis_size("img"))[::-1]:
        place = place + size * ((distance // stride) % radix)
        size *= radix
    return place * tiles + owners % tiles


def reduce_tiles(keep, send, tiles):
    strip = lax.axis_index("strip")
    across = strip // 2
    img = lax.axis_index("img")
    groups = lax.axis_size("img")
    (radix, _), *later = radices(groups)
    part = keep + swap(send, "strip", 1)
    part = part.reshape(2, groups // radix, radix, -1, part.shape[-1])
    low = img % radix
    total = None
    for d in range(2):
        for e in range(radix):
            piece = lax.dynamic_index_in_dim(part, across ^ d, 0, False)
            piece = lax.dynamic_index_in_dim(piece, low ^ e, 1, False)
            if d or e:
                pairs = [
                    (a * groups + b, (a ^ (2 * d)) * groups + (b ^ e))
                    for a in range(4)
                    for b in range(groups)
                ]
                piece = lax.ppermute(piece, ("strip", "img"), pairs)
            piece = piece.astype(F32)
            total = piece if total is None else total + piece
    left = groups // radix
    for radix, stride in later:
        part = total.astype(BF16).reshape(left // radix, radix, *total.shape[-2:])
        low = (img // stride) % radix
        total = lax.dynamic_index_in_dim(part, low, 1, False).astype(F32)
        for d in range(1, radix):
            piece = lax.dynamic_index_in_dim(part, low ^ d, 1, False)
            total = total + swap(piece, "img", d * stride).astype(F32)
        left //= radix
    total = total.astype(BF16).reshape(tiles, -1, total.shape[-1])
    return [total] + [swap(total, "strip", d) for d in range(1, 4)]


def reduce_small(small):
    steps = [("strip", 1), ("strip", 2)]
    for radix, stride in radices(lax.axis_size("img")):
        steps += [("img", stride << n) for n in range(radix.bit_length() - 1)]
    for number, (axis, distance) in enumerate(steps):
        other = swap(small, axis, distance)
        if number == len(steps) - 1:
            return small, other
        small = (small.astype(F32) + other.astype(F32)).astype(BF16)


def body(
    features,
    cotangent,
    present,
    owners,
    tile_master,
    tile_mom1,
    tile_mom2,
    stat_left,
    stat_right,
    basis_left,
    basis_right,
    proj_master,
    proj_mom1,
    proj_mom2,
    dec_master,
    dec_mom1,
    dec_mom2,
    code_master,
    code_mom1,
    code_mom2,
):
    images, height, wide, channels = features.shape
    tiles = tile_master.shape[0]
    img = lax.axis_index("img")
    strip = lax.axis_index("strip")
    core = strip % 2
    parts = gather_tiles(tile_master.astype(BF16))
    place = tile_place(owners, tiles)
    alive = lax.dynamic_slice_in_dim(present, img * images, images).astype(F32)
    count = jnp.sum(present).astype(F32) * (height * lax.axis_size("strip") * wide)
    latent = proj_master.shape[1]
    scale = LOSS_WEIGHT / (count * latent)
    code_low = code_master.T.astype(BF16)
    code_full = code_low.astype(F32)
    norms = jnp.sum(code_full * code_full, axis=0)[None] / SOFTMAX_WARMTH
    top, bottom = features[:, 0], features[:, height - 1]
    near, far = swap_edges(jnp.where(core == 0, bottom, top), jnp.where(core == 0, top, bottom))
    (decoded, d_pre, d_resid, near_out, far_out, keep, send, small) = main_call(
        place,
        owners,
        alive,
        2.0 * scale * alive,
        core.reshape(1),
        features,
        near,
        far,
        cotangent,
        parts,
        proj_master.T.astype(BF16),
        dec_master.astype(BF16),
        code_low,
        norms,
    )
    near, far = swap_edges(near_out, far_out)
    one, two = reduce_small(small)
    input_grad = input_call(place, core.reshape(1), features, d_resid, d_pre, near, far, parts)
    quarters = reduce_tiles(keep, send, tiles)
    out = tile_call(
        strip.reshape(1),
        scale.reshape(1),
        quarters,
        [tile_master, tile_mom1, tile_mom2, stat_left, stat_right, basis_left, basis_right],
        one,
        two,
        [
            proj_master.T,
            proj_mom1.T,
            proj_mom2.T,
            dec_master,
            dec_mom1,
            dec_mom2,
            code_master.T,
            code_mom1.T,
            code_mom2.T,
        ],
    )
    small = [a.T for a in out[7:10]] + list(out[10:13]) + [a.T for a in out[13:16]]
    return (decoded, input_grad, out[16].reshape(()), *out[:7], *small)


def solution(mesh):
    big = P("img", "strip", None, None)
    tile = P("img", None, None)
    in_specs = (big, big, P(), P()) + (tile,) * 7 + (P(),) * 9
    out_specs = (big, big, P()) + (tile,) * 7 + (P(),) * 9
    return jax.shard_map(body, mesh=mesh, in_specs=in_specs, out_specs=out_specs, check_vma=False)
```

```python
import jax
import jax.numpy as jnp
from jax import lax
from jax.experimental import pallas as pl
from jax.experimental.pallas import tpu as pltpu
from jax.sharding import PartitionSpec as P

STEP = 5
BETA_ONE = 0.9
BETA_TWO = 0.95
EPSILON = 1e-08
WEIGHT_DECAY = 0.01
SOFTMAX_WARMTH = 4.0
LOSS_WEIGHT = 1.25
TILE_RATE = 0.05
PROJ_RATE = 0.05
DEC_RATE = 0.1
CODE_RATE = 0.3

F32 = jnp.float32
BF16 = jnp.bfloat16
NN = ((1,), (0,))
NT = ((1,), (1,))
TN = ((0,), (0,))
GELU_A = 0.7978845608028654
GELU_B = 0.044715
LOSS_ROWS = 16
MAIN_VMEM = 56 * 1024 * 1024
FINISH_VMEM = 56 * 1024 * 1024


def dot(a, b, dims=NN):
    return lax.dot_general(a, b, (dims, ((), ())), preferred_element_type=F32)


def gelu_tanh(x):
    return jnp.tanh(GELU_A * (x + GELU_B * (x * x * x)))


def gelu(x):
    return 0.5 * x * (1.0 + gelu_tanh(x))


def gelu_both(x):
    square = x * x
    t = jnp.tanh(GELU_A * x * (1.0 + GELU_B * square))
    half = 0.5 * (1.0 + t)
    slope = half + 0.5 * x * (1.0 - t * t) * (GELU_A + 3.0 * GELU_A * GELU_B * square)
    return x * half, slope


def column_shifts(rows, wide):
    count = rows.shape[0]
    column = lax.broadcasted_iota(jnp.int32, rows.shape, 0) % wide
    before = jnp.where(column == 0, 0.0, pltpu.roll(rows, 1, 0))
    after = jnp.where(column == wide - 1, 0.0, pltpu.roll(rows, count - 1, 0))
    return before, after


def place_weights(places, ids, parts, put):
    half = parts[0].shape[1]
    count = len(parts) // 2
    size = parts[0].shape[0]
    for t in range(40):
        which = lax.div(places[t], size)
        index = lax.rem(places[t], size)
        for side in range(2):
            block = parts[side * count][index]
            for n in range(1, count):
                block = jnp.where(which == n, parts[side * count + n][index], block)
            put(t, block, pl.multiple_of((lax.rem(ids[0], 2) ^ side) * half, half))


def loss_scale(present, positions, latent):
    count = jnp.sum(present[...].astype(F32)) * positions
    return LOSS_WEIGHT / (count * latent)


def shift_lines(line, first, last):
    wide = line.shape[0]
    before = jnp.where(first, 0.0, pltpu.roll(line, 1, 0)).astype(BF16)
    after = jnp.where(last, 0.0, pltpu.roll(line, wide - 1, 0)).astype(BF16)
    return before, after


def main_kernel(batch, part_count, *refs):
    ids, places, slots, present = refs[:4]
    present_row, feat, near, far, cot = refs[4:9]
    parts = refs[9 : 9 + part_count]
    proj_full, dec_full, code_full = refs[9 + part_count : 12 + part_count]
    (decoded, d_pre_out, d_resid_out, near_out, far_out, weights, keep, send) = refs[
        12 + part_count : 20 + part_count
    ]
    (mixer, framed, d_pre_turned, sums, g_mixer, g_proj, g_dec, g_code, totals, loss) = refs[
        20 + part_count : 30 + part_count
    ]
    proj, dec, code, norms, scale = refs[30 + part_count :]
    step = pl.program_id(0)
    steps = pl.num_programs(0)
    height, wide, channels = feat.shape[1:]
    count = height * wide
    tile = parts[0].shape[2]
    half = tile // 2
    images = framed.shape[0]
    lead = lax.rem(ids[0], 2) == 0

    @pl.when(step == 0)
    def _():
        def put(t, block, row):
            i, j = (t // 2) % 2, t % 2
            if t < 36:
                p = t // 4
                start = (p % 3) * channels + i * tile
                weights[p // 3, pl.ds(start + row, half), j * tile : (j + 1) * tile] = block
            else:
                mixer[pl.ds(i * tile + row, half), j * tile : (j + 1) * tile] = block

        place_weights(places, ids, parts, put)
        proj[...] = proj_full[...].astype(BF16)
        dec[...] = dec_full[...].astype(BF16)
        code[...] = code_full[...].astype(BF16)
        words = code[...].astype(F32)
        norms[...] = jnp.sum(words * words, axis=0, keepdims=True) * (1.0 / SOFTMAX_WARMTH)
        scale[0] = 2.0 * loss_scale(present_row, 4 * count, proj.shape[0])
        for ref in (g_mixer, g_proj, g_dec, g_code, totals, loss):
            ref[...] = jnp.zeros_like(ref)

    column = lax.broadcasted_iota(jnp.int32, (wide, channels), 0)
    first = column == 0
    last = column == wide - 1

    def chain(n):
        image = step * batch + n
        alive = present[ids[1] * images + image].astype(F32)
        pull = alive * scale[0]
        for r in range(height + 2):
            if r == 0:
                line = jnp.where(lead, far[n].astype(F32), near[n].astype(F32))
            elif r == height + 1:
                line = jnp.where(lead, near[n].astype(F32), far[n].astype(F32))
            else:
                line = feat[n, r - 1].astype(F32)
            line = gelu(line)
            before, after = shift_lines(line, first, last)
            rows = slice(r * wide, (r + 1) * wide)
            framed[image, rows, 0:channels] = before
            framed[image, rows, channels : 2 * channels] = line.astype(BF16)
            framed[image, rows, 2 * channels :] = after
        yield
        preact = dot(framed[image, 0:count, :], weights[0])
        preact += dot(framed[image, wide : wide + count, :], weights[1])
        preact += dot(framed[image, 2 * wide : 2 * wide + count, :], weights[2])
        yield
        inner, slope = gelu_both(preact)
        inner = inner.astype(BF16)
        yield
        feats = feat[n].reshape(count, channels).astype(F32)
        resid = (feats + dot(inner, mixer[...])).astype(BF16)
        yield
        latent = dot(resid, proj[...], NT)
        latent_low = latent.astype(BF16)
        yield
        logits = (2.0 / SOFTMAX_WARMTH) * dot(latent_low, code[...]) - norms[...]
        yield
        powers = jnp.exp(logits - jnp.max(logits, axis=1, keepdims=True))
        probs = powers * (1.0 / jnp.sum(powers, axis=1, keepdims=True))
        probs_low = probs.astype(BF16)
        yield
        quant = dot(probs_low, code[...], NT)
        quant_low = quant.astype(BF16)
        yield
        out = (dot(quant_low, dec[...]) * alive).astype(BF16)
        decoded[n] = out.reshape(height, wide, channels)
        diff = latent - quant
        loss[...] += alive * jnp.sum(diff * diff, axis=0, keepdims=True)
        back_out = (cot[n].reshape(count, channels).astype(F32) * alive).astype(BF16)
        pulled = pull * diff
        d_quant = (dot(back_out, dec[...], NT) - pulled).astype(BF16)
        g_dec[...] += dot(quant_low, back_out, TN)
        yield
        d_probs = dot(d_quant, code[...])
        yield
        d_logits = probs * (d_probs - jnp.sum(probs * d_probs, axis=1, keepdims=True))
        d_logits = d_logits.astype(BF16)
        totals[...] += jnp.sum(d_logits.astype(F32), axis=0, keepdims=True)
        yield
        d_latent = ((2.0 / SOFTMAX_WARMTH) * dot(d_logits, code[...], NT) + pulled).astype(BF16)
        yield
        d_resid = dot(d_latent, proj[...]).astype(BF16)
        d_resid_out[n] = d_resid.reshape(height, wide, channels)
        g_code[...] += dot(d_quant, probs_low, TN)
        g_code[...] += (2.0 / SOFTMAX_WARMTH) * dot(latent_low, d_logits, TN)
        yield
        d_pre = (slope * dot(d_resid, mixer[...], NT)).astype(BF16)
        g_proj[...] += dot(d_latent, resid, TN)
        yield
        d_pre_out[n] = d_pre.reshape(height, wide, channels)
        top, bottom = d_pre[:wide], d_pre[count - wide :]
        near_out[n] = jnp.where(lead, bottom, top)
        far_out[n] = jnp.where(lead, top, bottom)
        g_mixer[...] += dot(d_resid, inner, TN)
        yield
        d_pre_turned[image] = d_pre.T

    live = [chain(n) for n in range(batch)]
    while live:
        live = [c for c in live if next(c, True) is None]

    @pl.when(step == steps - 1)
    def _():
        for line in range(3):
            total = None
            for n in range(images):
                term = dot(d_pre_turned[n], framed[n, line * wide : line * wide + count, :])
                total = term if total is None else total + term
            sums[line] = total
        for ref in (keep, send):
            ref[...] = jnp.zeros_like(ref)
        quarter = tile // 4
        for t in range(40):
            i, j = (t // 2) % 2, t % 2
            if t < 36:
                p = t // 4
                left = (p % 3) * channels + i * tile
                block = sums[p // 3, j * tile : (j + 1) * tile, left : left + tile]
            else:
                block = g_mixer[j * tile : (j + 1) * tile, i * tile : (i + 1) * tile]
            block = block.astype(BF16)
            for q in range(0, 4, 2):
                even = block[q * quarter : (q + 1) * quarter]
                odd = block[(q + 1) * quarter : (q + 2) * quarter]
                row = pl.ds(pl.multiple_of(slots[t] * quarter, quarter), quarter)
                keep[q // 2, row] = jnp.where(lead, even, odd)
                send[q // 2, row] = jnp.where(lead, odd, even)
        g_words = g_code[...] - (2.0 / SOFTMAX_WARMTH) * totals[...] * code[...].astype(F32)
        blocks = []
        for grad in (g_proj[...], g_dec[...], g_words):
            for left in range(0, grad.shape[1], 128):
                blocks.append(grad[:, left : left + 128].astype(BF16))
        size = blocks[0].shape[0]
        each = len(blocks) // 4
        start = keep.shape[1] - each * size - LOSS_ROWS
        for x in range(2):
            for n in range(each):
                even, odd = blocks[2 * x * each + n], blocks[(2 * x + 1) * each + n]
                row = slice(start + n * size, start + (n + 1) * size)
                keep[x, row] = jnp.where(lead, even, odd)
                send[x, row] = jnp.where(lead, odd, even)
        row = start + each * size
        value = jnp.broadcast_to(loss[...] * (1.0 / LOSS_ROWS), (LOSS_ROWS, loss.shape[1]))
        keep[0, row:, 0 : loss.shape[1]] = jnp.where(lead, value, 0.0).astype(BF16)
        send[0, row:, 0 : loss.shape[1]] = jnp.where(lead, 0.0, value).astype(BF16)


def main_call(ids, places, slots, present, feat, near, far, cot, parts, proj, dec, code):
    images, height, wide, channels = feat.shape
    latent, words = code.shape
    size, half, tile = parts[0].shape
    slot_count = size * len(parts) // 2
    batch = 5 if images % 5 == 0 else 1
    smem = pl.BlockSpec(memory_space=pltpu.SMEM)
    strip = pl.BlockSpec((batch, height, wide, channels), lambda i: (i, 0, 0, 0))
    line = pl.BlockSpec((batch, wide, channels), lambda i: (i, 0, 0))

    def whole(shape):
        return pl.BlockSpec(shape, lambda i: (0,) * len(shape))

    big = jax.ShapeDtypeStruct(feat.shape, BF16)
    edge = jax.ShapeDtypeStruct(near.shape, BF16)
    rows = (2 * latent * channels + latent * words) // (4 * 128) + LOSS_ROWS
    part = jax.ShapeDtypeStruct((2, slot_count * tile // 4 + rows, tile), BF16)
    weights = jax.ShapeDtypeStruct((3, 3 * channels, channels), BF16)
    shapes = (big, big, big, edge, edge, weights, part, part)
    return pl.pallas_call(
        lambda *refs: main_kernel(batch, len(parts), *refs),
        grid=(images // batch,),
        in_specs=[smem] * 4
        + [whole((1, present.shape[0])), strip, line, line, strip]
        + [whole(a.shape) for a in (*parts, proj, dec, code)],
        out_specs=[strip] * 3 + [line] * 2 + [whole(s.shape) for s in shapes[5:]],
        out_shape=shapes,
        scratch_shapes=[
            pltpu.VMEM((channels, channels), BF16),
            pltpu.VMEM((images, (height + 2) * wide, 3 * channels), BF16),
            pltpu.VMEM((images, channels, height * wide), BF16),
            pltpu.VMEM((3, channels, 3 * channels), F32),
            pltpu.VMEM((channels, channels), F32),
            pltpu.VMEM((latent, channels), F32),
            pltpu.VMEM((latent, channels), F32),
            pltpu.VMEM((latent, words), F32),
            pltpu.VMEM((1, words), F32),
            pltpu.VMEM((1, latent), F32),
            pltpu.VMEM(proj.shape, BF16),
            pltpu.VMEM(dec.shape, BF16),
            pltpu.VMEM(code.shape, BF16),
            pltpu.VMEM((1, words), F32),
            pltpu.SMEM((1,), F32),
        ],
        compiler_params=pltpu.CompilerParams(vmem_limit_bytes=MAIN_VMEM),
        name="main",
    )(ids, places, slots, present, present[None], feat, near, far, cot, *parts, proj, dec, code)


BLOCK = 32
RANK = 4


def split3(x):
    high = x.astype(BF16)
    rest = x - high.astype(F32)
    middle = rest.astype(BF16)
    return high, middle, (rest - middle.astype(F32)).astype(BF16)


def dot_exact(a, b, dims=NN):
    left = jnp.concatenate([a[n] for n in (0, 0, 1, 1, 0, 2)], axis=dims[0][0])
    right = jnp.concatenate([b[n] for n in (0, 1, 0, 1, 2, 0)], axis=dims[1][0])
    return dot(left, right, dims)


def inverse_factors(pairs, beside):
    half = 64
    lane = lax.broadcasted_iota(jnp.int32, (8, 128), 1)
    sub = lax.broadcasted_iota(jnp.int32, (8, 128), 0)
    base = jnp.where(lane >= half, half, 0)
    inner = lane - base
    count = BLOCK // 8

    def pick(x, k):
        return jnp.take_along_axis(x, base + k, axis=1)

    mats = []
    for one, two in pairs:
        zero = jnp.zeros((BLOCK, half - BLOCK), F32)
        wide = jnp.concatenate([one, zero, two, zero], axis=1)
        mats.append(
            [
                wide[8 * v : 8 * v + 8] + jnp.where(inner == sub + (8 * v + BLOCK), 1.0, 0.0)
                for v in range(count)
            ]
        )
    for start in range(0, BLOCK, RANK):
        beside()
        v0, s0 = start // 8, start % 8
        for rows in mats:
            pivots = [jnp.broadcast_to(rows[v0][s0 + i : s0 + i + 1], (8, 128)) for i in range(RANK)]
            columns = [pick(rows[v0], start + j) for j in range(RANK)]
            core = {
                (i, j): jnp.broadcast_to(columns[j][s0 + i : s0 + i + 1], (8, 128))
                for i in range(RANK)
                for j in range(i, RANK)
            }
            lower = {}
            scaled = []
            for i in range(RANK):
                root = lax.rsqrt(core[i, i])
                for j in range(i + 1, RANK):
                    lower[j, i] = core[i, j] * (root * root)
                for j in range(i + 1, RANK):
                    for k in range(j, RANK):
                        core[j, k] = core[j, k] - lower[j, i] * core[i, k]
                    pivots[j] = pivots[j] - lower[j, i] * pivots[i]
                scaled.append((root, pivots[i] * root))
            if start + RANK < BLOCK:
                solved = [None] * RANK
                for i in range(RANK - 1, -1, -1):
                    solved[i] = scaled[i][1] * scaled[i][0]
                    for j in range(i + 1, RANK):
                        solved[i] = solved[i] - lower[j, i] * solved[j]
            for v in range(v0, count):
                new = rows[v]
                if v > v0 or s0 + RANK < 8:
                    for j in range(RANK):
                        column = columns[j] if v == v0 else pick(rows[v], start + j)
                        new = new - column * solved[j]
                if v == v0:
                    if s0 > 0:
                        new = jnp.where(sub < s0, rows[v], new)
                    for i in range(RANK):
                        new = jnp.where(sub == s0 + i, scaled[i][1], new)
                rows[v] = new
    return [jnp.concatenate(rows, axis=0) for rows in mats]


def small_update(present, shape, sums, arrays, outs):
    total = jnp.concatenate([sums[q, : sums.shape[1] - LOSS_ROWS] for q in range(4)], axis=0).astype(F32)
    row = 0
    for n, rate in enumerate((PROJ_RATE, DEC_RATE, CODE_RATE)):
        rows, columns = arrays[3 * n].shape
        pieces = []
        for _ in range(columns // 128):
            pieces.append(total[row : row + rows])
            row += rows
        grad = jnp.concatenate(pieces, axis=1)
        new = plain_adam(grad, *(a[...] for a in arrays[3 * n : 3 * n + 3]), rate)
        for out, value in zip(outs[3 * n : 3 * n + 3], new):
            out[...] = value
    loss = sums[0, sums.shape[1] - LOSS_ROWS :].astype(F32)
    scale = loss_scale(present, 4 * shape[1] * shape[2], arrays[0].shape[0])
    outs[9][...] = jnp.sum(loss, axis=(0, 1), keepdims=True) * scale


def input_units(weights, feat, d_resid, d_pre, near, far, lead, out, done):
    images, height, wide, channels = feat.shape
    column = lax.broadcasted_iota(jnp.int32, (wide, channels), 0)
    first = column == 0
    last = column == wide - 1
    count = height * wide
    for base in range(0, images, 2):
        group = range(base, base + 2)
        sides = []
        for n in group:
            lines = []
            for r in range(height + 2):
                if r == 0:
                    line = jnp.where(lead, far[n], near[n])
                elif r == height + 1:
                    line = jnp.where(lead, near[n], far[n])
                else:
                    line = d_pre[n, r - 1]
                before, after = shift_lines(line.astype(F32), first, last)
                lines.append((before, line, after))
            sides.append([jnp.concatenate([l[s] for l in lines], axis=0) for s in range(3)])
        acts = [None for n in group]
        for a in range(3):
            for k in range(len(acts)):
                window = jnp.concatenate([sides[k][b][a * wide : a * wide + count] for b in range(3)], axis=1)
                weight = jnp.concatenate([weights[2 - a, (2 - b) * channels : (3 - b) * channels, :] for b in range(3)], axis=1)
                term = dot(window, weight, NT)
                acts[k] = term if acts[k] is None else acts[k] + term
        for k, n in enumerate(group):
            _, slope = gelu_both(feat[n].reshape(count, channels).astype(F32))
            total = d_resid[n].reshape(count, channels).astype(F32) + slope * acts[k]
            out[n] = total.astype(BF16).reshape(height, wide, channels)
            done(n)
        yield


def adam_units(tiles, grad_turned, first_new, second_new, master_new, small):
    master, first, second, basis_left, basis_right = tiles
    for t in range(master.shape[0]):
        one_low = basis_left[t].astype(BF16)
        two_low = basis_right[t].astype(BF16)
        turned = dot(one_low, grad_turned[t], ((0,), (1,)))
        turned = dot(turned.astype(BF16), two_low)
        mom = BETA_ONE * first[t] + (1.0 - BETA_ONE) * turned
        var = BETA_TWO * second[t] + (1.0 - BETA_TWO) * turned * turned
        first_new[t] = mom
        second_new[t] = var
        ratio = mom / (1.0 - BETA_ONE**STEP) / (jnp.sqrt(var / (1.0 - BETA_TWO**STEP)) + EPSILON)
        back = dot(dot(one_low, ratio.astype(BF16)).astype(BF16), two_low, NT)
        master_new[t] = master[t] - TILE_RATE * (back + WEIGHT_DECAY * master[t])
        yield
    small()
    yield


CHUNKS = 4


def finish_kernel(*refs):
    ids, present = refs[:2]
    quarters = refs[2:6]
    master, first, second, left, right, basis_left, basis_right = refs[6:13]
    small_arrays = refs[13:22]
    loads = refs[22:28]
    (master_new, first_new, second_new, left_new, right_new, basis_left_new, basis_right_new) = refs[
        28:35
    ]
    small_outs = refs[35:45]
    input_grad = refs[45]
    work, grad_turned, small_sums = refs[46:49]
    held = refs[49:55]
    out, load_sems, store_sems = refs[55:]
    count, tile = master.shape[:2]
    images = out.shape[0]
    copies = [
        pltpu.make_async_copy(src, dst, load_sems.at[n]) for n, (src, dst) in enumerate(zip(loads, held))
    ]
    for copy in copies:
        copy.start()
    for d in range(4):
        quarter = tile // 4
        row = pl.multiple_of((ids[0] ^ d) * quarter, quarter)
        rows = count * quarter
        grad_turned[:, pl.ds(row, quarter), :] = quarters[d][:rows].reshape(count, quarter, tile)
        small_sums[ids[0] ^ d] = quarters[d][rows:]
    for t in range(count):
        grad = grad_turned[t]
        left_new[t] = BETA_TWO * left[t] + (1.0 - BETA_TWO) * dot(grad, grad, TN)
        right_new[t] = BETA_TWO * right[t] + (1.0 - BETA_TWO) * dot(grad, grad, NT)
        for side, (stat, basis) in enumerate(((left_new, basis_left), (right_new, basis_right))):
            moved = dot_exact(split3(stat[t]), split3(basis[t]))
            turned = moved.T
            work[2 * t + side, :, :tile] = dot_exact(split3(turned), split3(moved))
            work[2 * t + side, :, tile:] = turned
    for copy in copies:
        copy.wait()
    group = images // CHUNKS if images % CHUNKS == 0 else images
    stores = []

    def done(n):
        if n % group == group - 1:
            part = pl.ds(n + 1 - group, group)
            sem = store_sems.at[len(stores)]
            stores.append(pltpu.make_async_copy(out.at[part], input_grad.at[part], sem))
            stores[-1].start()

    units = [
        adam_units(
            (master, first, second, basis_left, basis_right),
            grad_turned,
            first_new,
            second_new,
            master_new,
            lambda: small_update(present, out.shape, small_sums, small_arrays, small_outs),
        ),
        input_units(*held, lax.rem(ids[0], 2) == 0, out, done),
    ]
    total = count + 1 + images // 2
    slots = tile // RANK
    used = [0, 0]

    def beside():
        used[0] += 1
        while used[1] < total * used[0] // slots:
            used[1] += 1
            if next(units[0], True) is not None:
                units.pop(0)
                next(units[0])

    for low in range(0, tile, BLOCK):
        high = low + BLOCK
        factors = inverse_factors(
            [
                (work[2 * t, low:high, low:high], work[2 * t + 1, low:high, low:high])
                for t in range(count)
            ],
            beside,
        )
        for n in range(2 * count):
            start = (n % 2) * 64 + BLOCK
            factor = split3(factors[n // 2][:, start : start + BLOCK])
            panel = dot_exact(factor, split3(work[n, low:high, :]))
            work[n, low:high, tile:] = panel[:, tile:]
            if high < tile:
                panel = split3(panel)
                work[n, high:, :] = work[n, high:, :] - dot_exact(
                    [p[:, high:tile] for p in panel], panel, TN
                )
    for t in range(count):
        basis_left_new[t] = work[2 * t, :, tile:].T
        basis_right_new[t] = work[2 * t + 1, :, tile:].T
    for store in stores:
        store.wait()


def finish_call(ids, present, quarters, arrays, small_arrays, loads):
    shape = jax.ShapeDtypeStruct(arrays[0].shape, F32)
    smem = pl.BlockSpec(memory_space=pltpu.SMEM)
    vmem = pl.BlockSpec(memory_space=pltpu.VMEM)
    hbm = pl.BlockSpec(memory_space=pl.ANY)
    count, tile = shape.shape[:2]
    shapes = [shape] * 7 + [jax.ShapeDtypeStruct(a.shape, F32) for a in small_arrays]
    shapes.append(jax.ShapeDtypeStruct((1, 1), F32))
    shapes.append(jax.ShapeDtypeStruct(loads[1].shape, BF16))
    return pl.pallas_call(
        finish_kernel,
        in_specs=[smem] + [vmem] * 21 + [hbm] * len(loads),
        out_specs=[vmem] * 17 + [hbm],
        out_shape=shapes,
        scratch_shapes=[
            pltpu.VMEM((2 * count, tile, 2 * tile), F32),
            pltpu.VMEM((count, tile, tile), BF16),
            pltpu.VMEM((4, quarters[0].shape[0] - count * tile // 4, tile), BF16),
            *(pltpu.VMEM(a.shape, a.dtype) for a in loads),
            pltpu.VMEM(loads[1].shape, BF16),
            pltpu.SemaphoreType.DMA((len(loads),)),
            pltpu.SemaphoreType.DMA((CHUNKS,)),
        ],
        compiler_params=pltpu.CompilerParams(vmem_limit_bytes=FINISH_VMEM),
        name="finish",
    )(ids, present[None], *quarters, *arrays, *small_arrays, *loads)


def plain_adam(gradient, master, first, second, rate):
    first_new = BETA_ONE * first + (1.0 - BETA_ONE) * gradient
    second_new = BETA_TWO * second + (1.0 - BETA_TWO) * gradient * gradient
    ratio = (
        first_new
        / (1.0 - BETA_ONE**STEP)
        / (jnp.sqrt(second_new / (1.0 - BETA_TWO**STEP)) + EPSILON)
    )
    return (master - rate * (ratio + WEIGHT_DECAY * master), first_new, second_new)


def swap(x, axis, distance):
    count = lax.axis_size(axis)
    return lax.ppermute(x, axis, [(i, i ^ distance) for i in range(count)])


def radices(count):
    out = []
    stride = 1
    while stride < count:
        left = (count // stride).bit_length() - 1
        radix = 2 if left % 2 else 4
        out.append((radix, stride))
        stride *= radix
    return out


def swap_edges(near, far):
    return swap(near, "strip", 1), lax.ppermute(far, "strip", [(1, 2), (2, 1)])


def gather_tiles(mine, meanwhile):
    core = lax.axis_index("strip") % 2
    half = mine.shape[1] // 2
    part = lax.dynamic_slice_in_dim(mine, core * half, half, axis=1)
    *steps, (last, _) = radices(lax.axis_size("img"))[::-1]
    for number, (radix, stride) in enumerate(steps):
        parts = [part] + [swap(part, "img", d * stride) for d in range(1, radix)]
        if number < len(steps) - 1:
            part = jnp.concatenate(parts, axis=0)
    count = len(parts) // 2
    pairs = [jnp.concatenate(parts[n * count : (n + 1) * count], axis=0) for n in range(2)]
    pairs, meanwhile = lax.optimization_barrier((pairs, meanwhile))
    arrays = [swap(pair, "img", d) if d else pair for d in range(last) for pair in pairs]
    return arrays + [swap(a, "strip", 1) for a in arrays], meanwhile


def tile_places(owners, tiles):
    distance = (owners // tiles) ^ lax.axis_index("img")
    place = jnp.zeros_like(owners)
    size = 1
    for radix, stride in radices(lax.axis_size("img"))[::-1]:
        place = place + size * ((distance // stride) % radix)
        size *= radix
    return place * tiles + owners % tiles


def tree_sum(terms):
    terms = [t.astype(F32) for t in terms]
    while len(terms) > 1:
        terms = [terms[n] + terms[n + 1] for n in range(0, len(terms), 2)]
    return terms[0]


def reduce_all(keep, send, tiles, quarter):
    strip = lax.axis_index("strip")
    across = strip // 2
    img = lax.axis_index("img")
    groups = lax.axis_size("img")
    (radix, _), *later = radices(groups)
    low = img % radix
    size = tiles * quarter
    columns = keep.shape[-1]
    part = keep + swap(send, "strip", 1)
    left = groups // radix
    terms = []
    for d in range(2):
        for e in range(radix):
            both = lax.dynamic_index_in_dim(part, across ^ d, 0, False)
            piece = both[: groups * size].reshape(left, radix, size, columns)
            piece = lax.dynamic_index_in_dim(piece, low ^ e, 1, False).reshape(left * size, columns)
            piece = jnp.concatenate([piece, both[groups * size :]], axis=0)
            if d or e:
                pairs = [
                    (a * groups + b, (a ^ (2 * d)) * groups + (b ^ e))
                    for a in range(4)
                    for b in range(groups)
                ]
                piece = lax.ppermute(piece, ("strip", "img"), pairs)
            terms.append(piece)
    total = tree_sum(terms).astype(BF16)
    for radix, stride in later:
        low = (img // stride) % radix
        terms = []
        for d in range(radix):
            piece = total[: left * size].reshape(left // radix, radix, size, columns)
            piece = lax.dynamic_index_in_dim(piece, low ^ d, 1, False)
            piece = piece.reshape(left // radix * size, columns)
            piece = jnp.concatenate([piece, total[left * size :]], axis=0)
            terms.append(swap(piece, "img", d * stride) if d else piece)
        total = tree_sum(terms).astype(BF16)
        left //= radix
    return [total] + [swap(total, "strip", d) for d in range(1, 4)]


def body(
    features,
    cotangent,
    present,
    owners,
    tile_master,
    tile_mom1,
    tile_mom2,
    stat_left,
    stat_right,
    basis_left,
    basis_right,
    proj_master,
    proj_mom1,
    proj_mom2,
    dec_master,
    dec_mom1,
    dec_mom2,
    code_master,
    code_mom1,
    code_mom2,
):
    images, height, wide, channels = features.shape
    tiles = tile_master.shape[0]
    img = lax.axis_index("img")
    strip = lax.axis_index("strip")
    core = strip % 2
    ids = jnp.stack([strip, img]).astype(jnp.int32)
    ready = (ids, tile_places(owners, tiles))
    parts, (ids, places) = gather_tiles(tile_master.astype(BF16), ready)
    top, bottom = features[:, 0], features[:, height - 1]
    near, far = swap_edges(jnp.where(core == 0, bottom, top), jnp.where(core == 0, top, bottom))
    (decoded, d_pre, d_resid, near_out, far_out, weights, keep, send) = main_call(
        ids,
        places,
        owners,
        present,
        features,
        near,
        far,
        cotangent,
        parts,
        proj_master.T,
        dec_master,
        code_master.T,
    )
    near, far = swap_edges(near_out, far_out)
    quarters = reduce_all(keep, send, tiles, tile_master.shape[1] // 4)
    out = finish_call(
        ids,
        present,
        quarters,
        [tile_master, tile_mom1, tile_mom2, stat_left, stat_right, basis_left, basis_right],
        [
            proj_master.T,
            proj_mom1.T,
            proj_mom2.T,
            dec_master,
            dec_mom1,
            dec_mom2,
            code_master.T,
            code_mom1.T,
            code_mom2.T,
        ],
        [weights, features, d_resid, d_pre, near, far],
    )
    small = [a.T for a in out[7:10]] + list(out[10:13]) + [a.T for a in out[13:16]]
    return (decoded, out[17], out[16].reshape(()), *out[:7], *small)


def solution(mesh):
    big = P("img", "strip", None, None)
    tile = P("img", None, None)
    in_specs = (big, big, P(), P()) + (tile,) * 7 + (P(),) * 9
    out_specs = (big, big, P()) + (tile,) * 7 + (P(),) * 9
    return jax.shard_map(body, mesh=mesh, in_specs=in_specs, out_specs=out_specs, check_vma=False)
```

```python
import jax
import jax.numpy as jnp
from jax import lax
from jax.experimental import pallas as pl
from jax.experimental.pallas import tpu as pltpu
from jax.sharding import PartitionSpec as P

STEP = 5
BETA_ONE = 0.9
BETA_TWO = 0.95
EPSILON = 1e-08
WEIGHT_DECAY = 0.01
SOFTMAX_WARMTH = 4.0
LOSS_WEIGHT = 1.25
TILE_RATE = 0.05
PROJ_RATE = 0.05
DEC_RATE = 0.1
CODE_RATE = 0.3

F32 = jnp.float32
BF16 = jnp.bfloat16
NN = ((1,), (0,))
NT = ((1,), (1,))
TN = ((0,), (0,))
GELU_A = 0.7978845608028654
GELU_B = 0.044715
LOSS_ROWS = 16
MAIN_VMEM = 56 * 1024 * 1024
FINISH_VMEM = 56 * 1024 * 1024


def dot(a, b, dims=NN):
    return lax.dot_general(a, b, (dims, ((), ())), preferred_element_type=F32)


def gelu_tanh(x):
    return jnp.tanh(GELU_A * (x + GELU_B * (x * x * x)))


def gelu(x):
    return 0.5 * x * (1.0 + gelu_tanh(x))


def gelu_both(x):
    square = x * x
    t = jnp.tanh(GELU_A * x * (1.0 + GELU_B * square))
    half = 0.5 * (1.0 + t)
    slope = half + 0.5 * x * (1.0 - t * t) * (GELU_A + 3.0 * GELU_A * GELU_B * square)
    return x * half, slope


def column_shifts(rows, wide):
    count = rows.shape[0]
    column = lax.broadcasted_iota(jnp.int32, rows.shape, 0) % wide
    before = jnp.where(column == 0, 0.0, pltpu.roll(rows, 1, 0))
    after = jnp.where(column == wide - 1, 0.0, pltpu.roll(rows, count - 1, 0))
    return before, after


def place_weights(places, ids, parts, put):
    half = parts[0].shape[1]
    count = len(parts) // 2
    size = parts[0].shape[0]
    for t in range(40):
        which = lax.div(places[t], size)
        index = lax.rem(places[t], size)
        for side in range(2):
            block = parts[side * count][index]
            for n in range(1, count):
                block = jnp.where(which == n, parts[side * count + n][index], block)
            put(t, block, pl.multiple_of((lax.rem(ids[0], 2) ^ side) * half, half))


def loss_scale(present, positions, latent):
    count = jnp.sum(present[...].astype(F32)) * positions
    return LOSS_WEIGHT / (count * latent)


def shift_lines(line, first, last):
    wide = line.shape[0]
    before = jnp.where(first, 0.0, pltpu.roll(line, 1, 0)).astype(BF16)
    after = jnp.where(last, 0.0, pltpu.roll(line, wide - 1, 0)).astype(BF16)
    return before, after


def main_kernel(batch, part_count, *refs):
    ids, places, slots, present = refs[:4]
    present_row, feat, near, far, cot = refs[4:9]
    parts = refs[9 : 9 + part_count]
    proj_full, dec_full, code_full = refs[9 + part_count : 12 + part_count]
    (decoded, d_pre_out, d_resid_out, near_out, far_out, weights_back, keep, send) = refs[
        12 + part_count : 20 + part_count
    ]
    (weights, mixer, framed, d_pre_turned, sums, g_mixer, g_proj, g_dec, g_code, totals, loss) = refs[
        20 + part_count : 31 + part_count
    ]
    proj, dec, code, norms, scale = refs[31 + part_count :]
    step = pl.program_id(0)
    steps = pl.num_programs(0)
    height, wide, channels = feat.shape[1:]
    count = height * wide
    tile = parts[0].shape[2]
    half = tile // 2
    images = framed.shape[0]
    lead = lax.rem(ids[0], 2) == 0

    @pl.when(step == 0)
    def _():
        def put(t, block, row):
            i, j = (t // 2) % 2, t % 2
            if t < 36:
                p = t // 4
                start = (p % 3) * channels + i * tile
                weights[p // 3, pl.ds(start + row, half), j * tile : (j + 1) * tile] = block
            else:
                mixer[pl.ds(i * tile + row, half), j * tile : (j + 1) * tile] = block

        place_weights(places, ids, parts, put)
        proj[...] = proj_full[...].astype(BF16)
        dec[...] = dec_full[...].astype(BF16)
        code[...] = code_full[...].astype(BF16)
        words = code[...].astype(F32)
        norms[...] = jnp.sum(words * words, axis=0, keepdims=True) * (1.0 / SOFTMAX_WARMTH)
        scale[0] = 2.0 * loss_scale(present_row, 4 * count, proj.shape[0])
        for ref in (g_mixer, g_proj, g_dec, g_code, totals, loss):
            ref[...] = jnp.zeros_like(ref)

    column = lax.broadcasted_iota(jnp.int32, (wide, channels), 0)
    first = column == 0
    last = column == wide - 1

    def chain(n):
        image = step * batch + n
        alive = present[ids[1] * images + image].astype(F32)
        pull = alive * scale[0]
        for r in range(height + 2):
            if r == 0:
                line = jnp.where(lead, far[n].astype(F32), near[n].astype(F32))
            elif r == height + 1:
                line = jnp.where(lead, near[n].astype(F32), far[n].astype(F32))
            else:
                line = feat[n, r - 1].astype(F32)
            line = gelu(line)
            before, after = shift_lines(line, first, last)
            rows = slice(r * wide, (r + 1) * wide)
            framed[image, rows, 0:channels] = before
            framed[image, rows, channels : 2 * channels] = line.astype(BF16)
            framed[image, rows, 2 * channels :] = after
        yield
        preact = dot(framed[image, 0:count, :], weights[0])
        preact += dot(framed[image, wide : wide + count, :], weights[1])
        preact += dot(framed[image, 2 * wide : 2 * wide + count, :], weights[2])
        yield
        inner, slope = gelu_both(preact)
        inner = inner.astype(BF16)
        yield
        feats = feat[n].reshape(count, channels).astype(F32)
        resid = (feats + dot(inner, mixer[...])).astype(BF16)
        yield
        latent = dot(resid, proj[...], NT)
        latent_low = latent.astype(BF16)
        yield
        logits = (2.0 / SOFTMAX_WARMTH) * dot(latent_low, code[...]) - norms[...]
        yield
        powers = jnp.exp(logits - jnp.max(logits, axis=1, keepdims=True))
        probs = powers * (1.0 / jnp.sum(powers, axis=1, keepdims=True))
        probs_low = probs.astype(BF16)
        yield
        quant = dot(probs_low, code[...], NT)
        quant_low = quant.astype(BF16)
        yield
        out = (dot(quant_low, dec[...]) * alive).astype(BF16)
        decoded[n] = out.reshape(height, wide, channels)
        diff = latent - quant
        loss[...] += alive * jnp.sum(diff * diff, axis=0, keepdims=True)
        back_out = (cot[n].reshape(count, channels).astype(F32) * alive).astype(BF16)
        pulled = pull * diff
        d_quant = (dot(back_out, dec[...], NT) - pulled).astype(BF16)
        g_dec[...] += dot(quant_low, back_out, TN)
        yield
        d_probs = dot(d_quant, code[...])
        yield
        d_logits = probs * (d_probs - jnp.sum(probs * d_probs, axis=1, keepdims=True))
        d_logits = d_logits.astype(BF16)
        totals[...] += jnp.sum(d_logits.astype(F32), axis=0, keepdims=True)
        yield
        d_latent = ((2.0 / SOFTMAX_WARMTH) * dot(d_logits, code[...], NT) + pulled).astype(BF16)
        yield
        d_resid = dot(d_latent, proj[...]).astype(BF16)
        d_resid_out[n] = d_resid.reshape(height, wide, channels)
        g_code[...] += dot(d_quant, probs_low, TN)
        g_code[...] += (2.0 / SOFTMAX_WARMTH) * dot(latent_low, d_logits, TN)
        yield
        d_pre = (slope * dot(d_resid, mixer[...], NT)).astype(BF16)
        g_proj[...] += dot(d_latent, resid, TN)
        yield
        d_pre_out[n] = d_pre.reshape(height, wide, channels)
        top, bottom = d_pre[:wide], d_pre[count - wide :]
        near_out[n] = jnp.where(lead, bottom, top)
        far_out[n] = jnp.where(lead, top, bottom)
        g_mixer[...] += dot(d_resid, inner, TN)
        yield
        d_pre_turned[image] = d_pre.T

    live = [chain(n) for n in range(batch)]
    while live:
        live = [c for c in live if next(c, True) is None]

    @pl.when(step == steps - 1)
    def _():
        for a in range(3):
            for b in range(3):
                block = weights[2 - a, (2 - b) * channels : (3 - b) * channels, :]
                weights_back[a, b * channels : (b + 1) * channels, :] = block.T
        for line in range(3):
            total = None
            for n in range(images):
                term = dot(d_pre_turned[n], framed[n, line * wide : line * wide + count, :])
                total = term if total is None else total + term
            sums[line] = total
        for ref in (keep, send):
            ref[...] = jnp.zeros_like(ref)
        quarter = tile // 4
        for t in range(40):
            i, j = (t // 2) % 2, t % 2
            if t < 36:
                p = t // 4
                left = (p % 3) * channels + i * tile
                block = sums[p // 3, j * tile : (j + 1) * tile, left : left + tile]
            else:
                block = g_mixer[j * tile : (j + 1) * tile, i * tile : (i + 1) * tile]
            block = block.astype(BF16)
            for q in range(0, 4, 2):
                even = block[q * quarter : (q + 1) * quarter]
                odd = block[(q + 1) * quarter : (q + 2) * quarter]
                row = pl.ds(pl.multiple_of(slots[t] * quarter, quarter), quarter)
                keep[q // 2, row] = jnp.where(lead, even, odd)
                send[q // 2, row] = jnp.where(lead, odd, even)
        g_words = g_code[...] - (2.0 / SOFTMAX_WARMTH) * totals[...] * code[...].astype(F32)
        blocks = []
        for grad in (g_proj[...], g_dec[...], g_words):
            for left in range(0, grad.shape[1], 128):
                blocks.append(grad[:, left : left + 128].astype(BF16))
        size = blocks[0].shape[0]
        each = len(blocks) // 4
        start = keep.shape[1] - each * size - LOSS_ROWS
        for x in range(2):
            for n in range(each):
                even, odd = blocks[2 * x * each + n], blocks[(2 * x + 1) * each + n]
                row = slice(start + n * size, start + (n + 1) * size)
                keep[x, row] = jnp.where(lead, even, odd)
                send[x, row] = jnp.where(lead, odd, even)
        row = start + each * size
        value = jnp.broadcast_to(loss[...] * (1.0 / LOSS_ROWS), (LOSS_ROWS, loss.shape[1]))
        keep[0, row:, 0 : loss.shape[1]] = jnp.where(lead, value, 0.0).astype(BF16)
        send[0, row:, 0 : loss.shape[1]] = jnp.where(lead, 0.0, value).astype(BF16)


def main_call(ids, places, slots, present, feat, near, far, cot, parts, proj, dec, code):
    images, height, wide, channels = feat.shape
    latent, words = code.shape
    size, half, tile = parts[0].shape
    slot_count = size * len(parts) // 2
    batch = 5 if images % 5 == 0 else 1
    smem = pl.BlockSpec(memory_space=pltpu.SMEM)
    strip = pl.BlockSpec((batch, height, wide, channels), lambda i: (i, 0, 0, 0))
    line = pl.BlockSpec((batch, wide, channels), lambda i: (i, 0, 0))

    def whole(shape):
        return pl.BlockSpec(shape, lambda i: (0,) * len(shape))

    big = jax.ShapeDtypeStruct(feat.shape, BF16)
    edge = jax.ShapeDtypeStruct(near.shape, BF16)
    rows = (2 * latent * channels + latent * words) // (4 * 128) + LOSS_ROWS
    part = jax.ShapeDtypeStruct((2, slot_count * tile // 4 + rows, tile), BF16)
    weights = jax.ShapeDtypeStruct((3, 3 * channels, channels), BF16)
    shapes = (big, big, big, edge, edge, weights, part, part)
    return pl.pallas_call(
        lambda *refs: main_kernel(batch, len(parts), *refs),
        grid=(images // batch,),
        in_specs=[smem] * 4
        + [whole((1, present.shape[0])), strip, line, line, strip]
        + [whole(a.shape) for a in (*parts, proj, dec, code)],
        out_specs=[strip] * 3 + [line] * 2 + [whole(s.shape) for s in shapes[5:]],
        out_shape=shapes,
        scratch_shapes=[
            pltpu.VMEM((3, 3 * channels, channels), BF16),
            pltpu.VMEM((channels, channels), BF16),
            pltpu.VMEM((images, (height + 2) * wide, 3 * channels), BF16),
            pltpu.VMEM((images, channels, height * wide), BF16),
            pltpu.VMEM((3, channels, 3 * channels), F32),
            pltpu.VMEM((channels, channels), F32),
            pltpu.VMEM((latent, channels), F32),
            pltpu.VMEM((latent, channels), F32),
            pltpu.VMEM((latent, words), F32),
            pltpu.VMEM((1, words), F32),
            pltpu.VMEM((1, latent), F32),
            pltpu.VMEM(proj.shape, BF16),
            pltpu.VMEM(dec.shape, BF16),
            pltpu.VMEM(code.shape, BF16),
            pltpu.VMEM((1, words), F32),
            pltpu.SMEM((1,), F32),
        ],
        compiler_params=pltpu.CompilerParams(vmem_limit_bytes=MAIN_VMEM),
        name="main",
    )(ids, places, slots, present, present[None], feat, near, far, cot, *parts, proj, dec, code)


BLOCK = 32
RANK = 4


def split3(x):
    high = x.astype(BF16)
    rest = x - high.astype(F32)
    middle = rest.astype(BF16)
    return high, middle, (rest - middle.astype(F32)).astype(BF16)


def dot_exact(a, b, dims=NN):
    left = jnp.concatenate([a[n] for n in (0, 0, 1, 1, 0, 2)], axis=dims[0][0])
    right = jnp.concatenate([b[n] for n in (0, 1, 0, 1, 2, 0)], axis=dims[1][0])
    return dot(left, right, dims)


def inverse_factors(pairs, beside):
    half = 64
    lane = lax.broadcasted_iota(jnp.int32, (8, 128), 1)
    sub = lax.broadcasted_iota(jnp.int32, (8, 128), 0)
    base = jnp.where(lane >= half, half, 0)
    inner = lane - base
    count = BLOCK // 8

    def pick(x, k):
        return jnp.take_along_axis(x, base + k, axis=1)

    mats = []
    for one, two in pairs:
        zero = jnp.zeros((BLOCK, half - BLOCK), F32)
        wide = jnp.concatenate([one, zero, two, zero], axis=1)
        mats.append(
            [
                wide[8 * v : 8 * v + 8] + jnp.where(inner == sub + (8 * v + BLOCK), 1.0, 0.0)
                for v in range(count)
            ]
        )
    for start in range(0, BLOCK, RANK):
        beside()
        v0, s0 = start // 8, start % 8
        for rows in mats:
            pivots = [jnp.broadcast_to(rows[v0][s0 + i : s0 + i + 1], (8, 128)) for i in range(RANK)]
            columns = [pick(rows[v0], start + j) for j in range(RANK)]
            core = {
                (i, j): jnp.broadcast_to(columns[j][s0 + i : s0 + i + 1], (8, 128))
                for i in range(RANK)
                for j in range(i, RANK)
            }
            lower = {}
            scaled = []
            for i in range(RANK):
                root = lax.rsqrt(core[i, i])
                for j in range(i + 1, RANK):
                    lower[j, i] = core[i, j] * (root * root)
                for j in range(i + 1, RANK):
                    for k in range(j, RANK):
                        core[j, k] = core[j, k] - lower[j, i] * core[i, k]
                    pivots[j] = pivots[j] - lower[j, i] * pivots[i]
                scaled.append((root, pivots[i] * root))
            if start + RANK < BLOCK:
                solved = [None] * RANK
                for i in range(RANK - 1, -1, -1):
                    solved[i] = scaled[i][1] * scaled[i][0]
                    for j in range(i + 1, RANK):
                        solved[i] = solved[i] - lower[j, i] * solved[j]
            for v in range(v0, count):
                new = rows[v]
                if v > v0 or s0 + RANK < 8:
                    for j in range(RANK):
                        column = columns[j] if v == v0 else pick(rows[v], start + j)
                        new = new - column * solved[j]
                if v == v0:
                    if s0 > 0:
                        new = jnp.where(sub < s0, rows[v], new)
                    for i in range(RANK):
                        new = jnp.where(sub == s0 + i, scaled[i][1], new)
                rows[v] = new
    return [jnp.concatenate(rows, axis=0) for rows in mats]


def small_update(present, shape, sums, arrays, outs):
    total = jnp.concatenate([sums[q, : sums.shape[1] - LOSS_ROWS] for q in range(4)], axis=0).astype(F32)
    row = 0
    for n, rate in enumerate((PROJ_RATE, DEC_RATE, CODE_RATE)):
        rows, columns = arrays[3 * n].shape
        pieces = []
        for _ in range(columns // 128):
            pieces.append(total[row : row + rows])
            row += rows
        grad = jnp.concatenate(pieces, axis=1)
        new = plain_adam(grad, *(a[...] for a in arrays[3 * n : 3 * n + 3]), rate)
        for out, value in zip(outs[3 * n : 3 * n + 3], new):
            out[...] = value
    loss = sums[0, sums.shape[1] - LOSS_ROWS :].astype(F32)
    scale = loss_scale(present, 4 * shape[1] * shape[2], arrays[0].shape[0])
    outs[9][...] = jnp.sum(loss, axis=(0, 1), keepdims=True) * scale


def taps(line, first, last):
    before, after = shift_lines(line.astype(F32), first, last)
    return jnp.concatenate([before, line, after], axis=1)


def inner_kernel(batch, weights, feat, d_resid, d_pre, out):
    height, wide, channels = feat.shape[1:]
    column = lax.broadcasted_iota(jnp.int32, (wide, channels), 0)
    first = column == 0
    last = column == wide - 1
    lines = height - 2
    rows = lines * wide
    sides = []
    for n in range(batch):
        seen = [taps(d_pre[n, r], first, last) for r in range(height)]
        sides.append(jnp.concatenate(seen, axis=0))
    acts = [None] * batch
    for a in range(3):
        for n in range(batch):
            term = dot(sides[n][a * wide : a * wide + rows], weights[a])
            acts[n] = term if acts[n] is None else acts[n] + term
    for n in range(batch):
        for r in range(lines):
            _, slope = gelu_both(feat[n, 1 + r].astype(F32))
            act = acts[n][r * wide : (r + 1) * wide]
            out[n, 1 + r] = (d_resid[n, 1 + r].astype(F32) + slope * act).astype(BF16)
        for r in (0, height - 1):
            out[n, r] = jnp.zeros((wide, channels), BF16)


def inner_call(weights, feat, d_resid, d_pre):
    images, height, wide, channels = feat.shape
    batch = 5 if images % 5 == 0 else 1
    strip = pl.BlockSpec((batch, height, wide, channels), lambda i: (i, 0, 0, 0))
    return pl.pallas_call(
        lambda *refs: inner_kernel(batch, *refs),
        grid=(images // batch,),
        in_specs=[pl.BlockSpec(weights.shape, lambda i: (0, 0, 0)), strip, strip, strip],
        out_specs=strip,
        out_shape=jax.ShapeDtypeStruct(feat.shape, BF16),
        compiler_params=pltpu.CompilerParams(vmem_limit_bytes=FINISH_VMEM),
        name="inner_lines",
    )(weights, feat, d_resid, d_pre)


def edge_units(group, weights, feats, d_resids, d_pres, near, far, lead, outs):
    images, _, wide, channels = d_pres[0].shape
    column = lax.broadcasted_iota(jnp.int32, (wide, channels), 0)
    first = column == 0
    last = column == wide - 1
    for base in range(0, images, group):
        members = [(n, end) for n in range(base, base + group) for end in range(2)]
        seen = []
        for n, end in members:
            if end == 0:
                lines = [jnp.where(lead, far[n], near[n]), d_pres[0][n, 0], d_pres[0][n, 1]]
            else:
                lines = [d_pres[1][n, 0], d_pres[1][n, 1], jnp.where(lead, near[n], far[n])]
            seen.append([taps(line, first, last) for line in lines])
        act = None
        for a in range(3):
            term = dot(jnp.concatenate([s[a] for s in seen], axis=0), weights[a])
            act = term if act is None else act + term
        for k, (n, end) in enumerate(members):
            _, slope = gelu_both(feats[end][n].astype(F32))
            total = d_resids[end][n].astype(F32) + slope * act[k * wide : (k + 1) * wide]
            outs[end][n] = total.astype(BF16)
        yield


def adam_units(tiles, grad_turned, first_new, second_new, master_new, small):
    master, first, second, basis_left, basis_right = tiles
    for t in range(master.shape[0]):
        one_low = basis_left[t].astype(BF16)
        two_low = basis_right[t].astype(BF16)
        turned = dot(one_low, grad_turned[t], ((0,), (1,)))
        turned = dot(turned.astype(BF16), two_low)
        mom = BETA_ONE * first[t] + (1.0 - BETA_ONE) * turned
        var = BETA_TWO * second[t] + (1.0 - BETA_TWO) * turned * turned
        first_new[t] = mom
        second_new[t] = var
        ratio = mom / (1.0 - BETA_ONE**STEP) / (jnp.sqrt(var / (1.0 - BETA_TWO**STEP)) + EPSILON)
        back = dot(dot(one_low, ratio.astype(BF16)).astype(BF16), two_low, NT)
        master_new[t] = master[t] - TILE_RATE * (back + WEIGHT_DECAY * master[t])
        yield
    small()
    yield


EDGE_GROUP = 4


def finish_kernel(*refs):
    ids, present = refs[:2]
    quarters = refs[2:6]
    master, first, second, left, right, basis_left, basis_right = refs[6:13]
    small_arrays = refs[13:22]
    weights_far, feat, d_resid, d_pre, near_far, far_far = refs[22:28]
    (master_new, first_new, second_new, left_new, right_new, basis_left_new, basis_right_new) = refs[
        29:36
    ]
    small_outs = refs[36:46]
    input_grad = refs[46]
    work, grad_turned, small_sums = refs[47:50]
    weights, feats, d_resids, d_pres, near, far, outs, load_sems, store_sems = refs[50:]
    count, tile = master.shape[:2]
    images, height = feat.shape[:2]
    ends = (0, height - 1)
    loads = [(weights_far, weights), (near_far, near), (far_far, far)]
    for end in range(2):
        loads.append((feat.at[:, ends[end]], feats.at[end]))
        loads.append((d_resid.at[:, ends[end]], d_resids.at[end]))
        loads.append((d_pre.at[:, pl.ds(end * (height - 2), 2)], d_pres.at[end]))
    copies = [
        pltpu.make_async_copy(src, dst, load_sems.at[n]) for n, (src, dst) in enumerate(loads)
    ]
    for copy in copies:
        copy.start()
    for d in range(4):
        quarter = tile // 4
        row = pl.multiple_of((ids[0] ^ d) * quarter, quarter)
        rows = count * quarter
        grad_turned[:, pl.ds(row, quarter), :] = quarters[d][:rows].reshape(count, quarter, tile)
        small_sums[ids[0] ^ d] = quarters[d][rows:]
    for t in range(count):
        grad = grad_turned[t]
        left_new[t] = BETA_TWO * left[t] + (1.0 - BETA_TWO) * dot(grad, grad, TN)
        right_new[t] = BETA_TWO * right[t] + (1.0 - BETA_TWO) * dot(grad, grad, NT)
        for side, (stat, basis) in enumerate(((left_new, basis_left), (right_new, basis_right))):
            moved = dot_exact(split3(stat[t]), split3(basis[t]))
            turned = moved.T
            work[2 * t + side, :, :tile] = dot_exact(split3(turned), split3(moved))
            work[2 * t + side, :, tile:] = turned
    for copy in copies:
        copy.wait()
    group = EDGE_GROUP if images % EDGE_GROUP == 0 else 1
    units = [
        adam_units(
            (master, first, second, basis_left, basis_right),
            grad_turned,
            first_new,
            second_new,
            master_new,
            lambda: small_update(present, feat.shape, small_sums, small_arrays, small_outs),
        ),
        edge_units(
            group,
            weights,
            [feats.at[end] for end in range(2)],
            [d_resids.at[end] for end in range(2)],
            [d_pres.at[end] for end in range(2)],
            near,
            far,
            lax.rem(ids[0], 2) == 0,
            [outs.at[end] for end in range(2)],
        ),
    ]
    total = count + 1 + images // group
    slots = tile // RANK
    used = [0, 0]

    def beside():
        used[0] += 1
        while used[1] < total * used[0] // slots:
            used[1] += 1
            if next(units[0], True) is not None:
                units.pop(0)
                next(units[0])

    for low in range(0, tile, BLOCK):
        high = low + BLOCK
        factors = inverse_factors(
            [
                (work[2 * t, low:high, low:high], work[2 * t + 1, low:high, low:high])
                for t in range(count)
            ],
            beside,
        )
        for n in range(2 * count):
            start = (n % 2) * 64 + BLOCK
            factor = split3(factors[n // 2][:, start : start + BLOCK])
            panel = dot_exact(factor, split3(work[n, low:high, :]))
            work[n, low:high, tile:] = panel[:, tile:]
            if high < tile:
                panel = split3(panel)
                work[n, high:, :] = work[n, high:, :] - dot_exact(
                    [p[:, high:tile] for p in panel], panel, TN
                )
    for t in range(count):
        basis_left_new[t] = work[2 * t, :, tile:].T
        basis_right_new[t] = work[2 * t + 1, :, tile:].T
    stores = [
        pltpu.make_async_copy(outs.at[end], input_grad.at[:, ends[end]], store_sems.at[end])
        for end in range(2)
    ]
    for store in stores:
        store.start()
    for store in stores:
        store.wait()


def finish_call(ids, present, quarters, arrays, small_arrays, loads):
    shape = jax.ShapeDtypeStruct(arrays[0].shape, F32)
    smem = pl.BlockSpec(memory_space=pltpu.SMEM)
    vmem = pl.BlockSpec(memory_space=pltpu.VMEM)
    hbm = pl.BlockSpec(memory_space=pl.ANY)
    count, tile = shape.shape[:2]
    shapes = [shape] * 7 + [jax.ShapeDtypeStruct(a.shape, F32) for a in small_arrays]
    shapes.append(jax.ShapeDtypeStruct((1, 1), F32))
    weights, feat, _, _, near, far, partial = loads
    images, height, wide, channels = feat.shape
    shapes.append(jax.ShapeDtypeStruct(feat.shape, BF16))
    ends = (2, images, wide, channels)
    return pl.pallas_call(
        finish_kernel,
        in_specs=[smem] + [vmem] * 21 + [hbm] * len(loads),
        out_specs=[vmem] * 17 + [hbm],
        out_shape=shapes,
        scratch_shapes=[
            pltpu.VMEM((2 * count, tile, 2 * tile), F32),
            pltpu.VMEM((count, tile, tile), BF16),
            pltpu.VMEM((4, quarters[0].shape[0] - count * tile // 4, tile), BF16),
            pltpu.VMEM(weights.shape, BF16),
            pltpu.VMEM(ends, BF16),
            pltpu.VMEM(ends, BF16),
            pltpu.VMEM((2, images, 2, wide, channels), BF16),
            pltpu.VMEM(near.shape, BF16),
            pltpu.VMEM(far.shape, BF16),
            pltpu.VMEM(ends, BF16),
            pltpu.SemaphoreType.DMA((9,)),
            pltpu.SemaphoreType.DMA((2,)),
        ],
        input_output_aliases={22 + len(loads) - 1: 17},
        compiler_params=pltpu.CompilerParams(vmem_limit_bytes=FINISH_VMEM),
        name="finish",
    )(ids, present[None], *quarters, *arrays, *small_arrays, *loads)


def plain_adam(gradient, master, first, second, rate):
    first_new = BETA_ONE * first + (1.0 - BETA_ONE) * gradient
    second_new = BETA_TWO * second + (1.0 - BETA_TWO) * gradient * gradient
    ratio = (
        first_new
        / (1.0 - BETA_ONE**STEP)
        / (jnp.sqrt(second_new / (1.0 - BETA_TWO**STEP)) + EPSILON)
    )
    return (master - rate * (ratio + WEIGHT_DECAY * master), first_new, second_new)


def swap(x, axis, distance):
    count = lax.axis_size(axis)
    return lax.ppermute(x, axis, [(i, i ^ distance) for i in range(count)])


def radices(count):
    out = []
    stride = 1
    while stride < count:
        left = (count // stride).bit_length() - 1
        radix = 2 if left % 2 else 4
        out.append((radix, stride))
        stride *= radix
    return out


def swap_edges(near, far):
    return swap(near, "strip", 1), lax.ppermute(far, "strip", [(1, 2), (2, 1)])


def gather_tiles(mine, meanwhile):
    core = lax.axis_index("strip") % 2
    half = mine.shape[1] // 2
    part = lax.dynamic_slice_in_dim(mine, core * half, half, axis=1)
    *steps, (last, _) = radices(lax.axis_size("img"))[::-1]
    for number, (radix, stride) in enumerate(steps):
        parts = [part] + [swap(part, "img", d * stride) for d in range(1, radix)]
        if number < len(steps) - 1:
            part = jnp.concatenate(parts, axis=0)
    count = len(parts) // 2
    pairs = [jnp.concatenate(parts[n * count : (n + 1) * count], axis=0) for n in range(2)]
    pairs, meanwhile = lax.optimization_barrier((pairs, meanwhile))
    arrays = [swap(pair, "img", d) if d else pair for d in range(last) for pair in pairs]
    return arrays + [swap(a, "strip", 1) for a in arrays], meanwhile


def tile_places(owners, tiles):
    distance = (owners // tiles) ^ lax.axis_index("img")
    place = jnp.zeros_like(owners)
    size = 1
    for radix, stride in radices(lax.axis_size("img"))[::-1]:
        place = place + size * ((distance // stride) % radix)
        size *= radix
    return place * tiles + owners % tiles


def tree_sum(terms):
    terms = [t.astype(F32) for t in terms]
    while len(terms) > 1:
        terms = [terms[n] + terms[n + 1] for n in range(0, len(terms), 2)]
    return terms[0]


def reduce_all(keep, send, tiles, quarter, inner, inputs):
    strip = lax.axis_index("strip")
    across = strip // 2
    img = lax.axis_index("img")
    groups = lax.axis_size("img")
    (radix, _), *later = radices(groups)
    low = img % radix
    size = tiles * quarter
    columns = keep.shape[-1]
    part = keep + swap(send, "strip", 1)
    left = groups // radix
    terms = []
    part, inputs = lax.optimization_barrier((part, inputs))
    for d in range(2):
        for e in range(radix):
            both = lax.dynamic_index_in_dim(part, across ^ d, 0, False)
            piece = both[: groups * size].reshape(left, radix, size, columns)
            piece = lax.dynamic_index_in_dim(piece, low ^ e, 1, False).reshape(left * size, columns)
            piece = jnp.concatenate([piece, both[groups * size :]], axis=0)
            if d or e:
                pairs = [
                    (a * groups + b, (a ^ (2 * d)) * groups + (b ^ e))
                    for a in range(4)
                    for b in range(groups)
                ]
                piece = lax.ppermute(piece, ("strip", "img"), pairs)
            terms.append(piece)
    terms, result = lax.optimization_barrier((terms, inner(*inputs)))
    total = tree_sum(terms).astype(BF16)
    for radix, stride in later:
        low = (img // stride) % radix
        terms = []
        for d in range(radix):
            piece = total[: left * size].reshape(left // radix, radix, size, columns)
            piece = lax.dynamic_index_in_dim(piece, low ^ d, 1, False)
            piece = piece.reshape(left // radix * size, columns)
            piece = jnp.concatenate([piece, total[left * size :]], axis=0)
            terms.append(swap(piece, "img", d * stride) if d else piece)
        total = tree_sum(terms).astype(BF16)
        left //= radix
    return [total] + [swap(total, "strip", d) for d in range(1, 4)], result


def body(
    features,
    cotangent,
    present,
    owners,
    tile_master,
    tile_mom1,
    tile_mom2,
    stat_left,
    stat_right,
    basis_left,
    basis_right,
    proj_master,
    proj_mom1,
    proj_mom2,
    dec_master,
    dec_mom1,
    dec_mom2,
    code_master,
    code_mom1,
    code_mom2,
):
    images, height, wide, channels = features.shape
    tiles = tile_master.shape[0]
    img = lax.axis_index("img")
    strip = lax.axis_index("strip")
    core = strip % 2
    ids = jnp.stack([strip, img]).astype(jnp.int32)
    ready = (ids, tile_places(owners, tiles))
    parts, (ids, places) = gather_tiles(tile_master.astype(BF16), ready)
    top, bottom = features[:, 0], features[:, height - 1]
    near, far = swap_edges(jnp.where(core == 0, bottom, top), jnp.where(core == 0, top, bottom))
    (decoded, d_pre, d_resid, near_out, far_out, weights, keep, send) = main_call(
        ids,
        places,
        owners,
        present,
        features,
        near,
        far,
        cotangent,
        parts,
        proj_master.T,
        dec_master,
        code_master.T,
    )
    near, far = swap_edges(near_out, far_out)
    quarters, partial = reduce_all(
        keep,
        send,
        tiles,
        tile_master.shape[1] // 4,
        inner_call,
        (weights, features, d_resid, d_pre),
    )
    out = finish_call(
        ids,
        present,
        quarters,
        [tile_master, tile_mom1, tile_mom2, stat_left, stat_right, basis_left, basis_right],
        [
            proj_master.T,
            proj_mom1.T,
            proj_mom2.T,
            dec_master,
            dec_mom1,
            dec_mom2,
            code_master.T,
            code_mom1.T,
            code_mom2.T,
        ],
        [weights, features, d_resid, d_pre, near, far, partial],
    )
    small = [a.T for a in out[7:10]] + list(out[10:13]) + [a.T for a in out[13:16]]
    return (decoded, out[17], out[16].reshape(()), *out[:7], *small)


def solution(mesh):
    big = P("img", "strip", None, None)
    tile = P("img", None, None)
    in_specs = (big, big, P(), P()) + (tile,) * 7 + (P(),) * 9
    out_specs = (big, big, P()) + (tile,) * 7 + (P(),) * 9
    return jax.shard_map(body, mesh=mesh, in_specs=in_specs, out_specs=out_specs, check_vma=False)
```

```python
import jax
import jax.numpy as jnp
from jax import lax
from jax.experimental import pallas as pl
from jax.experimental.pallas import tpu as pltpu
from jax.sharding import PartitionSpec as P

STEP = 5
BETA_ONE = 0.9
BETA_TWO = 0.95
EPSILON = 1e-08
WEIGHT_DECAY = 0.01
SOFTMAX_WARMTH = 4.0
LOSS_WEIGHT = 1.25
TILE_RATE = 0.05
PROJ_RATE = 0.05
DEC_RATE = 0.1
CODE_RATE = 0.3

F32 = jnp.float32
BF16 = jnp.bfloat16
NN = ((1,), (0,))
NT = ((1,), (1,))
TN = ((0,), (0,))
GELU_A = 0.7978845608028654
GELU_B = 0.044715
LOSS_ROWS = 16
MAIN_VMEM = 56 * 1024 * 1024
FINISH_VMEM = 56 * 1024 * 1024


def dot(a, b, dims=NN):
    return lax.dot_general(a, b, (dims, ((), ())), preferred_element_type=F32)


def gelu_tanh(x):
    return jnp.tanh(GELU_A * (x + GELU_B * (x * x * x)))


def gelu(x):
    return 0.5 * x * (1.0 + gelu_tanh(x))


def gelu_both(x):
    square = x * x
    t = jnp.tanh(GELU_A * x * (1.0 + GELU_B * square))
    half = 0.5 * (1.0 + t)
    slope = half + 0.5 * x * (1.0 - t * t) * (GELU_A + 3.0 * GELU_A * GELU_B * square)
    return x * half, slope


def column_shifts(rows, wide):
    count = rows.shape[0]
    column = lax.broadcasted_iota(jnp.int32, rows.shape, 0) % wide
    before = jnp.where(column == 0, 0.0, pltpu.roll(rows, 1, 0))
    after = jnp.where(column == wide - 1, 0.0, pltpu.roll(rows, count - 1, 0))
    return before, after


def place_weights(places, ids, parts, put):
    half = parts[0].shape[1]
    count = len(parts) // 2
    size = parts[0].shape[0]
    for t in range(40):
        which = lax.div(places[t], size)
        index = lax.rem(places[t], size)
        for side in range(2):
            block = parts[side * count][index]
            for n in range(1, count):
                block = jnp.where(which == n, parts[side * count + n][index], block)
            put(t, block, pl.multiple_of((lax.rem(ids[0], 2) ^ side) * half, half))


def loss_scale(present, positions, latent):
    count = jnp.sum(present[...].astype(F32)) * positions
    return LOSS_WEIGHT / (count * latent)


def shift_lines(line, first, last):
    wide = line.shape[0]
    before = jnp.where(first, 0.0, pltpu.roll(line, 1, 0)).astype(BF16)
    after = jnp.where(last, 0.0, pltpu.roll(line, wide - 1, 0)).astype(BF16)
    return before, after


def main_kernel(batch, part_count, *refs):
    ids, places, slots, present = refs[:4]
    present_row, feat, near, far, cot = refs[4:9]
    parts = refs[9 : 9 + part_count]
    proj_full, dec_full, code_full = refs[9 + part_count : 12 + part_count]
    (decoded_far, d_pre_far, d_resid_far, near_out, far_out, weights_far, keep, send) = refs[
        12 + part_count : 20 + part_count
    ]
    (weights, mixer, framed, d_pre_turned, g_mixer, g_proj, g_dec, g_code, totals, loss) = refs[
        20 + part_count : 30 + part_count
    ]
    proj, dec, code, norms, scale = refs[30 + part_count : 35 + part_count]
    decoded, d_pre_out, d_resid_out, weights_back, big_sems, weight_sem = refs[35 + part_count :]
    step = pl.program_id(0)
    steps = pl.num_programs(0)
    height, wide, channels = feat.shape[1:]
    count = height * wide
    tile = parts[0].shape[2]
    half = tile // 2
    images = framed.shape[0]
    lead = lax.rem(ids[0], 2) == 0

    @pl.when(step == 0)
    def _():
        def put(t, block, row):
            i, j = (t // 2) % 2, t % 2
            if t < 36:
                p = t // 4
                start = (p % 3) * channels + i * tile
                weights[p // 3, pl.ds(start + row, half), j * tile : (j + 1) * tile] = block
            else:
                mixer[pl.ds(i * tile + row, half), j * tile : (j + 1) * tile] = block

        place_weights(places, ids, parts, put)
        proj[...] = proj_full[...].astype(BF16)
        dec[...] = dec_full[...].astype(BF16)
        code[...] = code_full[...].astype(BF16)
        words = code[...].astype(F32)
        norms[...] = jnp.sum(words * words, axis=0, keepdims=True) * (1.0 / SOFTMAX_WARMTH)
        scale[0] = 2.0 * loss_scale(present_row, 4 * count, proj.shape[0])
        for ref in (keep, send, g_mixer, g_proj, g_dec, g_code, totals, loss):
            ref[...] = jnp.zeros_like(ref)

    @pl.when(step == 0)
    def _():
        for a in range(3):
            for b in range(3):
                block = weights[2 - a, (2 - b) * channels : (3 - b) * channels, :]
                weights_back[a, b * channels : (b + 1) * channels, :] = block.T
        pltpu.make_async_copy(weights_back, weights_far, weight_sem).start()

    column = lax.broadcasted_iota(jnp.int32, (wide, channels), 0)
    first = column == 0
    last = column == wide - 1

    def chain(n):
        image = step * batch + n
        alive = present[ids[1] * images + image].astype(F32)
        pull = alive * scale[0]
        for r in range(height + 2):
            if r == 0:
                line = jnp.where(lead, far[n].astype(F32), near[n].astype(F32))
            elif r == height + 1:
                line = jnp.where(lead, near[n].astype(F32), far[n].astype(F32))
            else:
                line = feat[n, r - 1].astype(F32)
            line = gelu(line)
            before, after = shift_lines(line, first, last)
            rows = slice(r * wide, (r + 1) * wide)
            framed[image, rows, 0:channels] = before
            framed[image, rows, channels : 2 * channels] = line.astype(BF16)
            framed[image, rows, 2 * channels :] = after
        yield
        preact = dot(framed[image, 0:count, :], weights[0])
        preact += dot(framed[image, wide : wide + count, :], weights[1])
        preact += dot(framed[image, 2 * wide : 2 * wide + count, :], weights[2])
        yield
        inner, slope = gelu_both(preact)
        inner = inner.astype(BF16)
        yield
        feats = feat[n].reshape(count, channels).astype(F32)
        resid = (feats + dot(inner, mixer[...])).astype(BF16)
        yield
        latent = dot(resid, proj[...], NT)
        latent_low = latent.astype(BF16)
        yield
        logits = (2.0 / SOFTMAX_WARMTH) * dot(latent_low, code[...]) - norms[...]
        yield
        powers = jnp.exp(logits - jnp.max(logits, axis=1, keepdims=True))
        probs = powers * (1.0 / jnp.sum(powers, axis=1, keepdims=True))
        probs_low = probs.astype(BF16)
        yield
        quant = dot(probs_low, code[...], NT)
        quant_low = quant.astype(BF16)
        yield
        out = (dot(quant_low, dec[...]) * alive).astype(BF16)
        decoded[image] = out.reshape(height, wide, channels)
        diff = latent - quant
        loss[...] += alive * jnp.sum(diff * diff, axis=0, keepdims=True)
        back_out = (cot[n].reshape(count, channels).astype(F32) * alive).astype(BF16)
        pulled = pull * diff
        d_quant = (dot(back_out, dec[...], NT) - pulled).astype(BF16)
        g_dec[...] += dot(quant_low, back_out, TN)
        yield
        d_probs = dot(d_quant, code[...])
        yield
        d_logits = probs * (d_probs - jnp.sum(probs * d_probs, axis=1, keepdims=True))
        d_logits = d_logits.astype(BF16)
        yield
        d_latent = ((2.0 / SOFTMAX_WARMTH) * dot(d_logits, code[...], NT) + pulled).astype(BF16)
        yield
        d_resid = dot(d_latent, proj[...]).astype(BF16)
        d_resid_out[image] = d_resid.reshape(height, wide, channels)
        g_code[...] += dot(d_quant, probs_low, TN)
        ones = jnp.ones((count, 16), BF16)
        both = dot(jnp.concatenate([latent_low, ones], axis=1), d_logits, TN)
        size = latent.shape[1]
        g_code[...] += (2.0 / SOFTMAX_WARMTH) * both[:size]
        totals[...] += both[size : size + 1]
        yield
        d_pre = (slope * dot(d_resid, mixer[...], NT)).astype(BF16)
        g_proj[...] += dot(d_latent, resid, TN)
        yield
        d_pre_out[image] = d_pre.reshape(height, wide, channels)
        top, bottom = d_pre[:wide], d_pre[count - wide :]
        near_out[n] = jnp.where(lead, bottom, top)
        far_out[n] = jnp.where(lead, top, bottom)
        g_mixer[...] += dot(d_resid, inner, TN)
        yield
        d_pre_turned[image] = d_pre.T

    live = [chain(n) for n in range(batch)]
    while live:
        live = [c for c in live if next(c, True) is None]
    bigs = ((decoded, decoded_far), (d_pre_out, d_pre_far), (d_resid_out, d_resid_far))

    def store(n, number):
        part = pl.ds(number * batch, batch)
        return pltpu.make_async_copy(bigs[n][0].at[part], bigs[n][1].at[part], big_sems.at[n, number])

    for n in range(3):
        store(n, step).start()

    @pl.when(step == steps - 1)
    def _():
        quarter = tile // 4

        def put(t, block):
            block = block.astype(BF16)
            for q in range(0, 4, 2):
                even = block[q * quarter : (q + 1) * quarter]
                odd = block[(q + 1) * quarter : (q + 2) * quarter]
                row = pl.ds(pl.multiple_of(slots[t] * quarter, quarter), quarter)
                keep[q // 2, row] = jnp.where(lead, even, odd)
                send[q // 2, row] = jnp.where(lead, odd, even)

        for t in range(36, 40):
            i, j = (t // 2) % 2, t % 2
            put(t, g_mixer[j * tile : (j + 1) * tile, i * tile : (i + 1) * tile])
        for line in range(3):
            total = None
            for n in range(images):
                term = dot(d_pre_turned[n], framed[n, line * wide : line * wide + count, :])
                total = term if total is None else total + term
            for t in range(12 * line, 12 * line + 12):
                i, j = (t // 2) % 2, t % 2
                left = (t // 4 % 3) * channels + i * tile
                put(t, total[j * tile : (j + 1) * tile, left : left + tile])
        g_words = g_code[...] - (2.0 / SOFTMAX_WARMTH) * totals[...] * code[...].astype(F32)
        blocks = []
        for grad in (g_proj[...], g_dec[...], g_words):
            for left in range(0, grad.shape[1], 128):
                blocks.append(grad[:, left : left + 128].astype(BF16))
        size = blocks[0].shape[0]
        each = len(blocks) // 4
        start = keep.shape[1] - each * size - LOSS_ROWS
        for x in range(2):
            for n in range(each):
                even, odd = blocks[2 * x * each + n], blocks[(2 * x + 1) * each + n]
                row = slice(start + n * size, start + (n + 1) * size)
                keep[x, row] = jnp.where(lead, even, odd)
                send[x, row] = jnp.where(lead, odd, even)
        row = start + each * size
        value = jnp.broadcast_to(loss[...] * (1.0 / LOSS_ROWS), (LOSS_ROWS, loss.shape[1]))
        keep[0, row:, 0 : loss.shape[1]] = jnp.where(lead, value, 0.0).astype(BF16)
        send[0, row:, 0 : loss.shape[1]] = jnp.where(lead, 0.0, value).astype(BF16)
        for number in range(images // batch):
            for n in range(3):
                store(n, number).wait()
        pltpu.make_async_copy(weights_back, weights_far, weight_sem).wait()


def main_call(ids, places, slots, present, feat, near, far, cot, parts, proj, dec, code):
    images, height, wide, channels = feat.shape
    latent, words = code.shape
    size, half, tile = parts[0].shape
    slot_count = size * len(parts) // 2
    batch = 5 if images % 5 == 0 else 1
    smem = pl.BlockSpec(memory_space=pltpu.SMEM)
    strip = pl.BlockSpec((batch, height, wide, channels), lambda i: (i, 0, 0, 0))
    line = pl.BlockSpec((batch, wide, channels), lambda i: (i, 0, 0))
    hbm = pl.BlockSpec(memory_space=pl.ANY)

    def whole(shape):
        return pl.BlockSpec(shape, lambda i: (0,) * len(shape))

    big = jax.ShapeDtypeStruct(feat.shape, BF16)
    edge = jax.ShapeDtypeStruct(near.shape, BF16)
    rows = (2 * latent * channels + latent * words) // (4 * 128) + LOSS_ROWS
    part = jax.ShapeDtypeStruct((2, slot_count * tile // 4 + rows, tile), BF16)
    weights = jax.ShapeDtypeStruct((3, 3 * channels, channels), BF16)
    shapes = (big, big, big, edge, edge, weights, part, part)
    return pl.pallas_call(
        lambda *refs: main_kernel(batch, len(parts), *refs),
        grid=(images // batch,),
        in_specs=[smem] * 4
        + [whole((1, present.shape[0])), strip, line, line, strip]
        + [whole(a.shape) for a in (*parts, proj, dec, code)],
        out_specs=[hbm] * 3 + [line] * 2 + [hbm] + [whole(s.shape) for s in shapes[6:]],
        out_shape=shapes,
        scratch_shapes=[
            pltpu.VMEM((3, 3 * channels, channels), BF16),
            pltpu.VMEM((channels, channels), BF16),
            pltpu.VMEM((images, (height + 2) * wide, 3 * channels), BF16),
            pltpu.VMEM((images, channels, height * wide), BF16),
            pltpu.VMEM((channels, channels), F32),
            pltpu.VMEM((latent, channels), F32),
            pltpu.VMEM((latent, channels), F32),
            pltpu.VMEM((latent, words), F32),
            pltpu.VMEM((1, words), F32),
            pltpu.VMEM((1, latent), F32),
            pltpu.VMEM(proj.shape, BF16),
            pltpu.VMEM(dec.shape, BF16),
            pltpu.VMEM(code.shape, BF16),
            pltpu.VMEM((1, words), F32),
            pltpu.SMEM((1,), F32),
            pltpu.VMEM(feat.shape, BF16),
            pltpu.VMEM(feat.shape, BF16),
            pltpu.VMEM(feat.shape, BF16),
            pltpu.VMEM(weights.shape, BF16),
            pltpu.SemaphoreType.DMA((3, images // batch)),
            pltpu.SemaphoreType.DMA,
        ],
        compiler_params=pltpu.CompilerParams(vmem_limit_bytes=MAIN_VMEM),
        name="main",
    )(ids, places, slots, present, present[None], feat, near, far, cot, *parts, proj, dec, code)


BLOCK = 32
RANK = 4


def split3(x):
    high = x.astype(BF16)
    rest = x - high.astype(F32)
    middle = rest.astype(BF16)
    return high, middle, (rest - middle.astype(F32)).astype(BF16)


def dot_exact(a, b, dims=NN):
    left = jnp.concatenate([a[n] for n in (0, 0, 1, 1, 0, 2)], axis=dims[0][0])
    right = jnp.concatenate([b[n] for n in (0, 1, 0, 1, 2, 0)], axis=dims[1][0])
    return dot(left, right, dims)


def inverse_factors(pairs, beside):
    half = 64
    lane = lax.broadcasted_iota(jnp.int32, (8, 128), 1)
    sub = lax.broadcasted_iota(jnp.int32, (8, 128), 0)
    base = jnp.where(lane >= half, half, 0)
    inner = lane - base
    count = BLOCK // 8

    def pick(x, k):
        return jnp.take_along_axis(x, base + k, axis=1)

    mats = []
    for one, two in pairs:
        zero = jnp.zeros((BLOCK, half - BLOCK), F32)
        wide = jnp.concatenate([one, zero, two, zero], axis=1)
        mats.append(
            [
                wide[8 * v : 8 * v + 8] + jnp.where(inner == sub + (8 * v + BLOCK), 1.0, 0.0)
                for v in range(count)
            ]
        )
    for start in range(0, BLOCK, RANK):
        beside()
        v0, s0 = start // 8, start % 8
        for rows in mats:
            pivots = [jnp.broadcast_to(rows[v0][s0 + i : s0 + i + 1], (8, 128)) for i in range(RANK)]
            columns = [pick(rows[v0], start + j) for j in range(RANK)]
            core = {
                (i, j): jnp.broadcast_to(columns[j][s0 + i : s0 + i + 1], (8, 128))
                for i in range(RANK)
                for j in range(i, RANK)
            }
            lower = {}
            scaled = []
            for i in range(RANK):
                root = lax.rsqrt(core[i, i])
                for j in range(i + 1, RANK):
                    lower[j, i] = core[i, j] * (root * root)
                for j in range(i + 1, RANK):
                    for k in range(j, RANK):
                        core[j, k] = core[j, k] - lower[j, i] * core[i, k]
                    pivots[j] = pivots[j] - lower[j, i] * pivots[i]
                scaled.append((root, pivots[i] * root))
            if start + RANK < BLOCK:
                solved = [None] * RANK
                for i in range(RANK - 1, -1, -1):
                    solved[i] = scaled[i][1] * scaled[i][0]
                    for j in range(i + 1, RANK):
                        solved[i] = solved[i] - lower[j, i] * solved[j]
            for v in range(v0, count):
                new = rows[v]
                if v > v0 or s0 + RANK < 8:
                    for j in range(RANK):
                        column = columns[j] if v == v0 else pick(rows[v], start + j)
                        new = new - column * solved[j]
                if v == v0:
                    if s0 > 0:
                        new = jnp.where(sub < s0, rows[v], new)
                    for i in range(RANK):
                        new = jnp.where(sub == s0 + i, scaled[i][1], new)
                rows[v] = new
    return [jnp.concatenate(rows, axis=0) for rows in mats]


def small_update(present, shape, sums, arrays, outs):
    total = jnp.concatenate([sums[q, : sums.shape[1] - LOSS_ROWS] for q in range(4)], axis=0).astype(F32)
    row = 0
    for n, rate in enumerate((PROJ_RATE, DEC_RATE, CODE_RATE)):
        rows, columns = arrays[3 * n].shape
        pieces = []
        for _ in range(columns // 128):
            pieces.append(total[row : row + rows])
            row += rows
        grad = jnp.concatenate(pieces, axis=1)
        new = plain_adam(grad, *(a[...] for a in arrays[3 * n : 3 * n + 3]), rate)
        for out, value in zip(outs[3 * n : 3 * n + 3], new):
            out[...] = value
    loss = sums[0, sums.shape[1] - LOSS_ROWS :].astype(F32)
    scale = loss_scale(present, 4 * shape[1] * shape[2], arrays[0].shape[0])
    outs[9][...] = jnp.sum(loss, axis=(0, 1), keepdims=True) * scale


def taps(line, first, last):
    before, after = shift_lines(line.astype(F32), first, last)
    return jnp.concatenate([before, line, after], axis=1)


def inner_kernel(batch, weights, feat, d_resid, d_pre, out):
    height, wide, channels = feat.shape[1:]
    column = lax.broadcasted_iota(jnp.int32, (wide, channels), 0)
    first = column == 0
    last = column == wide - 1
    lines = height - 2
    rows = lines * wide
    sides = []
    for n in range(batch):
        seen = [taps(d_pre[n, r], first, last) for r in range(height)]
        sides.append(jnp.concatenate(seen, axis=0))
    acts = [None] * batch
    for a in range(3):
        for n in range(batch):
            term = dot(sides[n][a * wide : a * wide + rows], weights[a])
            acts[n] = term if acts[n] is None else acts[n] + term
    for n in range(batch):
        for r in range(lines):
            _, slope = gelu_both(feat[n, 1 + r].astype(F32))
            act = acts[n][r * wide : (r + 1) * wide]
            out[n, 1 + r] = (d_resid[n, 1 + r].astype(F32) + slope * act).astype(BF16)
        for r in (0, height - 1):
            out[n, r] = jnp.zeros((wide, channels), BF16)


def inner_call(weights, feat, d_resid, d_pre):
    images, height, wide, channels = feat.shape
    batch = 5 if images % 5 == 0 else 1
    strip = pl.BlockSpec((batch, height, wide, channels), lambda i: (i, 0, 0, 0))
    return pl.pallas_call(
        lambda *refs: inner_kernel(batch, *refs),
        grid=(images // batch,),
        in_specs=[pl.BlockSpec(weights.shape, lambda i: (0, 0, 0)), strip, strip, strip],
        out_specs=strip,
        out_shape=jax.ShapeDtypeStruct(feat.shape, BF16),
        compiler_params=pltpu.CompilerParams(vmem_limit_bytes=FINISH_VMEM),
        name="inner_lines",
    )(weights, feat, d_resid, d_pre)


def edge_units(group, weights, feats, d_resids, d_pres, near, far, lead, outs):
    images, _, wide, channels = d_pres[0].shape
    column = lax.broadcasted_iota(jnp.int32, (wide, channels), 0)
    first = column == 0
    last = column == wide - 1
    for base in range(0, images, group):
        members = [(n, end) for n in range(base, base + group) for end in range(2)]
        seen = []
        for n, end in members:
            if end == 0:
                lines = [jnp.where(lead, far[n], near[n]), d_pres[0][n, 0], d_pres[0][n, 1]]
            else:
                lines = [d_pres[1][n, 0], d_pres[1][n, 1], jnp.where(lead, near[n], far[n])]
            seen.append([taps(line, first, last) for line in lines])
        act = None
        for a in range(3):
            term = dot(jnp.concatenate([s[a] for s in seen], axis=0), weights[a])
            act = term if act is None else act + term
        for k, (n, end) in enumerate(members):
            _, slope = gelu_both(feats[end][n].astype(F32))
            total = d_resids[end][n].astype(F32) + slope * act[k * wide : (k + 1) * wide]
            outs[end][n] = total.astype(BF16)
        yield


def adam_units(tiles, grad_turned, first_new, second_new, master_new, small):
    master, first, second, basis_left, basis_right = tiles
    for t in range(master.shape[0]):
        one_low = basis_left[t].astype(BF16)
        two_low = basis_right[t].astype(BF16)
        turned = dot(one_low, grad_turned[t], ((0,), (1,)))
        turned = dot(turned.astype(BF16), two_low)
        mom = BETA_ONE * first[t] + (1.0 - BETA_ONE) * turned
        var = BETA_TWO * second[t] + (1.0 - BETA_TWO) * turned * turned
        first_new[t] = mom
        second_new[t] = var
        ratio = mom / (1.0 - BETA_ONE**STEP) / (jnp.sqrt(var / (1.0 - BETA_TWO**STEP)) + EPSILON)
        back = dot(dot(one_low, ratio.astype(BF16)).astype(BF16), two_low, NT)
        master_new[t] = master[t] - TILE_RATE * (back + WEIGHT_DECAY * master[t])
        yield
    small()
    yield


EDGE_GROUP = 4


def finish_kernel(*refs):
    ids, present = refs[:2]
    quarters = refs[2:6]
    master, first, second, left, right, basis_left, basis_right = refs[6:13]
    small_arrays = refs[13:22]
    weights_far, feat, d_resid, d_pre, near_far, far_far = refs[22:28]
    (master_new, first_new, second_new, left_new, right_new, basis_left_new, basis_right_new) = refs[
        29:36
    ]
    small_outs = refs[36:46]
    input_grad = refs[46]
    work, grad_turned, small_sums = refs[47:50]
    weights, feats, d_resids, d_pres, near, far, outs, load_sems, store_sems = refs[50:]
    count, tile = master.shape[:2]
    images, height = feat.shape[:2]
    ends = (0, height - 1)
    loads = [(weights_far, weights), (near_far, near), (far_far, far)]
    for end in range(2):
        loads.append((feat.at[:, ends[end]], feats.at[end]))
        loads.append((d_resid.at[:, ends[end]], d_resids.at[end]))
        loads.append((d_pre.at[:, pl.ds(end * (height - 2), 2)], d_pres.at[end]))
    copies = [
        pltpu.make_async_copy(src, dst, load_sems.at[n]) for n, (src, dst) in enumerate(loads)
    ]
    for copy in copies:
        copy.start()
    for d in range(4):
        quarter = tile // 4
        row = pl.multiple_of((ids[0] ^ d) * quarter, quarter)
        rows = count * quarter
        grad_turned[:, pl.ds(row, quarter), :] = quarters[d][:rows].reshape(count, quarter, tile)
        small_sums[ids[0] ^ d] = quarters[d][rows:]
    for t in range(count):
        grad = grad_turned[t]
        left_new[t] = BETA_TWO * left[t] + (1.0 - BETA_TWO) * dot(grad, grad, TN)
        right_new[t] = BETA_TWO * right[t] + (1.0 - BETA_TWO) * dot(grad, grad, NT)
        for side, (stat, basis) in enumerate(((left_new, basis_left), (right_new, basis_right))):
            moved = dot_exact(split3(stat[t]), split3(basis[t]))
            turned = moved.T
            work[2 * t + side, :, :tile] = dot_exact(split3(turned), split3(moved))
            work[2 * t + side, :, tile:] = turned
    for copy in copies:
        copy.wait()
    group = EDGE_GROUP if images % EDGE_GROUP == 0 else 1
    units = [
        adam_units(
            (master, first, second, basis_left, basis_right),
            grad_turned,
            first_new,
            second_new,
            master_new,
            lambda: small_update(present, feat.shape, small_sums, small_arrays, small_outs),
        ),
        edge_units(
            group,
            weights,
            [feats.at[end] for end in range(2)],
            [d_resids.at[end] for end in range(2)],
            [d_pres.at[end] for end in range(2)],
            near,
            far,
            lax.rem(ids[0], 2) == 0,
            [outs.at[end] for end in range(2)],
        ),
    ]
    total = count + 1 + images // group
    slots = tile // RANK
    used = [0, 0]

    def beside():
        used[0] += 1
        while used[1] < total * used[0] // slots:
            used[1] += 1
            if next(units[0], True) is not None:
                units.pop(0)
                next(units[0])

    for low in range(0, tile, BLOCK):
        high = low + BLOCK
        factors = inverse_factors(
            [
                (work[2 * t, low:high, low:high], work[2 * t + 1, low:high, low:high])
                for t in range(count)
            ],
            beside,
        )
        for n in range(2 * count):
            start = (n % 2) * 64 + BLOCK
            factor = split3(factors[n // 2][:, start : start + BLOCK])
            panel = dot_exact(factor, split3(work[n, low:high, :]))
            work[n, low:high, tile:] = panel[:, tile:]
            if high < tile:
                panel = split3(panel)
                work[n, high:, :] = work[n, high:, :] - dot_exact(
                    [p[:, high:tile] for p in panel], panel, TN
                )
    for t in range(count):
        basis_left_new[t] = work[2 * t, :, tile:].T
        basis_right_new[t] = work[2 * t + 1, :, tile:].T
    stores = [
        pltpu.make_async_copy(outs.at[end], input_grad.at[:, ends[end]], store_sems.at[end])
        for end in range(2)
    ]
    for store in stores:
        store.start()
    for store in stores:
        store.wait()


def finish_call(ids, present, quarters, arrays, small_arrays, loads):
    shape = jax.ShapeDtypeStruct(arrays[0].shape, F32)
    smem = pl.BlockSpec(memory_space=pltpu.SMEM)
    vmem = pl.BlockSpec(memory_space=pltpu.VMEM)
    hbm = pl.BlockSpec(memory_space=pl.ANY)
    count, tile = shape.shape[:2]
    shapes = [shape] * 7 + [jax.ShapeDtypeStruct(a.shape, F32) for a in small_arrays]
    shapes.append(jax.ShapeDtypeStruct((1, 1), F32))
    weights, feat, _, _, near, far, partial = loads
    images, height, wide, channels = feat.shape
    shapes.append(jax.ShapeDtypeStruct(feat.shape, BF16))
    ends = (2, images, wide, channels)
    return pl.pallas_call(
        finish_kernel,
        in_specs=[smem] + [vmem] * 21 + [hbm] * len(loads),
        out_specs=[vmem] * 17 + [hbm],
        out_shape=shapes,
        scratch_shapes=[
            pltpu.VMEM((2 * count, tile, 2 * tile), F32),
            pltpu.VMEM((count, tile, tile), BF16),
            pltpu.VMEM((4, quarters[0].shape[0] - count * tile // 4, tile), BF16),
            pltpu.VMEM(weights.shape, BF16),
            pltpu.VMEM(ends, BF16),
            pltpu.VMEM(ends, BF16),
            pltpu.VMEM((2, images, 2, wide, channels), BF16),
            pltpu.VMEM(near.shape, BF16),
            pltpu.VMEM(far.shape, BF16),
            pltpu.VMEM(ends, BF16),
            pltpu.SemaphoreType.DMA((9,)),
            pltpu.SemaphoreType.DMA((2,)),
        ],
        input_output_aliases={22 + len(loads) - 1: 17},
        compiler_params=pltpu.CompilerParams(vmem_limit_bytes=FINISH_VMEM),
        name="finish",
    )(ids, present[None], *quarters, *arrays, *small_arrays, *loads)


def plain_adam(gradient, master, first, second, rate):
    first_new = BETA_ONE * first + (1.0 - BETA_ONE) * gradient
    second_new = BETA_TWO * second + (1.0 - BETA_TWO) * gradient * gradient
    ratio = (
        first_new
        / (1.0 - BETA_ONE**STEP)
        / (jnp.sqrt(second_new / (1.0 - BETA_TWO**STEP)) + EPSILON)
    )
    return (master - rate * (ratio + WEIGHT_DECAY * master), first_new, second_new)


def swap(x, axis, distance):
    count = lax.axis_size(axis)
    return lax.ppermute(x, axis, [(i, i ^ distance) for i in range(count)])


def radices(count):
    out = []
    stride = 1
    while stride < count:
        left = (count // stride).bit_length() - 1
        radix = 2 if left % 2 else 4
        out.append((radix, stride))
        stride *= radix
    return out


def swap_edges(near, far):
    return swap(near, "strip", 1), lax.ppermute(far, "strip", [(1, 2), (2, 1)])


def gather_tiles(mine, meanwhile):
    core = lax.axis_index("strip") % 2
    half = mine.shape[1] // 2
    part = lax.dynamic_slice_in_dim(mine, core * half, half, axis=1)
    *steps, (last, _) = radices(lax.axis_size("img"))[::-1]
    for number, (radix, stride) in enumerate(steps):
        parts = [part] + [swap(part, "img", d * stride) for d in range(1, radix)]
        if number < len(steps) - 1:
            part = jnp.concatenate(parts, axis=0)
    count = len(parts) // 2
    pairs = [jnp.concatenate(parts[n * count : (n + 1) * count], axis=0) for n in range(2)]
    pairs, meanwhile = lax.optimization_barrier((pairs, meanwhile))
    arrays = [swap(pair, "img", d) if d else pair for d in range(last) for pair in pairs]
    return arrays + [swap(a, "strip", 1) for a in arrays], meanwhile


def tile_places(owners, tiles):
    distance = (owners // tiles) ^ lax.axis_index("img")
    place = jnp.zeros_like(owners)
    size = 1
    for radix, stride in radices(lax.axis_size("img"))[::-1]:
        place = place + size * ((distance // stride) % radix)
        size *= radix
    return place * tiles + owners % tiles


def tree_sum(terms):
    terms = [t.astype(F32) for t in terms]
    while len(terms) > 1:
        terms = [terms[n] + terms[n + 1] for n in range(0, len(terms), 2)]
    return terms[0]


def reduce_all(keep, send, tiles, quarter, inner, inputs):
    strip = lax.axis_index("strip")
    across = strip // 2
    img = lax.axis_index("img")
    groups = lax.axis_size("img")
    (radix, _), *later = radices(groups)
    low = img % radix
    size = tiles * quarter
    columns = keep.shape[-1]
    part = keep + swap(send, "strip", 1)
    left = groups // radix
    terms = []
    part, inputs = lax.optimization_barrier((part, inputs))
    for d in range(2):
        for e in range(radix):
            both = lax.dynamic_index_in_dim(part, across ^ d, 0, False)
            piece = both[: groups * size].reshape(left, radix, size, columns)
            piece = lax.dynamic_index_in_dim(piece, low ^ e, 1, False).reshape(left * size, columns)
            piece = jnp.concatenate([piece, both[groups * size :]], axis=0)
            if d or e:
                pairs = [
                    (a * groups + b, (a ^ (2 * d)) * groups + (b ^ e))
                    for a in range(4)
                    for b in range(groups)
                ]
                piece = lax.ppermute(piece, ("strip", "img"), pairs)
            terms.append(piece)
    terms, result = lax.optimization_barrier((terms, inner(*inputs)))
    total = tree_sum(terms).astype(BF16)
    for radix, stride in later:
        low = (img // stride) % radix
        terms = []
        for d in range(radix):
            piece = total[: left * size].reshape(left // radix, radix, size, columns)
            piece = lax.dynamic_index_in_dim(piece, low ^ d, 1, False)
            piece = piece.reshape(left // radix * size, columns)
            piece = jnp.concatenate([piece, total[left * size :]], axis=0)
            terms.append(swap(piece, "img", d * stride) if d else piece)
        total = tree_sum(terms).astype(BF16)
        left //= radix
    return [total] + [swap(total, "strip", d) for d in range(1, 4)], result


def body(
    features,
    cotangent,
    present,
    owners,
    tile_master,
    tile_mom1,
    tile_mom2,
    stat_left,
    stat_right,
    basis_left,
    basis_right,
    proj_master,
    proj_mom1,
    proj_mom2,
    dec_master,
    dec_mom1,
    dec_mom2,
    code_master,
    code_mom1,
    code_mom2,
):
    images, height, wide, channels = features.shape
    tiles = tile_master.shape[0]
    img = lax.axis_index("img")
    strip = lax.axis_index("strip")
    core = strip % 2
    ids = jnp.stack([strip, img]).astype(jnp.int32)
    ready = (ids, tile_places(owners, tiles))
    parts, (ids, places) = gather_tiles(tile_master.astype(BF16), ready)
    top, bottom = features[:, 0], features[:, height - 1]
    near, far = swap_edges(jnp.where(core == 0, bottom, top), jnp.where(core == 0, top, bottom))
    (decoded, d_pre, d_resid, near_out, far_out, weights, keep, send) = main_call(
        ids,
        places,
        owners,
        present,
        features,
        near,
        far,
        cotangent,
        parts,
        proj_master.T,
        dec_master,
        code_master.T,
    )
    near, far = swap_edges(near_out, far_out)
    quarters, partial = reduce_all(
        keep,
        send,
        tiles,
        tile_master.shape[1] // 4,
        inner_call,
        (weights, features, d_resid, d_pre),
    )
    out = finish_call(
        ids,
        present,
        quarters,
        [tile_master, tile_mom1, tile_mom2, stat_left, stat_right, basis_left, basis_right],
        [
            proj_master.T,
            proj_mom1.T,
            proj_mom2.T,
            dec_master,
            dec_mom1,
            dec_mom2,
            code_master.T,
            code_mom1.T,
            code_mom2.T,
        ],
        [weights, features, d_resid, d_pre, near, far, partial],
    )
    small = [a.T for a in out[7:10]] + list(out[10:13]) + [a.T for a in out[13:16]]
    return (decoded, out[17], out[16].reshape(()), *out[:7], *small)


def solution(mesh):
    big = P("img", "strip", None, None)
    tile = P("img", None, None)
    in_specs = (big, big, P(), P()) + (tile,) * 7 + (P(),) * 9
    out_specs = (big, big, P()) + (tile,) * 7 + (P(),) * 9
    return jax.shard_map(body, mesh=mesh, in_specs=in_specs, out_specs=out_specs, check_vma=False)
```

```python
import jax
import jax.numpy as jnp
from jax import lax
from jax.experimental import pallas as pl
from jax.experimental.pallas import tpu as pltpu
from jax.sharding import PartitionSpec as P

STEP = 5
BETA_ONE = 0.9
BETA_TWO = 0.95
EPSILON = 1e-08
WEIGHT_DECAY = 0.01
SOFTMAX_WARMTH = 4.0
LOSS_WEIGHT = 1.25
TILE_RATE = 0.05
PROJ_RATE = 0.05
DEC_RATE = 0.1
CODE_RATE = 0.3

F32 = jnp.float32
BF16 = jnp.bfloat16
NN = ((1,), (0,))
NT = ((1,), (1,))
TN = ((0,), (0,))
GELU_A = 0.7978845608028654
GELU_B = 0.044715
LOSS_ROWS = 16
MAIN_VMEM = 56 * 1024 * 1024
FINISH_VMEM = 56 * 1024 * 1024


def dot(a, b, dims=NN):
    return lax.dot_general(a, b, (dims, ((), ())), preferred_element_type=F32)


def gelu_tanh(x):
    return jnp.tanh(GELU_A * (x + GELU_B * (x * x * x)))


def gelu(x):
    return 0.5 * x * (1.0 + gelu_tanh(x))


def gelu_both(x):
    square = x * x
    t = jnp.tanh(GELU_A * x * (1.0 + GELU_B * square))
    half = 0.5 * (1.0 + t)
    slope = half + 0.5 * x * (1.0 - t * t) * (GELU_A + 3.0 * GELU_A * GELU_B * square)
    return x * half, slope


def column_shifts(rows, wide):
    count = rows.shape[0]
    column = lax.broadcasted_iota(jnp.int32, rows.shape, 0) % wide
    before = jnp.where(column == 0, 0.0, pltpu.roll(rows, 1, 0))
    after = jnp.where(column == wide - 1, 0.0, pltpu.roll(rows, count - 1, 0))
    return before, after


def place_weights(places, ids, parts, put):
    half = parts[0].shape[1]
    count = len(parts) // 2
    size = parts[0].shape[0]
    for t in range(40):
        which = lax.div(places[t], size)
        index = lax.rem(places[t], size)
        for side in range(2):
            block = parts[side * count][index]
            for n in range(1, count):
                block = jnp.where(which == n, parts[side * count + n][index], block)
            put(t, block, pl.multiple_of((lax.rem(ids[0], 2) ^ side) * half, half))


def loss_scale(present, positions, latent):
    count = jnp.sum(present[...].astype(F32)) * positions
    return LOSS_WEIGHT / (count * latent)


def shift_lines(line, first, last):
    wide = line.shape[0]
    before = jnp.where(first, 0.0, pltpu.roll(line, 1, 0)).astype(BF16)
    after = jnp.where(last, 0.0, pltpu.roll(line, wide - 1, 0)).astype(BF16)
    return before, after


def main_kernel(batch, part_count, *refs):
    ids, places, slots, present = refs[:4]
    present_row, feat, near, far, cot = refs[4:9]
    parts = refs[9 : 9 + part_count]
    proj_full, dec_full, code_full = refs[9 + part_count : 12 + part_count]
    (decoded_far, d_pre_far, d_resid_far, near_out, far_out, weights_far, keep, send) = refs[
        12 + part_count : 20 + part_count
    ]
    (weights, mixer, framed, d_pre_turned, g_mixer, g_proj, g_dec, g_code, totals, loss) = refs[
        20 + part_count : 30 + part_count
    ]
    proj, dec, code, norms, scale = refs[30 + part_count : 35 + part_count]
    decoded, d_pre_out, d_resid_out, weights_back, big_sems, weight_sem = refs[35 + part_count :]
    step = pl.program_id(0)
    steps = pl.num_programs(0)
    height, wide, channels = feat.shape[1:]
    count = height * wide
    tile = parts[0].shape[2]
    half = tile // 2
    images = framed.shape[0]
    lead = lax.rem(ids[0], 2) == 0

    @pl.when(step == 0)
    def _():
        def put(t, block, row):
            i, j = (t // 2) % 2, t % 2
            if t < 36:
                p = t // 4
                start = (p % 3) * channels + i * tile
                weights[p // 3, pl.ds(start + row, half), j * tile : (j + 1) * tile] = block
            else:
                mixer[pl.ds(i * tile + row, half), j * tile : (j + 1) * tile] = block

        place_weights(places, ids, parts, put)
        proj[...] = proj_full[...].astype(BF16)
        dec[...] = dec_full[...].astype(BF16)
        code[...] = code_full[...].astype(BF16)
        words = code[...].astype(F32)
        norms[...] = jnp.sum(words * words, axis=0, keepdims=True) * (1.0 / SOFTMAX_WARMTH)
        scale[0] = 2.0 * loss_scale(present_row, 4 * count, proj.shape[0])
        for ref in (keep, send, g_mixer, g_proj, g_dec, g_code, totals, loss):
            ref[...] = jnp.zeros_like(ref)

    @pl.when(step == 0)
    def _():
        for a in range(3):
            for b in range(3):
                block = weights[2 - a, (2 - b) * channels : (3 - b) * channels, :]
                weights_back[a, b * channels : (b + 1) * channels, :] = block.T
        pltpu.make_async_copy(weights_back, weights_far, weight_sem).start()

    column = lax.broadcasted_iota(jnp.int32, (wide, channels), 0)
    first = column == 0
    last = column == wide - 1

    def chain(n):
        image = step * batch + n
        alive = present[ids[1] * images + image].astype(F32)
        pull = alive * scale[0]
        for r in range(height + 2):
            if r == 0:
                line = jnp.where(lead, far[n].astype(F32), near[n].astype(F32))
            elif r == height + 1:
                line = jnp.where(lead, near[n].astype(F32), far[n].astype(F32))
            else:
                line = feat[n, r - 1].astype(F32)
            line = gelu(line)
            before, after = shift_lines(line, first, last)
            rows = slice(r * wide, (r + 1) * wide)
            framed[image, rows, 0:channels] = before
            framed[image, rows, channels : 2 * channels] = line.astype(BF16)
            framed[image, rows, 2 * channels :] = after
        yield
        preact = dot(framed[image, 0:count, :], weights[0])
        preact += dot(framed[image, wide : wide + count, :], weights[1])
        preact += dot(framed[image, 2 * wide : 2 * wide + count, :], weights[2])
        yield
        inner, slope = gelu_both(preact)
        inner = inner.astype(BF16)
        yield
        feats = feat[n].reshape(count, channels).astype(F32)
        resid = (feats + dot(inner, mixer[...])).astype(BF16)
        yield
        latent = dot(resid, proj[...], NT)
        latent_low = latent.astype(BF16)
        yield
        logits = (2.0 / SOFTMAX_WARMTH) * dot(latent_low, code[...]) - norms[...]
        yield
        powers = jnp.exp(logits - jnp.max(logits, axis=1, keepdims=True))
        probs = powers * (1.0 / jnp.sum(powers, axis=1, keepdims=True))
        probs_low = probs.astype(BF16)
        yield
        quant = dot(probs_low, code[...], NT)
        quant_low = quant.astype(BF16)
        yield
        out = (dot(quant_low, dec[...]) * alive).astype(BF16)
        decoded[image] = out.reshape(height, wide, channels)
        diff = latent - quant
        loss[...] += alive * jnp.sum(diff * diff, axis=0, keepdims=True)
        back_out = (cot[n].reshape(count, channels).astype(F32) * alive).astype(BF16)
        pulled = pull * diff
        d_quant = (dot(back_out, dec[...], NT) - pulled).astype(BF16)
        g_dec[...] += dot(quant_low, back_out, TN)
        yield
        d_probs = dot(d_quant, code[...])
        yield
        d_logits = probs * (d_probs - jnp.sum(probs * d_probs, axis=1, keepdims=True))
        d_logits = d_logits.astype(BF16)
        yield
        d_latent = ((2.0 / SOFTMAX_WARMTH) * dot(d_logits, code[...], NT) + pulled).astype(BF16)
        yield
        d_resid = dot(d_latent, proj[...]).astype(BF16)
        d_resid_out[image] = d_resid.reshape(height, wide, channels)
        g_code[...] += dot(d_quant, probs_low, TN)
        ones = jnp.ones((count, 16), BF16)
        both = dot(jnp.concatenate([latent_low, ones], axis=1), d_logits, TN)
        size = latent.shape[1]
        g_code[...] += (2.0 / SOFTMAX_WARMTH) * both[:size]
        totals[...] += both[size : size + 1]
        yield
        d_pre = (slope * dot(d_resid, mixer[...], NT)).astype(BF16)
        g_proj[...] += dot(d_latent, resid, TN)
        yield
        d_pre_out[image] = d_pre.reshape(height, wide, channels)
        top, bottom = d_pre[:wide], d_pre[count - wide :]
        near_out[n] = jnp.where(lead, bottom, top)
        far_out[n] = jnp.where(lead, top, bottom)
        g_mixer[...] += dot(d_resid, inner, TN)
        yield
        d_pre_turned[image] = d_pre.T

    live = [chain(n) for n in range(batch)]
    while live:
        live = [c for c in live if next(c, True) is None]
    bigs = ((decoded, decoded_far), (d_pre_out, d_pre_far), (d_resid_out, d_resid_far))

    def store(n, number):
        part = pl.ds(number * batch, batch)
        return pltpu.make_async_copy(bigs[n][0].at[part], bigs[n][1].at[part], big_sems.at[n, number])

    for n in range(3):
        store(n, step).start()

    @pl.when(step == steps - 1)
    def _():
        quarter = tile // 4

        def put(t, block):
            block = block.astype(BF16)
            for q in range(0, 4, 2):
                even = block[q * quarter : (q + 1) * quarter]
                odd = block[(q + 1) * quarter : (q + 2) * quarter]
                row = pl.ds(pl.multiple_of(slots[t] * quarter, quarter), quarter)
                keep[q // 2, row] = jnp.where(lead, even, odd)
                send[q // 2, row] = jnp.where(lead, odd, even)

        for t in range(36, 40):
            i, j = (t // 2) % 2, t % 2
            put(t, g_mixer[j * tile : (j + 1) * tile, i * tile : (i + 1) * tile])
        for line in range(3):
            total = None
            for n in range(images):
                term = dot(d_pre_turned[n], framed[n, line * wide : line * wide + count, :])
                total = term if total is None else total + term
            for t in range(12 * line, 12 * line + 12):
                i, j = (t // 2) % 2, t % 2
                left = (t // 4 % 3) * channels + i * tile
                put(t, total[j * tile : (j + 1) * tile, left : left + tile])
        g_words = g_code[...] - (2.0 / SOFTMAX_WARMTH) * totals[...] * code[...].astype(F32)
        blocks = []
        for grad in (g_proj[...], g_dec[...], g_words):
            for left in range(0, grad.shape[1], 128):
                blocks.append(grad[:, left : left + 128].astype(BF16))
        size = blocks[0].shape[0]
        each = len(blocks) // 4
        start = keep.shape[1] - each * size - LOSS_ROWS
        for x in range(2):
            for n in range(each):
                even, odd = blocks[2 * x * each + n], blocks[(2 * x + 1) * each + n]
                row = slice(start + n * size, start + (n + 1) * size)
                keep[x, row] = jnp.where(lead, even, odd)
                send[x, row] = jnp.where(lead, odd, even)
        row = start + each * size
        value = jnp.broadcast_to(loss[...] * (1.0 / LOSS_ROWS), (LOSS_ROWS, loss.shape[1]))
        keep[0, row:, 0 : loss.shape[1]] = jnp.where(lead, value, 0.0).astype(BF16)
        send[0, row:, 0 : loss.shape[1]] = jnp.where(lead, 0.0, value).astype(BF16)
        for number in range(images // batch):
            for n in range(3):
                store(n, number).wait()
        pltpu.make_async_copy(weights_back, weights_far, weight_sem).wait()


def main_call(ids, places, slots, present, feat, near, far, cot, parts, proj, dec, code):
    images, height, wide, channels = feat.shape
    latent, words = code.shape
    size, half, tile = parts[0].shape
    slot_count = size * len(parts) // 2
    batch = 4 if images % 4 == 0 else 1
    smem = pl.BlockSpec(memory_space=pltpu.SMEM)
    strip = pl.BlockSpec((batch, height, wide, channels), lambda i: (i, 0, 0, 0))
    line = pl.BlockSpec((batch, wide, channels), lambda i: (i, 0, 0))
    hbm = pl.BlockSpec(memory_space=pl.ANY)

    def whole(shape):
        return pl.BlockSpec(shape, lambda i: (0,) * len(shape))

    big = jax.ShapeDtypeStruct(feat.shape, BF16)
    edge = jax.ShapeDtypeStruct(near.shape, BF16)
    rows = (2 * latent * channels + latent * words) // (4 * 128) + LOSS_ROWS
    part = jax.ShapeDtypeStruct((2, slot_count * tile // 4 + rows, tile), BF16)
    weights = jax.ShapeDtypeStruct((3, 3 * channels, channels), BF16)
    shapes = (big, big, big, edge, edge, weights, part, part)
    return pl.pallas_call(
        lambda *refs: main_kernel(batch, len(parts), *refs),
        grid=(images // batch,),
        in_specs=[smem] * 4
        + [whole((1, present.shape[0])), strip, line, line, strip]
        + [whole(a.shape) for a in (*parts, proj, dec, code)],
        out_specs=[hbm] * 3 + [line] * 2 + [hbm] + [whole(s.shape) for s in shapes[6:]],
        out_shape=shapes,
        scratch_shapes=[
            pltpu.VMEM((3, 3 * channels, channels), BF16),
            pltpu.VMEM((channels, channels), BF16),
            pltpu.VMEM((images, (height + 2) * wide, 3 * channels), BF16),
            pltpu.VMEM((images, channels, height * wide), BF16),
            pltpu.VMEM((channels, channels), F32),
            pltpu.VMEM((latent, channels), F32),
            pltpu.VMEM((latent, channels), F32),
            pltpu.VMEM((latent, words), F32),
            pltpu.VMEM((1, words), F32),
            pltpu.VMEM((1, latent), F32),
            pltpu.VMEM(proj.shape, BF16),
            pltpu.VMEM(dec.shape, BF16),
            pltpu.VMEM(code.shape, BF16),
            pltpu.VMEM((1, words), F32),
            pltpu.SMEM((1,), F32),
            pltpu.VMEM(feat.shape, BF16),
            pltpu.VMEM(feat.shape, BF16),
            pltpu.VMEM(feat.shape, BF16),
            pltpu.VMEM(weights.shape, BF16),
            pltpu.SemaphoreType.DMA((3, images // batch)),
            pltpu.SemaphoreType.DMA,
        ],
        compiler_params=pltpu.CompilerParams(vmem_limit_bytes=MAIN_VMEM),
        name="main",
    )(ids, places, slots, present, present[None], feat, near, far, cot, *parts, proj, dec, code)


BLOCK = 32
RANK = 4


def split3(x):
    high = x.astype(BF16)
    rest = x - high.astype(F32)
    middle = rest.astype(BF16)
    return high, middle, (rest - middle.astype(F32)).astype(BF16)


def dot_exact(a, b, dims=NN):
    left = jnp.concatenate([a[n] for n in (0, 0, 1, 1, 0, 2)], axis=dims[0][0])
    right = jnp.concatenate([b[n] for n in (0, 1, 0, 1, 2, 0)], axis=dims[1][0])
    return dot(left, right, dims)


def inverse_factors(pairs, beside):
    half = 64
    lane = lax.broadcasted_iota(jnp.int32, (8, 128), 1)
    sub = lax.broadcasted_iota(jnp.int32, (8, 128), 0)
    base = jnp.where(lane >= half, half, 0)
    inner = lane - base
    count = BLOCK // 8

    def pick(x, k):
        return jnp.take_along_axis(x, base + k, axis=1)

    mats = []
    for one, two in pairs:
        zero = jnp.zeros((BLOCK, half - BLOCK), F32)
        wide = jnp.concatenate([one, zero, two, zero], axis=1)
        mats.append(
            [
                wide[8 * v : 8 * v + 8] + jnp.where(inner == sub + (8 * v + BLOCK), 1.0, 0.0)
                for v in range(count)
            ]
        )
    for start in range(0, BLOCK, RANK):
        beside()
        v0, s0 = start // 8, start % 8
        for rows in mats:
            pivots = [jnp.broadcast_to(rows[v0][s0 + i : s0 + i + 1], (8, 128)) for i in range(RANK)]
            columns = [pick(rows[v0], start + j) for j in range(RANK)]
            core = {
                (i, j): jnp.broadcast_to(columns[j][s0 + i : s0 + i + 1], (8, 128))
                for i in range(RANK)
                for j in range(i, RANK)
            }
            lower = {}
            scaled = []
            for i in range(RANK):
                root = lax.rsqrt(core[i, i])
                for j in range(i + 1, RANK):
                    lower[j, i] = core[i, j] * (root * root)
                for j in range(i + 1, RANK):
                    for k in range(j, RANK):
                        core[j, k] = core[j, k] - lower[j, i] * core[i, k]
                    pivots[j] = pivots[j] - lower[j, i] * pivots[i]
                scaled.append((root, pivots[i] * root))
            if start + RANK < BLOCK:
                solved = [None] * RANK
                for i in range(RANK - 1, -1, -1):
                    solved[i] = scaled[i][1] * scaled[i][0]
                    for j in range(i + 1, RANK):
                        solved[i] = solved[i] - lower[j, i] * solved[j]
            for v in range(v0, count):
                new = rows[v]
                if v > v0 or s0 + RANK < 8:
                    for j in range(RANK):
                        column = columns[j] if v == v0 else pick(rows[v], start + j)
                        new = new - column * solved[j]
                if v == v0:
                    if s0 > 0:
                        new = jnp.where(sub < s0, rows[v], new)
                    for i in range(RANK):
                        new = jnp.where(sub == s0 + i, scaled[i][1], new)
                rows[v] = new
    return [jnp.concatenate(rows, axis=0) for rows in mats]


def small_update(present, shape, sums, arrays, outs):
    total = jnp.concatenate([sums[q, : sums.shape[1] - LOSS_ROWS] for q in range(4)], axis=0).astype(F32)
    row = 0
    for n, rate in enumerate((PROJ_RATE, DEC_RATE, CODE_RATE)):
        rows, columns = arrays[3 * n].shape
        pieces = []
        for _ in range(columns // 128):
            pieces.append(total[row : row + rows])
            row += rows
        grad = jnp.concatenate(pieces, axis=1)
        new = plain_adam(grad, *(a[...] for a in arrays[3 * n : 3 * n + 3]), rate)
        for out, value in zip(outs[3 * n : 3 * n + 3], new):
            out[...] = value
    loss = sums[0, sums.shape[1] - LOSS_ROWS :].astype(F32)
    scale = loss_scale(present, 4 * shape[1] * shape[2], arrays[0].shape[0])
    outs[9][...] = jnp.sum(loss, axis=(0, 1), keepdims=True) * scale


def taps(line, first, last):
    before, after = shift_lines(line.astype(F32), first, last)
    return jnp.concatenate([before, line, after], axis=1)


def inner_kernel(batch, weights, feat, d_resid, d_pre, out):
    height, wide, channels = feat.shape[1:]
    column = lax.broadcasted_iota(jnp.int32, (wide, channels), 0)
    first = column == 0
    last = column == wide - 1
    lines = height - 2
    rows = lines * wide
    sides = []
    for n in range(batch):
        seen = [taps(d_pre[n, r], first, last) for r in range(height)]
        sides.append(jnp.concatenate(seen, axis=0))
    acts = [None] * batch
    for a in range(3):
        for n in range(batch):
            term = dot(sides[n][a * wide : a * wide + rows], weights[a])
            acts[n] = term if acts[n] is None else acts[n] + term
    for n in range(batch):
        for r in range(lines):
            _, slope = gelu_both(feat[n, 1 + r].astype(F32))
            act = acts[n][r * wide : (r + 1) * wide]
            out[n, 1 + r] = (d_resid[n, 1 + r].astype(F32) + slope * act).astype(BF16)
        for r in (0, height - 1):
            out[n, r] = jnp.zeros((wide, channels), BF16)


def inner_call(weights, feat, d_resid, d_pre):
    images, height, wide, channels = feat.shape
    batch = 5 if images % 5 == 0 else 1
    strip = pl.BlockSpec((batch, height, wide, channels), lambda i: (i, 0, 0, 0))
    return pl.pallas_call(
        lambda *refs: inner_kernel(batch, *refs),
        grid=(images // batch,),
        in_specs=[pl.BlockSpec(weights.shape, lambda i: (0, 0, 0)), strip, strip, strip],
        out_specs=strip,
        out_shape=jax.ShapeDtypeStruct(feat.shape, BF16),
        compiler_params=pltpu.CompilerParams(vmem_limit_bytes=FINISH_VMEM),
        name="inner_lines",
    )(weights, feat, d_resid, d_pre)


def edge_units(group, weights, feats, d_resids, d_pres, near, far, lead, outs):
    images, _, wide, channels = d_pres[0].shape
    column = lax.broadcasted_iota(jnp.int32, (wide, channels), 0)
    first = column == 0
    last = column == wide - 1
    for base in range(0, images, group):
        members = [(n, end) for n in range(base, base + group) for end in range(2)]
        seen = []
        for n, end in members:
            if end == 0:
                lines = [jnp.where(lead, far[n], near[n]), d_pres[0][n, 0], d_pres[0][n, 1]]
            else:
                lines = [d_pres[1][n, 0], d_pres[1][n, 1], jnp.where(lead, near[n], far[n])]
            seen.append([taps(line, first, last) for line in lines])
        act = None
        for a in range(3):
            term = dot(jnp.concatenate([s[a] for s in seen], axis=0), weights[a])
            act = term if act is None else act + term
        for k, (n, end) in enumerate(members):
            _, slope = gelu_both(feats[end][n].astype(F32))
            total = d_resids[end][n].astype(F32) + slope * act[k * wide : (k + 1) * wide]
            outs[end][n] = total.astype(BF16)
        yield


def adam_units(tiles, grad_turned, first_new, second_new, master_new, small):
    master, first, second, basis_left, basis_right = tiles
    for t in range(master.shape[0]):
        one_low = basis_left[t].astype(BF16)
        two_low = basis_right[t].astype(BF16)
        turned = dot(one_low, grad_turned[t], ((0,), (1,)))
        turned = dot(turned.astype(BF16), two_low)
        mom = BETA_ONE * first[t] + (1.0 - BETA_ONE) * turned
        var = BETA_TWO * second[t] + (1.0 - BETA_TWO) * turned * turned
        first_new[t] = mom
        second_new[t] = var
        ratio = mom / (1.0 - BETA_ONE**STEP) / (jnp.sqrt(var / (1.0 - BETA_TWO**STEP)) + EPSILON)
        back = dot(dot(one_low, ratio.astype(BF16)).astype(BF16), two_low, NT)
        master_new[t] = master[t] - TILE_RATE * (back + WEIGHT_DECAY * master[t])
        yield
    small()
    yield


EDGE_GROUP = 2


def finish_kernel(*refs):
    ids, present = refs[:2]
    quarters = refs[2:6]
    master, first, second, left, right, basis_left, basis_right = refs[6:13]
    small_arrays = refs[13:22]
    weights_far, feat, d_resid, d_pre, near_far, far_far = refs[22:28]
    (master_new, first_new, second_new, left_new, right_new, basis_left_new, basis_right_new) = refs[
        29:36
    ]
    small_outs = refs[36:46]
    input_grad = refs[46]
    work, grad_turned, small_sums = refs[47:50]
    weights, feats, d_resids, d_pres, near, far, outs, load_sems, store_sems = refs[50:]
    count, tile = master.shape[:2]
    images, height = feat.shape[:2]
    ends = (0, height - 1)
    loads = [(weights_far, weights), (near_far, near), (far_far, far)]
    for end in range(2):
        loads.append((feat.at[:, ends[end]], feats.at[end]))
        loads.append((d_resid.at[:, ends[end]], d_resids.at[end]))
        loads.append((d_pre.at[:, pl.ds(end * (height - 2), 2)], d_pres.at[end]))
    copies = [
        pltpu.make_async_copy(src, dst, load_sems.at[n]) for n, (src, dst) in enumerate(loads)
    ]
    for copy in copies:
        copy.start()
    for d in range(4):
        quarter = tile // 4
        row = pl.multiple_of((ids[0] ^ d) * quarter, quarter)
        rows = count * quarter
        grad_turned[:, pl.ds(row, quarter), :] = quarters[d][:rows].reshape(count, quarter, tile)
        small_sums[ids[0] ^ d] = quarters[d][rows:]
    for t in range(count):
        grad = grad_turned[t]
        left_new[t] = BETA_TWO * left[t] + (1.0 - BETA_TWO) * dot(grad, grad, TN)
        right_new[t] = BETA_TWO * right[t] + (1.0 - BETA_TWO) * dot(grad, grad, NT)
        for side, (stat, basis) in enumerate(((left_new, basis_left), (right_new, basis_right))):
            moved = dot_exact(split3(stat[t]), split3(basis[t]))
            turned = moved.T
            work[2 * t + side, :, :tile] = dot_exact(split3(turned), split3(moved))
            work[2 * t + side, :, tile:] = turned
    for copy in copies:
        copy.wait()
    group = EDGE_GROUP if images % EDGE_GROUP == 0 else 1
    units = [
        adam_units(
            (master, first, second, basis_left, basis_right),
            grad_turned,
            first_new,
            second_new,
            master_new,
            lambda: small_update(present, feat.shape, small_sums, small_arrays, small_outs),
        ),
        edge_units(
            group,
            weights,
            [feats.at[end] for end in range(2)],
            [d_resids.at[end] for end in range(2)],
            [d_pres.at[end] for end in range(2)],
            near,
            far,
            lax.rem(ids[0], 2) == 0,
            [outs.at[end] for end in range(2)],
        ),
    ]
    total = count + 1 + images // group
    slots = tile // RANK
    used = [0, 0]

    def beside():
        used[0] += 1
        while used[1] < total * used[0] // slots:
            used[1] += 1
            if next(units[0], True) is not None:
                units.pop(0)
                next(units[0])

    for low in range(0, tile, BLOCK):
        high = low + BLOCK
        factors = inverse_factors(
            [
                (work[2 * t, low:high, low:high], work[2 * t + 1, low:high, low:high])
                for t in range(count)
            ],
            beside,
        )
        for n in range(2 * count):
            start = (n % 2) * 64 + BLOCK
            factor = split3(factors[n // 2][:, start : start + BLOCK])
            panel = dot_exact(factor, split3(work[n, low:high, :]))
            work[n, low:high, tile:] = panel[:, tile:]
            if high < tile:
                panel = split3(panel)
                work[n, high:, :] = work[n, high:, :] - dot_exact(
                    [p[:, high:tile] for p in panel], panel, TN
                )
    for t in range(count):
        basis_left_new[t] = work[2 * t, :, tile:].T
        basis_right_new[t] = work[2 * t + 1, :, tile:].T
    stores = [
        pltpu.make_async_copy(outs.at[end], input_grad.at[:, ends[end]], store_sems.at[end])
        for end in range(2)
    ]
    for store in stores:
        store.start()
    for store in stores:
        store.wait()


def finish_call(ids, present, quarters, arrays, small_arrays, loads):
    shape = jax.ShapeDtypeStruct(arrays[0].shape, F32)
    smem = pl.BlockSpec(memory_space=pltpu.SMEM)
    vmem = pl.BlockSpec(memory_space=pltpu.VMEM)
    hbm = pl.BlockSpec(memory_space=pl.ANY)
    count, tile = shape.shape[:2]
    shapes = [shape] * 7 + [jax.ShapeDtypeStruct(a.shape, F32) for a in small_arrays]
    shapes.append(jax.ShapeDtypeStruct((1, 1), F32))
    weights, feat, _, _, near, far, partial = loads
    images, height, wide, channels = feat.shape
    shapes.append(jax.ShapeDtypeStruct(feat.shape, BF16))
    ends = (2, images, wide, channels)
    return pl.pallas_call(
        finish_kernel,
        in_specs=[smem] + [vmem] * 21 + [hbm] * len(loads),
        out_specs=[vmem] * 17 + [hbm],
        out_shape=shapes,
        scratch_shapes=[
            pltpu.VMEM((2 * count, tile, 2 * tile), F32),
            pltpu.VMEM((count, tile, tile), BF16),
            pltpu.VMEM((4, quarters[0].shape[0] - count * tile // 4, tile), BF16),
            pltpu.VMEM(weights.shape, BF16),
            pltpu.VMEM(ends, BF16),
            pltpu.VMEM(ends, BF16),
            pltpu.VMEM((2, images, 2, wide, channels), BF16),
            pltpu.VMEM(near.shape, BF16),
            pltpu.VMEM(far.shape, BF16),
            pltpu.VMEM(ends, BF16),
            pltpu.SemaphoreType.DMA((9,)),
            pltpu.SemaphoreType.DMA((2,)),
        ],
        input_output_aliases={22 + len(loads) - 1: 17},
        compiler_params=pltpu.CompilerParams(vmem_limit_bytes=FINISH_VMEM),
        name="finish",
    )(ids, present[None], *quarters, *arrays, *small_arrays, *loads)


def plain_adam(gradient, master, first, second, rate):
    first_new = BETA_ONE * first + (1.0 - BETA_ONE) * gradient
    second_new = BETA_TWO * second + (1.0 - BETA_TWO) * gradient * gradient
    ratio = (
        first_new
        / (1.0 - BETA_ONE**STEP)
        / (jnp.sqrt(second_new / (1.0 - BETA_TWO**STEP)) + EPSILON)
    )
    return (master - rate * (ratio + WEIGHT_DECAY * master), first_new, second_new)


def swap(x, axis, distance):
    count = lax.axis_size(axis)
    return lax.ppermute(x, axis, [(i, i ^ distance) for i in range(count)])


def radices(count):
    out = []
    stride = 1
    while stride < count:
        left = (count // stride).bit_length() - 1
        radix = 2 if left % 2 else 4
        out.append((radix, stride))
        stride *= radix
    return out


def swap_edges(near, far):
    return swap(near, "strip", 1), lax.ppermute(far, "strip", [(1, 2), (2, 1)])


def gather_tiles(mine, meanwhile):
    core = lax.axis_index("strip") % 2
    half = mine.shape[1] // 2
    part = lax.dynamic_slice_in_dim(mine, core * half, half, axis=1)
    *steps, (last, _) = radices(lax.axis_size("img"))[::-1]
    for number, (radix, stride) in enumerate(steps):
        parts = [part] + [swap(part, "img", d * stride) for d in range(1, radix)]
        if number < len(steps) - 1:
            part = jnp.concatenate(parts, axis=0)
    count = len(parts) // 2
    pairs = [jnp.concatenate(parts[n * count : (n + 1) * count], axis=0) for n in range(2)]
    pairs, meanwhile = lax.optimization_barrier((pairs, meanwhile))
    arrays = [swap(pair, "img", d) if d else pair for d in range(last) for pair in pairs]
    return arrays + [swap(a, "strip", 1) for a in arrays], meanwhile


def tile_places(owners, tiles):
    distance = (owners // tiles) ^ lax.axis_index("img")
    place = jnp.zeros_like(owners)
    size = 1
    for radix, stride in radices(lax.axis_size("img"))[::-1]:
        place = place + size * ((distance // stride) % radix)
        size *= radix
    return place * tiles + owners % tiles


def tree_sum(terms):
    terms = [t.astype(F32) for t in terms]
    while len(terms) > 1:
        terms = [terms[n] + terms[n + 1] for n in range(0, len(terms), 2)]
    return terms[0]


def reduce_all(keep, send, tiles, quarter, inner, inputs):
    strip = lax.axis_index("strip")
    across = strip // 2
    img = lax.axis_index("img")
    groups = lax.axis_size("img")
    (radix, _), *later = radices(groups)
    low = img % radix
    size = tiles * quarter
    columns = keep.shape[-1]
    part = keep + swap(send, "strip", 1)
    left = groups // radix
    terms = []
    part, inputs = lax.optimization_barrier((part, inputs))
    for d in range(2):
        for e in range(radix):
            both = lax.dynamic_index_in_dim(part, across ^ d, 0, False)
            piece = both[: groups * size].reshape(left, radix, size, columns)
            piece = lax.dynamic_index_in_dim(piece, low ^ e, 1, False).reshape(left * size, columns)
            piece = jnp.concatenate([piece, both[groups * size :]], axis=0)
            if d or e:
                pairs = [
                    (a * groups + b, (a ^ (2 * d)) * groups + (b ^ e))
                    for a in range(4)
                    for b in range(groups)
                ]
                piece = lax.ppermute(piece, ("strip", "img"), pairs)
            terms.append(piece)
    terms, result = lax.optimization_barrier((terms, inner(*inputs)))
    total = tree_sum(terms).astype(BF16)
    for radix, stride in later:
        low = (img // stride) % radix
        terms = []
        for d in range(radix):
            piece = total[: left * size].reshape(left // radix, radix, size, columns)
            piece = lax.dynamic_index_in_dim(piece, low ^ d, 1, False)
            piece = piece.reshape(left // radix * size, columns)
            piece = jnp.concatenate([piece, total[left * size :]], axis=0)
            terms.append(swap(piece, "img", d * stride) if d else piece)
        total = tree_sum(terms).astype(BF16)
        left //= radix
    return [total] + [swap(total, "strip", d) for d in range(1, 4)], result


def body(
    features,
    cotangent,
    present,
    owners,
    tile_master,
    tile_mom1,
    tile_mom2,
    stat_left,
    stat_right,
    basis_left,
    basis_right,
    proj_master,
    proj_mom1,
    proj_mom2,
    dec_master,
    dec_mom1,
    dec_mom2,
    code_master,
    code_mom1,
    code_mom2,
):
    images, height, wide, channels = features.shape
    tiles = tile_master.shape[0]
    img = lax.axis_index("img")
    strip = lax.axis_index("strip")
    core = strip % 2
    ids = jnp.stack([strip, img]).astype(jnp.int32)
    ready = (ids, tile_places(owners, tiles))
    parts, (ids, places) = gather_tiles(tile_master.astype(BF16), ready)
    top, bottom = features[:, 0], features[:, height - 1]
    near, far = swap_edges(jnp.where(core == 0, bottom, top), jnp.where(core == 0, top, bottom))
    (decoded, d_pre, d_resid, near_out, far_out, weights, keep, send) = main_call(
        ids,
        places,
        owners,
        present,
        features,
        near,
        far,
        cotangent,
        parts,
        proj_master.T,
        dec_master,
        code_master.T,
    )
    near, far = swap_edges(near_out, far_out)
    quarters, partial = reduce_all(
        keep,
        send,
        tiles,
        tile_master.shape[1] // 4,
        inner_call,
        (weights, features, d_resid, d_pre),
    )
    out = finish_call(
        ids,
        present,
        quarters,
        [tile_master, tile_mom1, tile_mom2, stat_left, stat_right, basis_left, basis_right],
        [
            proj_master.T,
            proj_mom1.T,
            proj_mom2.T,
            dec_master,
            dec_mom1,
            dec_mom2,
            code_master.T,
            code_mom1.T,
            code_mom2.T,
        ],
        [weights, features, d_resid, d_pre, near, far, partial],
    )
    small = [a.T for a in out[7:10]] + list(out[10:13]) + [a.T for a in out[13:16]]
    return (decoded, out[17], out[16].reshape(()), *out[:7], *small)


def solution(mesh):
    big = P("img", "strip", None, None)
    tile = P("img", None, None)
    in_specs = (big, big, P(), P()) + (tile,) * 7 + (P(),) * 9
    out_specs = (big, big, P()) + (tile,) * 7 + (P(),) * 9
    return jax.shard_map(body, mesh=mesh, in_specs=in_specs, out_specs=out_specs, check_vma=False)
```
